32 devices in a mesh: gz: 4 (over z), gy: 2 (over y), gx: 4 (over x, core).
Axes of the slice: x: 2, y: 2, z: 4, core: 2. Of those that a mesh axis runs over, the one named last changes fastest.
Arguments:
- side_field: float32 [2, 192, 64, 512], P(None, 'gz', 'gy', 'gx'), may hold values from -6 to 6
- magnetogram: float32 [64, 512], P('gy', 'gx'), may hold values from -6 to 6
Outputs:
- potential: float32 [3, 192, 64, 512], P(None, 'gz', 'gy', 'gx')
The draws below stay inside these ranges and needn't reach their ends.
All inputs are finite; a program needn't handle non-finite values.
Results may differ from the reference program's by a relative error of at most 0.000021.
Values sent between devices are 32-bit elements; how exact they have to be, the bound alone decides.
No kernel may reach another device: no remote copies, remote signals or barrier semaphores. Data moves between devices by JAX's collectives and lax.ppermute only.
A program may use at most 64 MiB of HBM per device.

```python
import jax
import jax.numpy as jnp
from jax import lax

CZ = 48
NZ = 192
NY = 64
NX = 512


def shard_levels(stream_key, shape, pieces, low, top_value):
    factor_of = 1.0
    for dim, blocks in pieces:
        steps = jax.random.uniform(jax.random.fold_in(jax.random.fold_in(stream_key, 6), dim), (blocks,), jnp.float32, low / len(pieces), top_value / len(pieces))
        factor_of = factor_of * jnp.repeat(jnp.exp(steps), shape[dim] // blocks).reshape((-1,) + (1,) * (len(shape) - 1 - dim))
    return factor_of


def normal_values(stream_key, shape, width, bound, shards=(), kind=jnp.bfloat16):
    loudness = shard_levels(stream_key, shape, shards, -0.22, 0.18) if shards else 1.0
    result = jax.random.normal(stream_key, shape, jnp.float32) * width * loudness
    return jnp.minimum(jnp.maximum(result, -bound), bound).astype(kind)


def setup_inputs(seed: int = 0) -> dict:
    keys = jax.random.split(jax.random.key(seed), 3)
    side_field = normal_values(keys[0], (2, NZ, NY, NX), 1.0, 6.0, ((1, 4), (2, 2), (3, 4)), jnp.float32)
    magnetogram = normal_values(keys[1], (NY, NX), 1.0, 6.0, ((0, 2), (1, 4)), jnp.float32)
    return {"side_field": side_field, "magnetogram": magnetogram}


spacing = 0.0625
friction = 0.004


def forward_parts(values):
    anchor = values[:-1, :-1, :-1]
    return (values[1:, :-1, :-1] - anchor, values[:-1, 1:, :-1] - anchor, values[:-1, :-1, 1:] - anchor)


def backward_parts(values):
    corner = values[1:, 1:, 1:]
    return (corner - values[:-1, 1:, 1:], corner - values[1:, :-1, 1:], corner - values[1:, 1:, :-1])


def advance(padded):
    along_x = forward_parts(padded[0])
    along_y = forward_parts(padded[1])
    along_z = forward_parts(padded[2])
    field_x = (along_z[1] - along_y[0]) / spacing
    field_y = (along_x[0] - along_z[2]) / spacing
    field_z = (along_y[2] - along_x[1]) / spacing
    back_x = backward_parts(field_x)
    back_y = backward_parts(field_y)
    back_z = backward_parts(field_z)
    current_x = (back_z[1] - back_y[0]) / spacing
    current_y = (back_x[0] - back_z[2]) / spacing
    current_z = (back_y[2] - back_x[1]) / spacing
    cell_x = field_x[1:, 1:, 1:]
    cell_y = field_y[1:, 1:, 1:]
    cell_z = field_z[1:, 1:, 1:]
    denominator = cell_x * cell_x + cell_y * cell_y + cell_z * cell_z + 1.0
    speed_x = (current_y * cell_z - current_z * cell_y) / denominator
    speed_y = (current_z * cell_x - current_x * cell_z) / denominator
    speed_z = (current_x * cell_y - current_y * cell_x) / denominator
    drive_x = speed_y * cell_z - speed_z * cell_y
    drive_y = speed_z * cell_x - speed_x * cell_z
    drive_z = speed_x * cell_y - speed_y * cell_x
    inner = padded[:, 1:-1, 1:-1, 1:-1]
    return inner + friction * jnp.stack([drive_x, drive_y, drive_z])


def advance_all(potential):
    padded = jnp.pad(potential, ((0, 0), (1, 1), (1, 1), (1, 1)))

    def one_block(start):
        piece = lax.dynamic_slice_in_dim(padded, start, CZ + 2, axis=1)
        return advance(piece)

    starts = jnp.arange(NZ // CZ, dtype=jnp.int32) * CZ
    blocks = lax.map(one_block, starts)
    return jnp.transpose(blocks, (1, 0, 2, 3, 4)).reshape(3, NZ, NY, NX)


def reference(side_field, magnetogram):
    half = 0.5 * spacing
    base_x = -half * jnp.cumsum(magnetogram, axis=0)
    base_y = half * jnp.cumsum(magnetogram, axis=1)
    rising = jnp.cumsum(side_field, axis=1)
    potential = jnp.stack([base_x[None] + spacing * rising[1], base_y[None] - spacing * rising[0], jnp.zeros_like(rising[0])])
    for _ in range(2):
        potential = advance_all(potential)
    return potential
```

```python
import functools

import jax
import jax.numpy as jnp
from jax import lax
from jax.experimental import pallas as pl
from jax.experimental.pallas import tpu as pltpu
from jax.sharding import PartitionSpec as P

spacing = 0.0625
friction = 0.004
gain = friction / (spacing * spacing)
LANES = 128
PAD = 8
GROUP = LANES // 4


def near(index, count):
    return (index + 1) % count if index % 2 else (index - 1) % count


def swap(part, axis, partner):
    count = lax.axis_size(axis)
    return lax.ppermute(part, axis, [(i, partner(i)) for i in range(count)])


def swap_first(part, axis):
    return swap(part, axis, lambda i: i ^ 1)


def swap_second(part, axis):
    count = lax.axis_size(axis)
    return swap(part, axis, lambda i: near(i, count))


def far_steps(count):
    return [2] if count == 4 else list(range(2, count))


def lane_index(shape):
    return lax.broadcasted_iota(jnp.int32, shape, len(shape) - 1)


def row_index(shape):
    return lax.broadcasted_iota(jnp.int32, shape, len(shape) - 2)


def columns_at(values, slot):
    first = 4 * (slot % GROUP)
    rolled = pltpu.roll(values, (first + 2) % LANES, 1)
    lane = lane_index(values.shape)
    return jnp.where((lane >= first) & (lane < first + 4), rolled, 0.0)


def spread(values, first):
    lane = lane_index(values.shape)
    moved = pltpu.roll(values, (LANES - first) % LANES, 1) if first else values
    result = jnp.where(lane < 4, moved, 0.0)
    step = 4
    while step < LANES:
        result = result + pltpu.roll(result, step, 1)
        step *= 2
    return result


def totals_kernel(place, side, mag, first_out, second_out, total_out, rows_out, columns_out):
    depth = side.shape[1]
    z = place[0]
    for c in range(2):
        low0 = side[c, 0]
        low1 = low0 + side[c, 1]
        before = low1
        for layer in range(2, depth - 1):
            before = before + side[c, layer]
        total = before + side[c, depth - 1]
        odd = z % 2 == 1
        first_out[c, 0] = jnp.where(odd, low0, before)
        first_out[c, 1] = jnp.where(odd, low1, total)
        upward = odd | (z == 0)
        second_out[c, 0] = jnp.where(upward, before, low0)
        second_out[c, 1] = jnp.where(upward, total, low1)
        total_out[c] = total
    rows = mag[...]
    lane = lane_index(rows.shape)
    step = 1
    while step < LANES:
        rows = rows + jnp.where(lane >= step, pltpu.roll(rows, step, 1), 0.0)
        step *= 2
    rows_out[...] = rows
    columns = mag[...]
    row = row_index(columns.shape)
    step = 1
    while step < columns.shape[0]:
        columns = columns + jnp.where(row >= step, pltpu.roll(columns, step, 0), 0.0)
        step *= 2
    columns_out[...] = columns


def pack_kernel(side, packed_out, rows_out, running):
    depth, height = side.shape[1], side.shape[2]
    for c in range(2):
        total = jnp.zeros(side.shape[2:], jnp.float32)
        packed = [jnp.zeros(side.shape[2:], jnp.float32) for _ in range(2)]
        for layer in range(depth):
            total = total + side[c, layer]
            running[c, pl.ds(layer * height, height), :] = total
            slot = layer + 2
            packed[slot // GROUP] += columns_at(total, slot)
        for tile in range(2):
            packed_out[c, :, pl.ds(tile * LANES, LANES)] = packed[tile]
        for k, row in enumerate((0, 1, height - 2, height - 1)):
            rows_out[c, k] = running[c, pl.ds(row, depth, stride=height), :]


def z_kernel(
    count, depth, far, place, first, second, total, columns, column_carry, rows, packed, *rest
):
    others, (x_out, ext_out, base_out) = rest[:far], rest[far:]
    z, y = place[0], place[1]
    odd = z % 2 == 1
    for c in range(2):
        near_a, near_b = (first[c, 0], first[c, 1]), (second[c, 0], second[c, 1])
        low = [jnp.where(odd, a, b) for a, b in zip(near_a, near_b)]
        high = [jnp.where(odd, b, a) for a, b in zip(near_a, near_b)]
        carry = jnp.where(odd, near_a[1], 0.0)
        if count == 4:
            carry = carry + jnp.where((z == 2) | (z == 3), near_b[1], 0.0)
        for step, other in zip(far_steps(count), others):
            carry = carry + jnp.where((z ^ step) < z, other[c], 0.0)
        above = carry + total[c]
        layers = (carry - (low[1] - low[0]), carry, above + high[0], above + high[1])
        for k in range(4):
            ext_out[c, k] = layers[k]
        if c == 0:
            base = rows[...]
        else:
            base = -0.5 * (columns[...] + jnp.where(y > 0, column_carry[7:8, :], 0.0))
            base_out[...] = base
        lane = lane_index(carry.shape)
        everywhere = spread(pltpu.roll(carry, 2, 1), 0)
        for tile in range(2):
            slot = lane // 4 + tile * GROUP
            values = packed[c, :, pl.ds(tile * LANES, LANES)]
            inside = (slot >= 2) & (slot < depth + 2)
            values = values + jnp.where(inside, everywhere, 0.0)
            for k, at in enumerate((0, 1, depth + 2, depth + 3)):
                if at // GROUP == tile:
                    values = values + columns_at(layers[k], at)
            if (depth + 4) // GROUP == tile:
                values = values + columns_at(base, depth + 4)
            x_out[c, :, pl.ds(tile * LANES, LANES)] = values


def x_kernel(
    counts, depth, place, packed, first, second, far_rows, rows, base, ext, edges,
    strips_out, flat_out, ext_out, y_out,
):
    count_z, count_y, count_x = counts
    height = packed.shape[1]
    z, y, x = place[0], place[1], place[2]
    odd = x % 2 == 1
    base_tile, base_lane = (depth + 4) // GROUP, 4 * ((depth + 4) % GROUP)

    def tile_of(ref, c, tile):
        return ref[c, :, pl.ds(tile * LANES, LANES)]

    def row_totals(ref):
        return tile_of(ref, 0, base_tile)[:, base_lane + 1 : base_lane + 2]

    own_total = rows[...][:, LANES - 1 :]
    total_a, total_b = row_totals(first), row_totals(second)
    far_total = far_rows[...][:, LANES - 1 :]
    if count_x == 2:
        row_carry = jnp.where(odd, total_a, 0.0)
    elif count_x == 4:
        row_carry = jnp.where(odd, total_a, 0.0) + jnp.where(x >= 2, total_b + far_total, 0.0)
    else:
        row_carry = far_total
    left_total = jnp.where(odd, total_a, total_b)

    lane = lane_index((height, LANES))
    q = lane % 4
    for part in range(2):
        merged = []
        for c in range(2):
            tiles = []
            for tile in range(2):
                own, a, b = (tile_of(ref, c, tile) for ref in (packed, first, second))
                if part == 0:
                    tiles.append(jnp.where(q < 2, jnp.where(odd, a, b), own))
                else:
                    tiles.append(jnp.where(q < 2, own, jnp.where(odd, b, a)))
            merged.append(tiles)
        if part == 0:
            carry = jnp.where(q < 2, row_carry - left_total, row_carry)
        else:
            carry = jnp.where(q < 2, row_carry, row_carry + own_total)
        base_y = 0.5 * (spread(merged[0][base_tile], base_lane) + carry)
        base_x = spread(merged[1][base_tile], base_lane)
        for tile in range(2):
            slot = lane // 4 + tile * GROUP
            inside = (slot < depth + 4) & ((slot >= 2) | (z > 0))
            inside = inside & ((slot < depth + 2) | (z < count_z - 1))
            if part == 0:
                inside = inside & ((q >= 2) | (x > 0))
            else:
                inside = inside & ((q < 2) | (x < count_x - 1))
            place_at = pl.ds((part * 2 + tile) * LANES, LANES)
            strips_out[0, :, place_at] = jnp.where(inside, base_x + merged[1][tile], 0.0)
            strips_out[1, :, place_at] = jnp.where(inside, base_y - merged[0][tile], 0.0)

    base_x = base[...]
    base_y = 0.5 * (rows[...] + row_carry)
    flat_out[0] = base_x + ext[1, 1]
    flat_out[1] = base_y - ext[0, 1]
    for k in range(4):
        inside = (z > 0) if k < 2 else (z < count_z - 1)
        ext_out[0, k] = jnp.where(inside, base_x + ext[1, k], 0.0)
        ext_out[1, k] = jnp.where(inside, base_y - ext[0, k], 0.0)

    slots = slot_rows(depth)
    for message in range(y_out.shape[0]):
        downward = (y % 2 == 1) if message == 0 else (y % 2 == 0)
        for c in range(2):
            for r in range(2):
                start = (c * 2 + r) * slots
                low, high = pl.ds(r, 1), pl.ds(height - 2 + r, 1)
                flat = jnp.where(downward, flat_out[c, low, :], flat_out[c, high, :])
                edge = jnp.where(downward, edges[1 - c, r], edges[1 - c, 2 + r])
                edge = edge if c == 0 else -edge
                y_out[message, pl.ds(start + 2, depth), :] = flat + edge
                for k, at in enumerate((0, 1, depth + 2, depth + 3)):
                    y_out[message, pl.ds(start + at, 1), :] = jnp.where(
                        downward, ext_out[c, k, low, :], ext_out[c, k, high, :]
                    )
            for tile in range(4):
                start = 4 * slots + (c * 4 + tile) * 2
                lanes = pl.ds(tile * LANES, LANES)
                y_out[message, pl.ds(start, 2), :] = jnp.where(
                    downward,
                    strips_out[c, pl.ds(0, 2), lanes],
                    strips_out[c, pl.ds(height - 2, 2), lanes],
                )


def slot_rows(depth):
    return (depth + 4 + 7) // 8 * 8


def following(values, axis, step=1):
    return pltpu.roll(values, values.shape[axis] - step, axis)


def preceding(values, axis, step=1):
    return pltpu.roll(values, step, axis)


def push(a, field, current):
    square = field[0] * field[0] + field[1] * field[1] + field[2] * field[2]
    along = current[0] * field[0] + current[1] * field[1] + current[2] * field[2]
    factor = gain / (square + 1.0)
    p, q = along * factor, square * factor
    return [a[c] + (field[c] * p - current[c] * q) for c in range(3)]


def strip_field(a):
    x, y, z = a
    field_x = following(z, 0) - z - (following(y, 1, 4) - y)
    field_y = following(x, 1, 4) - x - (following(z, 1) - z)
    field_z = following(y, 1) - y - (following(x, 0) - x)
    return field_x, field_y, field_z


def strip_current(b):
    x, y, z = b
    current_x = z - preceding(z, 0) - (y - preceding(y, 1, 4))
    current_y = x - preceding(x, 1, 4) - (z - preceding(z, 1))
    current_z = y - preceding(y, 1) - (x - preceding(x, 0))
    return current_x, current_y, current_z


def step_kernel(
    counts, place, side, flat, ext, strips, first, second, out, state, field, later, halo, wide
):
    count_z, count_y, count_x = counts
    depth, height = side.shape[1], side.shape[2]
    z, y, x = place[0], place[1], place[2]
    slots = slot_rows(depth)
    layers = depth + 4
    padded = state.shape[2]
    odd = y % 2 == 1

    sums = [jnp.zeros((height, LANES), jnp.float32) for _ in range(2)]
    rows = pl.ds(PAD, height)
    for c in range(2):
        for k, at in enumerate((0, 1, depth + 2, depth + 3)):
            state[c, at, rows, :] = ext[c, k]

    def fill(layer, sums):
        sums = [total + side[c, layer] for c, total in enumerate(sums)]
        state[0, layer + 2, rows, :] = flat[0] + sums[1]
        state[1, layer + 2, rows, :] = flat[1] - sums[0]
        return sums

    lax.fori_loop(0, depth, fill, sums)

    for low in (True, False):
        exists = (y > 0) if low else (y < count_y - 1)
        row = PAD - 2 if low else PAD + height
        for c in range(2):
            flat_state = state.at[c].reshape(layers * padded, LANES)
            for r in range(2):
                take = pl.ds((c * 2 + r) * slots, layers)
                a, b = first[take, :], second[take, :]
                value = jnp.where(odd, a, b) if low else jnp.where(odd, b, a)
                flat_state[pl.ds(row + r, layers, stride=padded), :] = jnp.where(exists, value, 0.0)
            for tile in range(4):
                take = pl.ds(4 * slots + (c * 4 + tile) * 2, 2)
                a, b = first[take, :], second[take, :]
                value = jnp.where(odd, a, b) if low else jnp.where(odd, b, a)
                wide[c, pl.ds(row, 2), pl.ds(tile * LANES, LANES)] = jnp.where(exists, value, 0.0)
    wide[0, rows, :] = strips[0]
    wide[1, rows, :] = strips[1]

    half = 2 * LANES
    lane = lane_index((padded, 2 * half))
    row = row_index((padded, 2 * half))
    q = lane % 4
    slot = (lane % half) // 4
    right = lane >= half
    inside = (row >= PAD - 2) & (row < PAD + height + 2) & (slot < layers)
    inside = inside & ((row >= PAD) | (y > 0)) & ((row < PAD + height) | (y < count_y - 1))
    inside = inside & ((slot >= 2) | (z > 0)) & ((slot < depth + 2) | (z < count_z - 1))
    inside = inside & (right | (q >= 2) | (x > 0))
    inside = inside & (~right | (q < 2) | (x < count_x - 1))
    a = [jnp.where(inside, wide[c], 0.0) for c in range(2)]
    a.append(jnp.zeros_like(a[0]))
    b = strip_field(a)
    pick = (lane_index((padded, half)) % 4) == 2

    def keep(at, upper, lower):
        value = jnp.where(pick, upper[:, half:], lower[:, :half])
        halo[at, 0] = value[:, :LANES]
        halo[at, 1] = value[:, LANES:]

    keep(0, a[1], b[1])
    keep(1, a[2], b[2])
    a = [jnp.where(inside, value, 0.0) for value in push(a, b, strip_current(b))]
    b = strip_field(a)
    keep(2, a[1], b[1])
    keep(3, a[2], b[2])

    lane = lane_index((8, LANES))
    last, start = lane == LANES - 1, lane == 0

    def beside(at, layer, row):
        shift = LANES - 2 - 4 * (layer % GROUP)
        return pltpu.roll(halo[at, layer // GROUP, pl.ds(row, 8), :], shift, 1)

    def right_of(value, edge):
        return following(jnp.where(start, edge, value), 1)

    def left_of(value, edge):
        return preceding(jnp.where(last, edge, value), 1)

    def load(ref, c, layer, row):
        return ref[c, layer, pl.ds(row, 8), :]

    def first_field(layer, _):
        for tile in range(5):
            r = PAD - 2 + 8 * tile
            ax, ay = load(state, 0, layer, r), load(state, 1, layer, r)
            ay_right = right_of(ay, beside(0, layer, r))
            to = pl.ds(r, 8)
            field[0, layer, to, :] = ay - load(state, 1, layer + 1, r)
            field[1, layer, to, :] = load(state, 0, layer + 1, r) - ax
            field[2, layer, to, :] = ay_right - ay - (load(state, 0, layer, r + 1) - ax)
        return 0

    def currents(layer, r, at):
        bx, by, bz = (load(field, c, layer, r) for c in range(3))
        by_left = left_of(by, beside(at, layer, r))
        bz_left = left_of(bz, beside(at + 1, layer, r))
        jx = bz - load(field, 2, layer, r - 1) - (by - load(field, 1, layer - 1, r))
        jy = bx - load(field, 0, layer - 1, r) - (bz - bz_left)
        jz = by - by_left - (bx - load(field, 0, layer, r - 1))
        return (bx, by, bz), (jx, jy, jz)

    def first_push(layer, _):
        for tile in range(5):
            r = PAD - 1 + 8 * tile
            b, j = currents(layer, r, 0)
            a = [load(state, c, layer, r) for c in range(2)]
            a.append(jnp.zeros_like(a[0]))
            for c, value in enumerate(push(a, b, j)):
                later[c, layer, pl.ds(r, 8), :] = value
        return 0

    def second_field(layer, _):
        for tile in range(5):
            r = PAD - 1 + 8 * tile
            ax, ay, az = (load(later, c, layer, r) for c in range(3))
            ay_right = right_of(ay, beside(2, layer, r))
            az_right = right_of(az, beside(3, layer, r))
            to = pl.ds(r, 8)
            field[0, layer, to, :] = (
                load(later, 2, layer, r + 1) - az - (load(later, 1, layer + 1, r) - ay)
            )
            field[1, layer, to, :] = load(later, 0, layer + 1, r) - ax - (az_right - az)
            field[2, layer, to, :] = ay_right - ay - (load(later, 0, layer, r + 1) - ax)
        return 0

    def second_push(layer, _):
        for tile in range(height // 8):
            r = PAD + 8 * tile
            b, j = currents(layer, r, 2)
            a = [load(later, c, layer, r) for c in range(3)]
            for c, value in enumerate(push(a, b, j)):
                out[c, layer - 2, pl.ds(8 * tile, 8), :] = spacing * value
        return 0

    lax.fori_loop(0, depth + 3, first_field, 0)
    lax.fori_loop(1, depth + 3, first_push, 0)

    zeros = jnp.zeros((height + 8, LANES), jnp.float32)
    line = jnp.zeros((layers, LANES), jnp.float32)
    for c in range(3):
        for exists, layer in ((z > 0, 1), (z < count_z - 1, depth + 2)):

            @pl.when(jnp.logical_not(exists))
            def _():
                later[c, layer, pl.ds(PAD - 1, height + 8), :] = zeros

        for exists, row in ((y > 0, PAD - 1), (y < count_y - 1, PAD + height)):

            @pl.when(jnp.logical_not(exists))
            def _():
                flat_later = later.at[c].reshape(layers * padded, LANES)
                flat_later[pl.ds(row, layers, stride=padded), :] = line

    lax.fori_loop(1, depth + 2, second_field, 0)
    lax.fori_loop(2, depth + 2, second_push, 0)


def call(kernel, shapes, args, scratch=(), limit=16):
    vmem = pl.BlockSpec(memory_space=pltpu.VMEM)
    return pl.pallas_call(
        kernel,
        out_shape=[jax.ShapeDtypeStruct(shape, jnp.float32) for shape in shapes],
        in_specs=[pl.BlockSpec(memory_space=pltpu.SMEM)] + [vmem] * (len(args) - 1),
        out_specs=[vmem] * len(shapes),
        scratch_shapes=[pltpu.VMEM(shape, jnp.float32) for shape in scratch],
        compiler_params=pltpu.CompilerParams(vmem_limit_bytes=limit * 2**20),
    )(*args)


def gathered_carries(rows, columns):
    height, width = rows.shape
    x, y = lax.axis_index("gx"), lax.axis_index("gy")
    row_totals = lax.all_gather(rows[:, -1], "gx")
    before = (jnp.arange(row_totals.shape[0]) < x)[:, None]
    row_carry = jnp.sum(jnp.where(before, row_totals, 0.0), axis=0)
    column_totals = lax.all_gather(columns[-1], "gy")
    before = (jnp.arange(column_totals.shape[0]) < y)[:, None]
    column_carry = jnp.sum(jnp.where(before, column_totals, 0.0), axis=0)
    return (
        jnp.broadcast_to(row_carry[:, None], (height, width)),
        jnp.broadcast_to(column_carry[None], (8, width)),
    )


def local(side, mag):
    counts = tuple(lax.axis_size(axis) for axis in ("gz", "gy", "gx"))
    count_z, count_y, count_x = counts
    _, depth, height, width = side.shape
    place = jnp.stack([lax.axis_index(axis) for axis in ("gz", "gy", "gx")]).astype(jnp.int32)
    plane, block = (height, width), (2, height, width)

    first, second, total, rows, columns = call(
        totals_kernel, [(2, 2) + plane, (2, 2) + plane, block, plane, plane], [place, side, mag]
    )
    first = swap_first(first, "gz")
    second = swap_second(second, "gz") if count_z > 2 else first
    others = [
        swap(total, "gz", functools.partial(lambda step, i: i ^ step, step))
        for step in far_steps(count_z)
    ]
    direct = count_y == 2 and count_x in (2, 4)
    if direct:
        column_carry = swap_first(columns[-8:], "gy")
    else:
        row_carry, column_carry = gathered_carries(rows, columns)
    packed, edges = call(
        lambda _, *refs: pack_kernel(*refs),
        [(2, height, 2 * LANES), (2, 4, depth, width)],
        [place, side],
        [(2, depth * height, width)],
    )
    far = len(others)
    packed, ext, base = call(
        functools.partial(z_kernel, count_z, depth, far),
        [(2, height, 2 * LANES), (2, 4) + plane, plane],
        [place, first, second, total, columns, column_carry, rows, packed, *others],
    )
    first = swap_first(packed, "gx")
    second = swap_second(packed, "gx") if count_x > 2 else first
    if not direct:
        far_rows = row_carry
    elif count_x == 4:
        far_rows = swap(rows, "gx", lambda i: i ^ 2)
    else:
        far_rows = rows
    messages = 1 if count_y == 2 else 2
    message_rows = 4 * slot_rows(depth) + 16
    strips, flat, ext, edge_rows = call(
        functools.partial(x_kernel, counts, depth),
        [(2, height, 4 * LANES), block, (2, 4) + plane, (messages, message_rows, width)],
        [place, packed, first, second, far_rows, rows, base, ext, edges],
    )
    first = swap_first(edge_rows[0], "gy")
    second = swap_second(edge_rows[1], "gy") if count_y > 2 else first
    layers, padded = depth + 4, height + 2 * PAD
    (result,) = call(
        functools.partial(step_kernel, counts),
        [(3, depth) + plane],
        [place, side, flat, ext, strips, first, second],
        [
            (2, layers, padded, width),
            (3, layers, padded, width),
            (3, layers, padded, width),
            (4, 2, padded, LANES),
            (2, padded, 4 * LANES),
        ],
        limit=24,
    )
    return result


def solution(mesh):
    return jax.shard_map(
        local,
        mesh=mesh,
        in_specs=(P(None, "gz", "gy", "gx"), P("gy", "gx")),
        out_specs=P(None, "gz", "gy", "gx"),
        check_vma=False,
    )
```

```python
import functools

import jax
import jax.numpy as jnp
from jax import lax
from jax.experimental import pallas as pl
from jax.experimental.pallas import tpu as pltpu
from jax.sharding import PartitionSpec as P

spacing = 0.0625
friction = 0.004
gain = friction / (spacing * spacing)
LANES = 128
PAD = 8
GROUP = LANES // 4


def near(index, count):
    return (index + 1) % count if index % 2 else (index - 1) % count


def swap(part, axis, partner):
    count = lax.axis_size(axis)
    return lax.ppermute(part, axis, [(i, partner(i)) for i in range(count)])


def swap_first(part, axis):
    return swap(part, axis, lambda i: i ^ 1)


def swap_second(part, axis):
    count = lax.axis_size(axis)
    return swap(part, axis, lambda i: near(i, count))


def far_steps(count):
    return [2] if count == 4 else list(range(2, count))


def lane_index(shape):
    return lax.broadcasted_iota(jnp.int32, shape, len(shape) - 1)


def row_index(shape):
    return lax.broadcasted_iota(jnp.int32, shape, len(shape) - 2)


def columns_at(values, slot):
    first = 4 * (slot % GROUP)
    rolled = pltpu.roll(values, (first + 2) % LANES, 1)
    lane = lane_index(values.shape)
    return jnp.where((lane >= first) & (lane < first + 4), rolled, 0.0)


def spread(values, first):
    lane = lane_index(values.shape)
    moved = pltpu.roll(values, (LANES - first) % LANES, 1) if first else values
    result = jnp.where(lane < 4, moved, 0.0)
    step = 4
    while step < LANES:
        result = result + pltpu.roll(result, step, 1)
        step *= 2
    return result


def totals_kernel(place, side, mag, first_out, second_out, total_out, rows_out, columns_out):
    depth = side.shape[1]
    z = place[0]
    for c in range(2):
        low0 = side[c, 0]
        low1 = low0 + side[c, 1]
        before = low1
        for layer in range(2, depth - 1):
            before = before + side[c, layer]
        total = before + side[c, depth - 1]
        odd = z % 2 == 1
        first_out[c, 0] = jnp.where(odd, low0, before)
        first_out[c, 1] = jnp.where(odd, low1, total)
        upward = odd | (z == 0)
        second_out[c, 0] = jnp.where(upward, before, low0)
        second_out[c, 1] = jnp.where(upward, total, low1)
        total_out[c] = total
    rows = mag[...]
    lane = lane_index(rows.shape)
    step = 1
    while step < LANES:
        rows = rows + jnp.where(lane >= step, pltpu.roll(rows, step, 1), 0.0)
        step *= 2
    rows_out[...] = rows
    columns = mag[...]
    row = row_index(columns.shape)
    step = 1
    while step < columns.shape[0]:
        columns = columns + jnp.where(row >= step, pltpu.roll(columns, step, 0), 0.0)
        step *= 2
    columns_out[...] = columns


def pack_kernel(side, packed_out, rows_out, running):
    depth, height = side.shape[1], side.shape[2]
    for c in range(2):
        total = jnp.zeros(side.shape[2:], jnp.float32)
        packed = [jnp.zeros(side.shape[2:], jnp.float32) for _ in range(2)]
        for layer in range(depth):
            total = total + side[c, layer]
            running[c, pl.ds(layer * height, height), :] = total
            slot = layer + 2
            packed[slot // GROUP] += columns_at(total, slot)
        for tile in range(2):
            packed_out[c, :, pl.ds(tile * LANES, LANES)] = packed[tile]
        for k, row in enumerate((0, 1, height - 2, height - 1)):
            rows_out[c, k] = running[c, pl.ds(row, depth, stride=height), :]


def z_kernel(
    count, depth, far, place, first, second, total, columns, column_carry, rows, packed, *rest
):
    others, (x_out, ext_out, base_out) = rest[:far], rest[far:]
    z, y = place[0], place[1]
    odd = z % 2 == 1
    for c in range(2):
        near_a, near_b = (first[c, 0], first[c, 1]), (second[c, 0], second[c, 1])
        low = [jnp.where(odd, a, b) for a, b in zip(near_a, near_b)]
        high = [jnp.where(odd, b, a) for a, b in zip(near_a, near_b)]
        carry = jnp.where(odd, near_a[1], 0.0)
        if count == 4:
            carry = carry + jnp.where((z == 2) | (z == 3), near_b[1], 0.0)
        for step, other in zip(far_steps(count), others):
            carry = carry + jnp.where((z ^ step) < z, other[c], 0.0)
        above = carry + total[c]
        layers = (carry - (low[1] - low[0]), carry, above + high[0], above + high[1])
        for k in range(4):
            ext_out[c, k] = layers[k]
        if c == 0:
            base = rows[...]
        else:
            base = -0.5 * (columns[...] + jnp.where(y > 0, column_carry[7:8, :], 0.0))
            base_out[...] = base
        lane = lane_index(carry.shape)
        everywhere = spread(pltpu.roll(carry, 2, 1), 0)
        for tile in range(2):
            slot = lane // 4 + tile * GROUP
            values = packed[c, :, pl.ds(tile * LANES, LANES)]
            inside = (slot >= 2) & (slot < depth + 2)
            values = values + jnp.where(inside, everywhere, 0.0)
            for k, at in enumerate((0, 1, depth + 2, depth + 3)):
                if at // GROUP == tile:
                    values = values + columns_at(layers[k], at)
            if (depth + 4) // GROUP == tile:
                values = values + columns_at(base, depth + 4)
            x_out[c, :, pl.ds(tile * LANES, LANES)] = values


def x_kernel(
    counts, depth, place, packed, first, second, far_rows, rows, base, ext, edges,
    strips_out, flat_out, ext_out, y_out,
):
    count_z, count_y, count_x = counts
    height = packed.shape[1]
    z, y, x = place[0], place[1], place[2]
    odd = x % 2 == 1
    base_tile, base_lane = (depth + 4) // GROUP, 4 * ((depth + 4) % GROUP)

    def tile_of(ref, c, tile):
        return ref[c, :, pl.ds(tile * LANES, LANES)]

    def row_totals(ref):
        return tile_of(ref, 0, base_tile)[:, base_lane + 1 : base_lane + 2]

    own_total = rows[...][:, LANES - 1 :]
    total_a, total_b = row_totals(first), row_totals(second)
    far_total = far_rows[...][:, LANES - 1 :]
    if count_x == 2:
        row_carry = jnp.where(odd, total_a, 0.0)
    elif count_x == 4:
        row_carry = jnp.where(odd, total_a, 0.0) + jnp.where(x >= 2, total_b + far_total, 0.0)
    else:
        row_carry = far_total
    left_total = jnp.where(odd, total_a, total_b)

    lane = lane_index((height, LANES))
    q = lane % 4
    for part in range(2):
        merged = []
        for c in range(2):
            tiles = []
            for tile in range(2):
                own, a, b = (tile_of(ref, c, tile) for ref in (packed, first, second))
                if part == 0:
                    tiles.append(jnp.where(q < 2, jnp.where(odd, a, b), own))
                else:
                    tiles.append(jnp.where(q < 2, own, jnp.where(odd, b, a)))
            merged.append(tiles)
        if part == 0:
            carry = jnp.where(q < 2, row_carry - left_total, row_carry)
        else:
            carry = jnp.where(q < 2, row_carry, row_carry + own_total)
        base_y = 0.5 * (spread(merged[0][base_tile], base_lane) + carry)
        base_x = spread(merged[1][base_tile], base_lane)
        for tile in range(2):
            slot = lane // 4 + tile * GROUP
            inside = (slot < depth + 4) & ((slot >= 2) | (z > 0))
            inside = inside & ((slot < depth + 2) | (z < count_z - 1))
            if part == 0:
                inside = inside & ((q >= 2) | (x > 0))
            else:
                inside = inside & ((q < 2) | (x < count_x - 1))
            place_at = pl.ds((part * 2 + tile) * LANES, LANES)
            strips_out[0, :, place_at] = jnp.where(inside, base_x + merged[1][tile], 0.0)
            strips_out[1, :, place_at] = jnp.where(inside, base_y - merged[0][tile], 0.0)

    base_x = base[...]
    base_y = 0.5 * (rows[...] + row_carry)
    flat_out[0] = base_x + ext[1, 1]
    flat_out[1] = base_y - ext[0, 1]
    for k in range(4):
        inside = (z > 0) if k < 2 else (z < count_z - 1)
        ext_out[0, k] = jnp.where(inside, base_x + ext[1, k], 0.0)
        ext_out[1, k] = jnp.where(inside, base_y - ext[0, k], 0.0)

    slots = slot_rows(depth)
    for message in range(y_out.shape[0]):
        downward = (y % 2 == 1) if message == 0 else (y % 2 == 0)
        for c in range(2):
            for r in range(2):
                start = (c * 2 + r) * slots
                low, high = pl.ds(r, 1), pl.ds(height - 2 + r, 1)
                flat = jnp.where(downward, flat_out[c, low, :], flat_out[c, high, :])
                edge = jnp.where(downward, edges[1 - c, r], edges[1 - c, 2 + r])
                edge = edge if c == 0 else -edge
                y_out[message, pl.ds(start + 2, depth), :] = flat + edge
                for k, at in enumerate((0, 1, depth + 2, depth + 3)):
                    y_out[message, pl.ds(start + at, 1), :] = jnp.where(
                        downward, ext_out[c, k, low, :], ext_out[c, k, high, :]
                    )
            for tile in range(4):
                start = 4 * slots + (c * 4 + tile) * 2
                lanes = pl.ds(tile * LANES, LANES)
                y_out[message, pl.ds(start, 2), :] = jnp.where(
                    downward,
                    strips_out[c, pl.ds(0, 2), lanes],
                    strips_out[c, pl.ds(height - 2, 2), lanes],
                )


def slot_rows(depth):
    return (depth + 4 + 7) // 8 * 8


def following(values, axis, step=1):
    return pltpu.roll(values, values.shape[axis] - step, axis)


def preceding(values, axis, step=1):
    return pltpu.roll(values, step, axis)


def push(a, field, current):
    square = field[0] * field[0] + field[1] * field[1] + field[2] * field[2]
    along = current[0] * field[0] + current[1] * field[1] + current[2] * field[2]
    factor = gain / (square + 1.0)
    p, q = along * factor, square * factor
    return [a[c] + (field[c] * p - current[c] * q) for c in range(3)]


def strip_field(a):
    x, y, z = a
    field_x = following(z, 0) - z - (following(y, 1, 4) - y)
    field_y = following(x, 1, 4) - x - (following(z, 1) - z)
    field_z = following(y, 1) - y - (following(x, 0) - x)
    return field_x, field_y, field_z


def strip_current(b):
    x, y, z = b
    current_x = z - preceding(z, 0) - (y - preceding(y, 1, 4))
    current_y = x - preceding(x, 1, 4) - (z - preceding(z, 1))
    current_z = y - preceding(y, 1) - (x - preceding(x, 0))
    return current_x, current_y, current_z


def step_kernel(
    counts, place, side, flat, ext, strips, first, second, out, state, field, later, halo, wide
):
    count_z, count_y, count_x = counts
    depth, height = side.shape[1], side.shape[2]
    z, y, x = place[0], place[1], place[2]
    slots = slot_rows(depth)
    layers = depth + 4
    padded = state.shape[2]
    odd = y % 2 == 1

    sums = [jnp.zeros((height, LANES), jnp.float32) for _ in range(2)]
    rows = pl.ds(PAD, height)
    for c in range(2):
        for k, at in enumerate((0, 1, depth + 2, depth + 3)):
            state[c, at, rows, :] = ext[c, k]

    for layer in range(depth):
        sums = [total + side[c, layer] for c, total in enumerate(sums)]
        state[0, layer + 2, rows, :] = flat[0] + sums[1]
        state[1, layer + 2, rows, :] = flat[1] - sums[0]

    for low in (True, False):
        exists = (y > 0) if low else (y < count_y - 1)
        row = PAD - 2 if low else PAD + height
        for c in range(2):
            flat_state = state.at[c].reshape(layers * padded, LANES)
            for r in range(2):
                take = pl.ds((c * 2 + r) * slots, layers)
                a, b = first[take, :], second[take, :]
                value = jnp.where(odd, a, b) if low else jnp.where(odd, b, a)
                flat_state[pl.ds(row + r, layers, stride=padded), :] = jnp.where(exists, value, 0.0)
            for tile in range(4):
                take = pl.ds(4 * slots + (c * 4 + tile) * 2, 2)
                a, b = first[take, :], second[take, :]
                value = jnp.where(odd, a, b) if low else jnp.where(odd, b, a)
                wide[c, pl.ds(row, 2), pl.ds(tile * LANES, LANES)] = jnp.where(exists, value, 0.0)
    wide[0, rows, :] = strips[0]
    wide[1, rows, :] = strips[1]

    half = 2 * LANES
    lane = lane_index((padded, 2 * half))
    row = row_index((padded, 2 * half))
    q = lane % 4
    slot = (lane % half) // 4
    right = lane >= half
    inside = (row >= PAD - 2) & (row < PAD + height + 2) & (slot < layers)
    inside = inside & ((row >= PAD) | (y > 0)) & ((row < PAD + height) | (y < count_y - 1))
    inside = inside & ((slot >= 2) | (z > 0)) & ((slot < depth + 2) | (z < count_z - 1))
    inside = inside & (right | (q >= 2) | (x > 0))
    inside = inside & (~right | (q < 2) | (x < count_x - 1))
    a = [jnp.where(inside, wide[c], 0.0) for c in range(2)]
    a.append(jnp.zeros_like(a[0]))
    b = strip_field(a)
    pick = (lane_index((padded, half)) % 4) == 2

    def keep(at, upper, lower):
        value = jnp.where(pick, upper[:, half:], lower[:, :half])
        halo[at, 0] = value[:, :LANES]
        halo[at, 1] = value[:, LANES:]

    keep(0, a[1], b[1])
    keep(1, a[2], b[2])
    a = [jnp.where(inside, value, 0.0) for value in push(a, b, strip_current(b))]
    b = strip_field(a)
    keep(2, a[1], b[1])
    keep(3, a[2], b[2])

    lane = lane_index((8, LANES))
    last, start = lane == LANES - 1, lane == 0

    def beside(at, layer, row):
        shift = LANES - 2 - 4 * (layer % GROUP)
        return pltpu.roll(halo[at, layer // GROUP, pl.ds(row, 8), :], shift, 1)

    def right_of(value, edge):
        return following(jnp.where(start, edge, value), 1)

    def left_of(value, edge):
        return preceding(jnp.where(last, edge, value), 1)

    def load(ref, c, layer, row):
        return ref[c, layer, pl.ds(row, 8), :]

    def first_field(layer):
        for tile in range(5):
            r = PAD - 2 + 8 * tile
            ax, ay = load(state, 0, layer, r), load(state, 1, layer, r)
            ay_right = right_of(ay, beside(0, layer, r))
            to = pl.ds(r, 8)
            field[0, layer, to, :] = ay - load(state, 1, layer + 1, r)
            field[1, layer, to, :] = load(state, 0, layer + 1, r) - ax
            field[2, layer, to, :] = ay_right - ay - (load(state, 0, layer, r + 1) - ax)

    def currents(layer, r, at):
        bx, by, bz = (load(field, c, layer, r) for c in range(3))
        by_left = left_of(by, beside(at, layer, r))
        bz_left = left_of(bz, beside(at + 1, layer, r))
        jx = bz - load(field, 2, layer, r - 1) - (by - load(field, 1, layer - 1, r))
        jy = bx - load(field, 0, layer - 1, r) - (bz - bz_left)
        jz = by - by_left - (bx - load(field, 0, layer, r - 1))
        return (bx, by, bz), (jx, jy, jz)

    def first_push(layer):
        for tile in range(5):
            r = PAD - 1 + 8 * tile
            b, j = currents(layer, r, 0)
            a = [load(state, c, layer, r) for c in range(2)]
            a.append(jnp.zeros_like(a[0]))
            for c, value in enumerate(push(a, b, j)):
                later[c, layer, pl.ds(r, 8), :] = value

    def second_field(layer):
        for tile in range(5):
            r = PAD - 1 + 8 * tile
            ax, ay, az = (load(later, c, layer, r) for c in range(3))
            ay_right = right_of(ay, beside(2, layer, r))
            az_right = right_of(az, beside(3, layer, r))
            to = pl.ds(r, 8)
            field[0, layer, to, :] = (
                load(later, 2, layer, r + 1) - az - (load(later, 1, layer + 1, r) - ay)
            )
            field[1, layer, to, :] = load(later, 0, layer + 1, r) - ax - (az_right - az)
            field[2, layer, to, :] = ay_right - ay - (load(later, 0, layer, r + 1) - ax)

    def second_push(layer):
        for tile in range(height // 8):
            r = PAD + 8 * tile
            b, j = currents(layer, r, 2)
            a = [load(later, c, layer, r) for c in range(3)]
            for c, value in enumerate(push(a, b, j)):
                out[c, layer - 2, pl.ds(8 * tile, 8), :] = spacing * value

    for layer in range(0, depth + 3):
        first_field(layer)
    for layer in range(1, depth + 3):
        first_push(layer)

    zeros = jnp.zeros((height + 8, LANES), jnp.float32)
    line = jnp.zeros((layers, LANES), jnp.float32)
    for c in range(3):
        for exists, layer in ((z > 0, 1), (z < count_z - 1, depth + 2)):

            @pl.when(jnp.logical_not(exists))
            def _():
                later[c, layer, pl.ds(PAD - 1, height + 8), :] = zeros

        for exists, row in ((y > 0, PAD - 1), (y < count_y - 1, PAD + height)):

            @pl.when(jnp.logical_not(exists))
            def _():
                flat_later = later.at[c].reshape(layers * padded, LANES)
                flat_later[pl.ds(row, layers, stride=padded), :] = line

    for layer in range(1, depth + 2):
        second_field(layer)
    for layer in range(2, depth + 2):
        second_push(layer)


def call(kernel, shapes, args, scratch=(), limit=16):
    vmem = pl.BlockSpec(memory_space=pltpu.VMEM)
    return pl.pallas_call(
        kernel,
        out_shape=[jax.ShapeDtypeStruct(shape, jnp.float32) for shape in shapes],
        in_specs=[pl.BlockSpec(memory_space=pltpu.SMEM)] + [vmem] * (len(args) - 1),
        out_specs=[vmem] * len(shapes),
        scratch_shapes=[pltpu.VMEM(shape, jnp.float32) for shape in scratch],
        compiler_params=pltpu.CompilerParams(vmem_limit_bytes=limit * 2**20),
    )(*args)


def gathered_carries(rows, columns):
    height, width = rows.shape
    x, y = lax.axis_index("gx"), lax.axis_index("gy")
    row_totals = lax.all_gather(rows[:, -1], "gx")
    before = (jnp.arange(row_totals.shape[0]) < x)[:, None]
    row_carry = jnp.sum(jnp.where(before, row_totals, 0.0), axis=0)
    column_totals = lax.all_gather(columns[-1], "gy")
    before = (jnp.arange(column_totals.shape[0]) < y)[:, None]
    column_carry = jnp.sum(jnp.where(before, column_totals, 0.0), axis=0)
    return (
        jnp.broadcast_to(row_carry[:, None], (height, width)),
        jnp.broadcast_to(column_carry[None], (8, width)),
    )


def local(side, mag):
    counts = tuple(lax.axis_size(axis) for axis in ("gz", "gy", "gx"))
    count_z, count_y, count_x = counts
    _, depth, height, width = side.shape
    place = jnp.stack([lax.axis_index(axis) for axis in ("gz", "gy", "gx")]).astype(jnp.int32)
    plane, block = (height, width), (2, height, width)

    first, second, total, rows, columns = call(
        totals_kernel, [(2, 2) + plane, (2, 2) + plane, block, plane, plane], [place, side, mag]
    )
    first = swap_first(first, "gz")
    second = swap_second(second, "gz") if count_z > 2 else first
    others = [
        swap(total, "gz", functools.partial(lambda step, i: i ^ step, step))
        for step in far_steps(count_z)
    ]
    direct = count_y == 2 and count_x in (2, 4)
    if direct:
        column_carry = swap_first(columns[-8:], "gy")
    else:
        row_carry, column_carry = gathered_carries(rows, columns)
    packed, edges = call(
        lambda _, *refs: pack_kernel(*refs),
        [(2, height, 2 * LANES), (2, 4, depth, width)],
        [place, side],
        [(2, depth * height, width)],
    )
    far = len(others)
    packed, ext, base = call(
        functools.partial(z_kernel, count_z, depth, far),
        [(2, height, 2 * LANES), (2, 4) + plane, plane],
        [place, first, second, total, columns, column_carry, rows, packed, *others],
    )
    first = swap_first(packed, "gx")
    second = swap_second(packed, "gx") if count_x > 2 else first
    if not direct:
        far_rows = row_carry
    elif count_x == 4:
        far_rows = swap(rows, "gx", lambda i: i ^ 2)
    else:
        far_rows = rows
    messages = 1 if count_y == 2 else 2
    message_rows = 4 * slot_rows(depth) + 16
    strips, flat, ext, edge_rows = call(
        functools.partial(x_kernel, counts, depth),
        [(2, height, 4 * LANES), block, (2, 4) + plane, (messages, message_rows, width)],
        [place, packed, first, second, far_rows, rows, base, ext, edges],
    )
    first = swap_first(edge_rows[0], "gy")
    second = swap_second(edge_rows[1], "gy") if count_y > 2 else first
    layers, padded = depth + 4, height + 2 * PAD
    (result,) = call(
        functools.partial(step_kernel, counts),
        [(3, depth) + plane],
        [place, side, flat, ext, strips, first, second],
        [
            (2, layers, padded, width),
            (3, layers, padded, width),
            (3, layers, padded, width),
            (4, 2, padded, LANES),
            (2, padded, 4 * LANES),
        ],
        limit=24,
    )
    return result


def solution(mesh):
    return jax.shard_map(
        local,
        mesh=mesh,
        in_specs=(P(None, "gz", "gy", "gx"), P("gy", "gx")),
        out_specs=P(None, "gz", "gy", "gx"),
        check_vma=False,
    )
```

```python
import functools

import jax
import jax.numpy as jnp
from jax import lax
from jax.experimental import pallas as pl
from jax.experimental.pallas import tpu as pltpu
from jax.sharding import PartitionSpec as P

spacing = 0.0625
friction = 0.004
gain = friction / (spacing * spacing)
LANES = 128
PAD = 8
GROUP = LANES // 4


def near(index, count):
    return (index + 1) % count if index % 2 else (index - 1) % count


def swap(part, axis, partner):
    count = lax.axis_size(axis)
    return lax.ppermute(part, axis, [(i, partner(i)) for i in range(count)])


def swap_first(part, axis):
    return swap(part, axis, lambda i: i ^ 1)


def swap_second(part, axis):
    count = lax.axis_size(axis)
    return swap(part, axis, lambda i: near(i, count))


def far_steps(count):
    return [2] if count == 4 else list(range(2, count))


def lane_index(shape):
    return lax.broadcasted_iota(jnp.int32, shape, len(shape) - 1)


def row_index(shape):
    return lax.broadcasted_iota(jnp.int32, shape, len(shape) - 2)


def columns_at(values, slot):
    first = 4 * (slot % GROUP)
    rolled = pltpu.roll(values, (first + 2) % LANES, 1)
    lane = lane_index(values.shape)
    return jnp.where((lane >= first) & (lane < first + 4), rolled, 0.0)


def spread(values, first):
    lane = lane_index(values.shape)
    moved = pltpu.roll(values, (LANES - first) % LANES, 1) if first else values
    result = jnp.where(lane < 4, moved, 0.0)
    step = 4
    while step < LANES:
        result = result + pltpu.roll(result, step, 1)
        step *= 2
    return result


def totals_kernel(place, side, mag, first_out, second_out, total_out, rows_out, columns_out):
    depth = side.shape[1]
    z = place[0]
    for c in range(2):
        low0 = side[c, 0]
        low1 = low0 + side[c, 1]
        before = low1
        for layer in range(2, depth - 1):
            before = before + side[c, layer]
        total = before + side[c, depth - 1]
        odd = z % 2 == 1
        first_out[c, 0] = jnp.where(odd, low0, before)
        first_out[c, 1] = jnp.where(odd, low1, total)
        upward = odd | (z == 0)
        second_out[c, 0] = jnp.where(upward, before, low0)
        second_out[c, 1] = jnp.where(upward, total, low1)
        total_out[c] = total
    rows = mag[...]
    lane = lane_index(rows.shape)
    step = 1
    while step < LANES:
        rows = rows + jnp.where(lane >= step, pltpu.roll(rows, step, 1), 0.0)
        step *= 2
    rows_out[...] = rows
    columns = mag[...]
    row = row_index(columns.shape)
    step = 1
    while step < columns.shape[0]:
        columns = columns + jnp.where(row >= step, pltpu.roll(columns, step, 0), 0.0)
        step *= 2
    columns_out[...] = columns


def pack_kernel(side, packed_out, rows_out, running):
    depth, height = side.shape[1], side.shape[2]
    for c in range(2):
        total = jnp.zeros(side.shape[2:], jnp.float32)
        packed = [jnp.zeros(side.shape[2:], jnp.float32) for _ in range(2)]
        for layer in range(depth):
            total = total + side[c, layer]
            running[c, pl.ds(layer * height, height), :] = total
            slot = layer + 2
            packed[slot // GROUP] += columns_at(total, slot)
        for tile in range(2):
            packed_out[c, :, pl.ds(tile * LANES, LANES)] = packed[tile]
        for k, row in enumerate((0, 1, height - 2, height - 1)):
            rows_out[c, k] = running[c, pl.ds(row, depth, stride=height), :]


def z_kernel(
    count, depth, far, place, first, second, total, columns, column_carry, rows, packed, *rest
):
    others, (x_out, ext_out, base_out) = rest[:far], rest[far:]
    z, y = place[0], place[1]
    odd = z % 2 == 1
    for c in range(2):
        near_a, near_b = (first[c, 0], first[c, 1]), (second[c, 0], second[c, 1])
        low = [jnp.where(odd, a, b) for a, b in zip(near_a, near_b)]
        high = [jnp.where(odd, b, a) for a, b in zip(near_a, near_b)]
        carry = jnp.where(odd, near_a[1], 0.0)
        if count == 4:
            carry = carry + jnp.where((z == 2) | (z == 3), near_b[1], 0.0)
        for step, other in zip(far_steps(count), others):
            carry = carry + jnp.where((z ^ step) < z, other[c], 0.0)
        above = carry + total[c]
        layers = (carry - (low[1] - low[0]), carry, above + high[0], above + high[1])
        for k in range(4):
            ext_out[c, k] = layers[k]
        if c == 0:
            base = rows[...]
        else:
            base = -0.5 * (columns[...] + jnp.where(y > 0, column_carry[7:8, :], 0.0))
            base_out[...] = base
        lane = lane_index(carry.shape)
        everywhere = spread(pltpu.roll(carry, 2, 1), 0)
        for tile in range(2):
            slot = lane // 4 + tile * GROUP
            values = packed[c, :, pl.ds(tile * LANES, LANES)]
            inside = (slot >= 2) & (slot < depth + 2)
            values = values + jnp.where(inside, everywhere, 0.0)
            for k, at in enumerate((0, 1, depth + 2, depth + 3)):
                if at // GROUP == tile:
                    values = values + columns_at(layers[k], at)
            if (depth + 4) // GROUP == tile:
                values = values + columns_at(base, depth + 4)
            x_out[c, :, pl.ds(tile * LANES, LANES)] = values


def x_kernel(
    counts, depth, place, packed, first, second, far_rows, rows, base, ext, edges,
    strips_out, flat_out, ext_out, y_out,
):
    count_z, count_y, count_x = counts
    height = packed.shape[1]
    z, y, x = place[0], place[1], place[2]
    odd = x % 2 == 1
    base_tile, base_lane = (depth + 4) // GROUP, 4 * ((depth + 4) % GROUP)

    def tile_of(ref, c, tile):
        return ref[c, :, pl.ds(tile * LANES, LANES)]

    def row_totals(ref):
        return tile_of(ref, 0, base_tile)[:, base_lane + 1 : base_lane + 2]

    own_total = rows[...][:, LANES - 1 :]
    total_a, total_b = row_totals(first), row_totals(second)
    far_total = far_rows[...][:, LANES - 1 :]
    if count_x == 2:
        row_carry = jnp.where(odd, total_a, 0.0)
    elif count_x == 4:
        row_carry = jnp.where(odd, total_a, 0.0) + jnp.where(x >= 2, total_b + far_total, 0.0)
    else:
        row_carry = far_total
    left_total = jnp.where(odd, total_a, total_b)

    lane = lane_index((height, LANES))
    q = lane % 4
    for part in range(2):
        merged = []
        for c in range(2):
            tiles = []
            for tile in range(2):
                own, a, b = (tile_of(ref, c, tile) for ref in (packed, first, second))
                if part == 0:
                    tiles.append(jnp.where(q < 2, jnp.where(odd, a, b), own))
                else:
                    tiles.append(jnp.where(q < 2, own, jnp.where(odd, b, a)))
            merged.append(tiles)
        if part == 0:
            carry = jnp.where(q < 2, row_carry - left_total, row_carry)
        else:
            carry = jnp.where(q < 2, row_carry, row_carry + own_total)
        base_y = 0.5 * (spread(merged[0][base_tile], base_lane) + carry)
        base_x = spread(merged[1][base_tile], base_lane)
        for tile in range(2):
            slot = lane // 4 + tile * GROUP
            inside = (slot < depth + 4) & ((slot >= 2) | (z > 0))
            inside = inside & ((slot < depth + 2) | (z < count_z - 1))
            if part == 0:
                inside = inside & ((q >= 2) | (x > 0))
            else:
                inside = inside & ((q < 2) | (x < count_x - 1))
            place_at = pl.ds((part * 2 + tile) * LANES, LANES)
            strips_out[0, :, place_at] = jnp.where(inside, base_x + merged[1][tile], 0.0)
            strips_out[1, :, place_at] = jnp.where(inside, base_y - merged[0][tile], 0.0)

    base_x = base[...]
    base_y = 0.5 * (rows[...] + row_carry)
    flat_out[0] = base_x + ext[1, 1]
    flat_out[1] = base_y - ext[0, 1]
    for k in range(4):
        inside = (z > 0) if k < 2 else (z < count_z - 1)
        ext_out[0, k] = jnp.where(inside, base_x + ext[1, k], 0.0)
        ext_out[1, k] = jnp.where(inside, base_y - ext[0, k], 0.0)

    slots = slot_rows(depth)
    for message in range(y_out.shape[0]):
        downward = (y % 2 == 1) if message == 0 else (y % 2 == 0)
        for c in range(2):
            for r in range(2):
                start = (c * 2 + r) * slots
                low, high = pl.ds(r, 1), pl.ds(height - 2 + r, 1)
                flat = jnp.where(downward, flat_out[c, low, :], flat_out[c, high, :])
                edge = jnp.where(downward, edges[1 - c, r], edges[1 - c, 2 + r])
                edge = edge if c == 0 else -edge
                y_out[message, pl.ds(start + 2, depth), :] = flat + edge
                for k, at in enumerate((0, 1, depth + 2, depth + 3)):
                    y_out[message, pl.ds(start + at, 1), :] = jnp.where(
                        downward, ext_out[c, k, low, :], ext_out[c, k, high, :]
                    )
            for tile in range(4):
                start = 4 * slots + (c * 4 + tile) * 2
                lanes = pl.ds(tile * LANES, LANES)
                y_out[message, pl.ds(start, 2), :] = jnp.where(
                    downward,
                    strips_out[c, pl.ds(0, 2), lanes],
                    strips_out[c, pl.ds(height - 2, 2), lanes],
                )


def slot_rows(depth):
    return (depth + 4 + 7) // 8 * 8


def following(values, axis, step=1):
    return pltpu.roll(values, values.shape[axis] - step, axis)


def preceding(values, axis, step=1):
    return pltpu.roll(values, step, axis)


def push(a, field, current):
    square = field[0] * field[0] + field[1] * field[1] + field[2] * field[2]
    along = current[0] * field[0] + current[1] * field[1] + current[2] * field[2]
    factor = gain / (square + 1.0)
    p, q = along * factor, square * factor
    return [a[c] + (field[c] * p - current[c] * q) for c in range(3)]


def strip_field(a):
    x, y, z = a
    field_x = following(z, 0) - z - (following(y, 1, 4) - y)
    field_y = following(x, 1, 4) - x - (following(z, 1) - z)
    field_z = following(y, 1) - y - (following(x, 0) - x)
    return field_x, field_y, field_z


def strip_current(b):
    x, y, z = b
    current_x = z - preceding(z, 0) - (y - preceding(y, 1, 4))
    current_y = x - preceding(x, 1, 4) - (z - preceding(z, 1))
    current_z = y - preceding(y, 1) - (x - preceding(x, 0))
    return current_x, current_y, current_z


class Stepper:
    def __init__(self, counts, place, state, field, later, halo, depth, height):
        self.counts = counts
        self.z, self.y, self.x = place[0], place[1], place[2]
        self.state, self.field, self.later, self.halo = state, field, later, halo
        self.depth, self.height = depth, height
        self.padded = state.shape[2]
        lane = lane_index((8, LANES))
        self.last, self.start = lane == LANES - 1, lane == 0

    def load(self, ref, c, layer, row):
        return ref[c, layer, pl.ds(row, 8), :]

    def strips(self, wide):
        depth, height = self.depth, self.height
        count_z, count_y, count_x = self.counts
        half = 2 * LANES
        shape = (self.padded, 2 * half)
        lane, row = lane_index(shape), row_index(shape)
        q = lane % 4
        slot = (lane % half) // 4
        right = lane >= half
        inside = (row >= PAD - 2) & (row < PAD + height + 2) & (slot < depth + 4)
        inside = inside & ((row >= PAD) | (self.y > 0))
        inside = inside & ((row < PAD + height) | (self.y < count_y - 1))
        inside = inside & ((slot >= 2) | (self.z > 0))
        inside = inside & ((slot < depth + 2) | (self.z < count_z - 1))
        inside = inside & (right | (q >= 2) | (self.x > 0))
        inside = inside & (~right | (q < 2) | (self.x < count_x - 1))
        a = [jnp.where(inside, wide[c], 0.0) for c in range(2)]
        a.append(jnp.zeros_like(a[0]))
        b = strip_field(a)
        pick = (lane_index((self.padded, half)) % 4) == 2

        def keep(at, upper, lower):
            value = jnp.where(pick, upper[:, half:], lower[:, :half])
            self.halo[at, 0] = value[:, :LANES]
            self.halo[at, 1] = value[:, LANES:]

        keep(0, a[1], b[1])
        keep(1, a[2], b[2])
        a = [jnp.where(inside, value, 0.0) for value in push(a, b, strip_current(b))]
        b = strip_field(a)
        keep(2, a[1], b[1])
        keep(3, a[2], b[2])

    def beside(self, at, layer, row):
        shift = LANES - 2 - 4 * (layer % GROUP)
        return pltpu.roll(self.halo[at, layer // GROUP, pl.ds(row, 8), :], shift, 1)

    def right_of(self, value, edge):
        return following(jnp.where(self.start, edge, value), 1)

    def left_of(self, value, edge):
        return preceding(jnp.where(self.last, edge, value), 1)

    def first_field(self, layer, r):
        load, state = self.load, self.state
        ax, ay = load(state, 0, layer, r), load(state, 1, layer, r)
        ay_right = self.right_of(ay, self.beside(0, layer, r))
        to = pl.ds(r, 8)
        self.field[0, layer, to, :] = ay - load(state, 1, layer + 1, r)
        self.field[1, layer, to, :] = load(state, 0, layer + 1, r) - ax
        self.field[2, layer, to, :] = ay_right - ay - (load(state, 0, layer, r + 1) - ax)

    def currents(self, layer, r, at):
        load, field = self.load, self.field
        bx, by, bz = (load(field, c, layer, r) for c in range(3))
        by_left = self.left_of(by, self.beside(at, layer, r))
        bz_left = self.left_of(bz, self.beside(at + 1, layer, r))
        jx = bz - load(field, 2, layer, r - 1) - (by - load(field, 1, layer - 1, r))
        jy = bx - load(field, 0, layer - 1, r) - (bz - bz_left)
        jz = by - by_left - (bx - load(field, 0, layer, r - 1))
        return (bx, by, bz), (jx, jy, jz)

    def first_push(self, layer, r):
        b, j = self.currents(layer, r, 0)
        a = [self.load(self.state, c, layer, r) for c in range(2)]
        a.append(jnp.zeros_like(a[0]))
        for c, value in enumerate(push(a, b, j)):
            self.later[c, layer, pl.ds(r, 8), :] = value

    def second_field(self, layer, r):
        load, later = self.load, self.later
        ax, ay, az = (load(later, c, layer, r) for c in range(3))
        ay_right = self.right_of(ay, self.beside(2, layer, r))
        az_right = self.right_of(az, self.beside(3, layer, r))
        to = pl.ds(r, 8)
        self.field[0, layer, to, :] = (
            load(later, 2, layer, r + 1) - az - (load(later, 1, layer + 1, r) - ay)
        )
        self.field[1, layer, to, :] = load(later, 0, layer + 1, r) - ax - (az_right - az)
        self.field[2, layer, to, :] = ay_right - ay - (load(later, 0, layer, r + 1) - ax)

    def second_push(self, layer, r):
        b, j = self.currents(layer, r, 2)
        a = [self.load(self.later, c, layer, r) for c in range(3)]
        return [spacing * value for value in push(a, b, j)]

    def clear(self, rows):
        depth, height = self.depth, self.height
        count_z, count_y, _ = self.counts
        zeros = jnp.zeros((height + 8, LANES), jnp.float32)
        line = jnp.zeros((depth + 4, LANES), jnp.float32)
        for exists, layer in ((self.z > 0, 1), (self.z < count_z - 1, depth + 2)):

            @pl.when(jnp.logical_not(exists))
            def _():
                for c in range(3):
                    self.later[c, layer, pl.ds(PAD - 1, height + 8), :] = zeros

        if not rows:
            return
        for exists, row in ((self.y > 0, PAD - 1), (self.y < count_y - 1, PAD + height)):

            @pl.when(jnp.logical_not(exists))
            def _():
                for c in range(3):
                    flat_later = self.later.at[c].reshape((depth + 4) * self.padded, LANES)
                    flat_later[pl.ds(row, depth + 4, stride=self.padded), :] = line

    def run(self, tiles, rows, out, block, sems, pieces=6):
        depth = self.depth
        for layer in range(depth + 3):
            for r in tiles[0]:
                self.first_field(layer, r)
        for layer in range(1, depth + 3):
            for r in tiles[1]:
                self.first_push(layer, r)
        self.clear(rows)
        for layer in range(1, depth + 2):
            for r in tiles[2]:
                self.second_field(layer, r)
        copies = []
        size = depth // pieces
        for piece in range(pieces):
            layers = pl.ds(piece * size, size)
            for layer in range(piece * size, (piece + 1) * size):
                for k, r in enumerate(tiles[3]):
                    for c, value in enumerate(self.second_push(layer + 2, r)):
                        block[c, layer, pl.ds(8 * k, 8), :] = value
            k = 0
            while k < len(tiles[3]):
                run = 1
                while k + run < len(tiles[3]) and tiles[3][k + run] == tiles[3][k] + 8 * run:
                    run += 1
                copies.append(
                    pltpu.make_async_copy(
                        block.at[:, layers, pl.ds(8 * k, 8 * run), :],
                        out.at[:, layers, pl.ds(tiles[3][k] - PAD, 8 * run), :],
                        sems.at[piece, k],
                    )
                )
                copies[-1].start()
                k += run
        for copy in copies:
            copy.wait()


def inner_tiles(height):
    whole = [PAD + r for r in range(0, height, 8)]
    inner = whole[1:-1]
    return whole, whole, [r - 1 for r in inner] + [inner[-1]], inner


def outer_tiles(height):
    top = PAD + height - 8
    return (PAD - 2, top + 1), (PAD - 1, top + 1), (PAD - 1, top), (PAD, top)


def inner_kernel(
    counts, place, side, flat, ext, strips, state, field, later, out, halo, wide, block, sems
):
    depth, height = side.shape[1], side.shape[2]
    rows = pl.ds(PAD, height)
    for c in range(2):
        for k, at in enumerate((0, 1, depth + 2, depth + 3)):
            state[c, at, rows, :] = ext[c, k]
    sums = [jnp.zeros((height, LANES), jnp.float32) for _ in range(2)]
    for layer in range(depth):
        sums = [total + side[c, layer] for c, total in enumerate(sums)]
        state[0, layer + 2, rows, :] = flat[0] + sums[1]
        state[1, layer + 2, rows, :] = flat[1] - sums[0]
    for c in range(2):
        wide[c, rows, :] = strips[c]
        wide[c, pl.ds(0, PAD), :] = jnp.zeros((PAD, wide.shape[2]), jnp.float32)
        wide[c, pl.ds(PAD + height, PAD), :] = jnp.zeros((PAD, wide.shape[2]), jnp.float32)
    stepper = Stepper(counts, place, state, field, later, halo, depth, height)
    stepper.strips(wide)
    stepper.run(inner_tiles(height), False, out, block, sems)


def outer_kernel(
    counts, depth, place, strips, first, second, _s, _f, _l, _o,
    state, field, later, out, halo, wide, block, sems,
):
    _, count_y, _ = counts
    height, padded = strips.shape[1], state.shape[2]
    y = place[1]
    slots = slot_rows(depth)
    layers = depth + 4
    odd = y % 2 == 1
    for low in (True, False):
        exists = (y > 0) if low else (y < count_y - 1)
        row = PAD - 2 if low else PAD + height

        def received(take):
            a, b = first[take, :], second[take, :]
            value = jnp.where(odd, a, b) if low else jnp.where(odd, b, a)
            return jnp.where(exists, value, 0.0)

        for c in range(2):
            flat_state = state.at[c].reshape(layers * padded, LANES)
            for r in range(2):
                flat_state[pl.ds(row + r, layers, stride=padded), :] = received(
                    pl.ds((c * 2 + r) * slots, layers)
                )
            for tile in range(4):
                wide[c, pl.ds(row, 2), pl.ds(tile * LANES, LANES)] = received(
                    pl.ds(4 * slots + (c * 4 + tile) * 2, 2)
                )
    for c in range(2):
        wide[c, pl.ds(PAD, height), :] = strips[c]
    stepper = Stepper(counts, place, state, field, later, halo, depth, height)
    stepper.strips(wide)
    stepper.run(outer_tiles(height), True, out, block, sems)


def call(kernel, shapes, args, scratch=(), limit=16, far_out=0, far_in=(), aliases={}):
    vmem, far = pl.BlockSpec(memory_space=pltpu.VMEM), pl.BlockSpec(memory_space=pl.ANY)
    specs = [far if k in far_in else vmem for k in range(1, len(args))]
    return pl.pallas_call(
        kernel,
        out_shape=[jax.ShapeDtypeStruct(shape, jnp.float32) for shape in shapes],
        in_specs=[pl.BlockSpec(memory_space=pltpu.SMEM)] + specs,
        out_specs=[vmem] * (len(shapes) - far_out) + [far] * far_out,
        scratch_shapes=[
            pltpu.VMEM(shape, jnp.float32) if isinstance(shape, tuple) else shape
            for shape in scratch
        ],
        input_output_aliases=aliases,
        compiler_params=pltpu.CompilerParams(vmem_limit_bytes=limit * 2**20),
    )(*args)


def gathered_carries(rows, columns):
    height, width = rows.shape
    x, y = lax.axis_index("gx"), lax.axis_index("gy")
    row_totals = lax.all_gather(rows[:, -1], "gx")
    before = (jnp.arange(row_totals.shape[0]) < x)[:, None]
    row_carry = jnp.sum(jnp.where(before, row_totals, 0.0), axis=0)
    column_totals = lax.all_gather(columns[-1], "gy")
    before = (jnp.arange(column_totals.shape[0]) < y)[:, None]
    column_carry = jnp.sum(jnp.where(before, column_totals, 0.0), axis=0)
    return (
        jnp.broadcast_to(row_carry[:, None], (height, width)),
        jnp.broadcast_to(column_carry[None], (8, width)),
    )


def local(side, mag):
    counts = tuple(lax.axis_size(axis) for axis in ("gz", "gy", "gx"))
    count_z, count_y, count_x = counts
    _, depth, height, width = side.shape
    place = jnp.stack([lax.axis_index(axis) for axis in ("gz", "gy", "gx")]).astype(jnp.int32)
    plane, block = (height, width), (2, height, width)

    first, second, total, rows, columns = call(
        totals_kernel, [(2, 2) + plane, (2, 2) + plane, block, plane, plane], [place, side, mag]
    )
    first = swap_first(first, "gz")
    second = swap_second(second, "gz") if count_z > 2 else first
    others = [
        swap(total, "gz", functools.partial(lambda step, i: i ^ step, step))
        for step in far_steps(count_z)
    ]
    direct = count_y == 2 and count_x in (2, 4)
    if direct:
        column_carry = swap_first(columns[-8:], "gy")
    else:
        row_carry, column_carry = gathered_carries(rows, columns)
    packed, edges = call(
        lambda _, *refs: pack_kernel(*refs),
        [(2, height, 2 * LANES), (2, 4, depth, width)],
        [place, side],
        [(2, depth * height, width)],
    )
    far = len(others)
    packed, ext, base = call(
        functools.partial(z_kernel, count_z, depth, far),
        [(2, height, 2 * LANES), (2, 4) + plane, plane],
        [place, first, second, total, columns, column_carry, rows, packed, *others],
    )
    first = swap_first(packed, "gx")
    second = swap_second(packed, "gx") if count_x > 2 else first
    if not direct:
        far_rows = row_carry
    elif count_x == 4:
        far_rows = swap(rows, "gx", lambda i: i ^ 2)
    else:
        far_rows = rows
    messages = 1 if count_y == 2 else 2
    message_rows = 4 * slot_rows(depth) + 16
    strips, flat, ext, edge_rows = call(
        functools.partial(x_kernel, counts, depth),
        [(2, height, 4 * LANES), block, (2, 4) + plane, (messages, message_rows, width)],
        [place, packed, first, second, far_rows, rows, base, ext, edges],
    )
    first = swap_first(edge_rows[0], "gy")
    second = swap_second(edge_rows[1], "gy") if count_y > 2 else first
    grids = inner_steps(counts, place, side, flat, ext, strips)
    return outer_steps(counts, depth, place, strips, first, second, grids)


def inner_steps(counts, place, side, flat, ext, strips):
    _, depth, height, width = side.shape
    grid = (depth + 4, height + 2 * PAD, width)
    return call(
        functools.partial(inner_kernel, counts),
        [(2,) + grid, (3,) + grid, (3,) + grid, (3, depth, height, width)],
        [place, side, flat, ext, strips],
        [
            (4, 2, height + 2 * PAD, LANES),
            (2, height + 2 * PAD, 4 * LANES),
            (3, depth, height - 16, width),
            pltpu.SemaphoreType.DMA((6, 4)),
        ],
        far_out=1,
    )


def outer_steps(counts, depth, place, strips, first, second, grids):
    height, width = strips.shape[1], first.shape[1]
    result = call(
        functools.partial(outer_kernel, counts, depth),
        [grid.shape for grid in grids],
        [place, strips, first, second, *grids],
        [
            (4, 2, height + 2 * PAD, LANES),
            (2, height + 2 * PAD, 4 * LANES),
            (3, depth, 16, width),
            pltpu.SemaphoreType.DMA((6, 4)),
        ],
        far_out=1,
        far_in=(7,),
        aliases={4 + k: k for k in range(4)},
    )
    return result[3]


def solution(mesh):
    return jax.shard_map(
        local,
        mesh=mesh,
        in_specs=(P(None, "gz", "gy", "gx"), P("gy", "gx")),
        out_specs=P(None, "gz", "gy", "gx"),
        check_vma=False,
    )
```

```python
import functools

import jax
import jax.numpy as jnp
from jax import lax
from jax.experimental import pallas as pl
from jax.experimental.pallas import tpu as pltpu
from jax.sharding import PartitionSpec as P

spacing = 0.0625
friction = 0.004
gain = friction / (spacing * spacing)
LANES = 128
PAD = 8
GROUP = LANES // 4


def near(index, count):
    return (index + 1) % count if index % 2 else (index - 1) % count


def swap(part, axis, partner):
    count = lax.axis_size(axis)
    return lax.ppermute(part, axis, [(i, partner(i)) for i in range(count)])


def swap_first(part, axis):
    return swap(part, axis, lambda i: i ^ 1)


def swap_second(part, axis):
    count = lax.axis_size(axis)
    return swap(part, axis, lambda i: near(i, count))


def far_steps(count):
    return [2] if count == 4 else list(range(2, count))


def lane_index(shape):
    return lax.broadcasted_iota(jnp.int32, shape, len(shape) - 1)


def row_index(shape):
    return lax.broadcasted_iota(jnp.int32, shape, len(shape) - 2)


def columns_at(values, slot):
    first = 4 * (slot % GROUP)
    rolled = pltpu.roll(values, (first + 2) % LANES, 1)
    lane = lane_index(values.shape)
    return jnp.where((lane >= first) & (lane < first + 4), rolled, 0.0)


def spread(values, first):
    lane = lane_index(values.shape)
    moved = pltpu.roll(values, (LANES - first) % LANES, 1) if first else values
    alone = jnp.where(lane < 4, moved, 0.0)
    four = (alone + pltpu.roll(alone, 4, 1)) + (pltpu.roll(alone, 8, 1) + pltpu.roll(alone, 12, 1))
    parts = [four] + [pltpu.roll(four, step, 1) for step in range(16, LANES, 16)]
    while len(parts) > 1:
        parts = [a + b for a, b in zip(parts[::2], parts[1::2])]
    return parts[0]


def totals_kernel(
    place, side, mag, first_out, second_out, total_out, rows_out, columns_out, held, plane, sems
):
    depth = side.shape[1]
    z = place[0]
    size = depth // 4
    fetch_plane = pltpu.make_async_copy(mag, plane, sems.at[8])
    fetch_plane.start()
    fetches = []
    for piece in range(4):
        for c in range(2):
            layers = pl.ds(piece * size, size)
            fetches.append(
                pltpu.make_async_copy(
                    side.at[c, layers], held.at[c, layers], sems.at[piece * 2 + c]
                )
            )
            fetches[-1].start()
    fetch_plane.wait()
    rows = columns = plane[...]
    lane, row = lane_index(rows.shape), row_index(rows.shape)
    step = 1
    while step < LANES:
        rows = rows + jnp.where(lane >= step, pltpu.roll(rows, step, 1), 0.0)
        step *= 2
    rows_out[...] = rows
    step = 1
    while step < columns.shape[0]:
        columns = columns + jnp.where(row >= step, pltpu.roll(columns, step, 0), 0.0)
        step *= 2
    columns_out[...] = columns

    odd = z % 2 == 1
    upward = odd | (z == 0)
    low = [None, None]
    sums = [None, None]
    for piece in range(4):
        for c in range(2):
            fetches[piece * 2 + c].wait()
            total = sums[c]
            for layer in range(piece * size, (piece + 1) * size):
                if layer == depth - 1:
                    before = total
                total = held[c, layer] if layer == 0 else total + held[c, layer]
                if layer == 0:
                    low0 = total
                if layer == 1:
                    low[c] = (low0, total)
            sums[c] = total
            if piece == 3:
                low0, low1 = low[c]
                first_out[c, 0] = jnp.where(odd, low0, before)
                first_out[c, 1] = jnp.where(odd, low1, total)
                second_out[c, 0] = jnp.where(upward, before, low0)
                second_out[c, 1] = jnp.where(upward, total, low1)
                total_out[c] = total


def pack_kernel(side, packed_out, rows_out, running):
    depth, height = side.shape[1], side.shape[2]
    for c in range(2):
        total = jnp.zeros(side.shape[2:], jnp.float32)
        packed = [jnp.zeros(side.shape[2:], jnp.float32) for _ in range(2)]
        for layer in range(depth):
            total = total + side[c, layer]
            running[c, pl.ds(layer * height, height), :] = total
            slot = layer + 2
            packed[slot // GROUP] += columns_at(total, slot)
        for tile in range(2):
            packed_out[c, :, pl.ds(tile * LANES, LANES)] = packed[tile]
        for k, row in enumerate((0, 1, height - 2, height - 1)):
            rows_out[c, k] = running[c, pl.ds(row, depth, stride=height), :]


def z_kernel(
    count, depth, far, place, first, second, total, columns, column_carry, rows, packed, *rest
):
    others, (x_out, ext_out, flat_out) = rest[:far], rest[far:]
    z, y = place[0], place[1]
    odd = z % 2 == 1
    for c in range(2):
        near_a, near_b = (first[c, 0], first[c, 1]), (second[c, 0], second[c, 1])
        low = [jnp.where(odd, a, b) for a, b in zip(near_a, near_b)]
        high = [jnp.where(odd, b, a) for a, b in zip(near_a, near_b)]
        carry = jnp.where(odd, near_a[1], 0.0)
        if count == 4:
            carry = carry + jnp.where((z == 2) | (z == 3), near_b[1], 0.0)
        for step, other in zip(far_steps(count), others):
            carry = carry + jnp.where((z ^ step) < z, other[c], 0.0)
        if c == 0:
            shared = 0.5 * rows[...] - carry
        else:
            before = jnp.where(y > 0, column_carry[7:8, :], 0.0)
            shared = carry - 0.5 * (columns[...] + before)
        layers = (low[0] - low[1], None, total[c] + high[0], total[c] + high[1])
        flat_out[c] = shared
        for k in (0, 2, 3):
            ext_out[c, k] = layers[k]
        ext_out[c, 1] = jnp.zeros_like(carry)
        for tile in range(2):
            values = packed[c, :, pl.ds(tile * LANES, LANES)]
            slots = [(0, layers[0]), (depth + 2, layers[2]), (depth + 3, layers[3])]
            for at, layer in slots + [(depth + 4, shared), (depth + 5, rows[...])]:
                if at // GROUP == tile:
                    values = values + columns_at(layer, at)
            x_out[c, :, pl.ds(tile * LANES, LANES)] = values


def x_kernel(
    counts, depth, place, packed, first, second, far_rows, rows, shared, beside, edges,
    strips_out, flat_out, ext_out, y_out,
):
    count_z, count_y, count_x = counts
    height = packed.shape[1]
    z, y, x = place[0], place[1], place[2]
    odd = x % 2 == 1
    base_tile, base_lane = (depth + 4) // GROUP, 4 * ((depth + 4) % GROUP)
    rows_tile, rows_lane = (depth + 5) // GROUP, 4 * ((depth + 5) % GROUP)

    def tile_of(ref, c, tile):
        return ref[c, :, pl.ds(tile * LANES, LANES)]

    def row_totals(ref):
        return tile_of(ref, 0, rows_tile)[:, rows_lane + 1 : rows_lane + 2]

    own_total = rows[...][:, LANES - 1 :]
    total_a, total_b = row_totals(first), row_totals(second)
    far_total = far_rows[...][:, LANES - 1 :]
    if count_x == 2:
        row_carry = jnp.where(odd, total_a, 0.0)
    elif count_x == 4:
        row_carry = jnp.where(odd, total_a, 0.0) + jnp.where(x >= 2, total_b + far_total, 0.0)
    else:
        row_carry = far_total
    left_total = jnp.where(odd, total_a, total_b)

    lane = lane_index((height, LANES))
    q = lane % 4
    for part in range(2):
        merged = []
        for c in range(2):
            tiles = []
            for tile in range(2):
                own, a, b = (tile_of(ref, c, tile) for ref in (packed, first, second))
                if part == 0:
                    tiles.append(jnp.where(q < 2, jnp.where(odd, a, b), own))
                else:
                    tiles.append(jnp.where(q < 2, own, jnp.where(odd, b, a)))
            merged.append(tiles)
        if part == 0:
            carry = jnp.where(q < 2, row_carry - left_total, row_carry)
        else:
            carry = jnp.where(q < 2, row_carry, row_carry + own_total)
        base_y = spread(merged[0][base_tile], base_lane) + 0.5 * carry
        base_x = spread(merged[1][base_tile], base_lane)
        for tile in range(2):
            slot = lane // 4 + tile * GROUP
            inside = (slot < depth + 4) & ((slot >= 2) | (z > 0))
            inside = inside & ((slot < depth + 2) | (z < count_z - 1))
            if part == 0:
                inside = inside & ((q >= 2) | (x > 0))
            else:
                inside = inside & ((q < 2) | (x < count_x - 1))
            place_at = pl.ds((part * 2 + tile) * LANES, LANES)
            strips_out[0, :, place_at] = jnp.where(inside, base_x + merged[1][tile], 0.0)
            strips_out[1, :, place_at] = jnp.where(inside, base_y - merged[0][tile], 0.0)

    flat_x = shared[1]
    flat_y = shared[0] + 0.5 * row_carry
    flat_out[0] = flat_x
    flat_out[1] = flat_y
    for k in range(4):
        inside = (z > 0) if k < 2 else (z < count_z - 1)
        ext_out[0, k] = jnp.where(inside, flat_x + beside[1, k], 0.0)
        ext_out[1, k] = jnp.where(inside, flat_y - beside[0, k], 0.0)

    slots = slot_rows(depth)
    for message in range(y_out.shape[0]):
        downward = (y % 2 == 1) if message == 0 else (y % 2 == 0)
        for c in range(2):
            for r in range(2):
                start = (c * 2 + r) * slots
                low, high = pl.ds(r, 1), pl.ds(height - 2 + r, 1)
                flat = jnp.where(downward, flat_out[c, low, :], flat_out[c, high, :])
                edge = jnp.where(downward, edges[1 - c, r], edges[1 - c, 2 + r])
                edge = edge if c == 0 else -edge
                y_out[message, pl.ds(start + 2, depth), :] = flat + edge
                for k, at in enumerate((0, 1, depth + 2, depth + 3)):
                    y_out[message, pl.ds(start + at, 1), :] = jnp.where(
                        downward, ext_out[c, k, low, :], ext_out[c, k, high, :]
                    )
            for tile in range(4):
                start = 4 * slots + (c * 4 + tile) * 2
                lanes = pl.ds(tile * LANES, LANES)
                y_out[message, pl.ds(start, 2), :] = jnp.where(
                    downward,
                    strips_out[c, pl.ds(0, 2), lanes],
                    strips_out[c, pl.ds(height - 2, 2), lanes],
                )


def slot_rows(depth):
    return (depth + 4 + 7) // 8 * 8


def following(values, axis, step=1):
    return pltpu.roll(values, values.shape[axis] - step, axis)


def preceding(values, axis, step=1):
    return pltpu.roll(values, step, axis)


def push(a, field, current):
    square = field[0] * field[0] + field[1] * field[1] + field[2] * field[2]
    along = current[0] * field[0] + current[1] * field[1] + current[2] * field[2]
    factor = gain / (square + 1.0)
    p, q = along * factor, square * factor
    return [a[c] + (field[c] * p - current[c] * q) for c in range(3)]


def strip_field(a):
    x, y, z = a
    field_x = following(z, 0) - z - (following(y, 1, 4) - y)
    field_y = following(x, 1, 4) - x - (following(z, 1) - z)
    field_z = following(y, 1) - y - (following(x, 0) - x)
    return field_x, field_y, field_z


def strip_current(b):
    x, y, z = b
    current_x = z - preceding(z, 0) - (y - preceding(y, 1, 4))
    current_y = x - preceding(x, 1, 4) - (z - preceding(z, 1))
    current_z = y - preceding(y, 1) - (x - preceding(x, 0))
    return current_x, current_y, current_z


class Stepper:
    def __init__(self, counts, place, state, field, later, halo, depth, height):
        self.counts = counts
        self.z, self.y, self.x = place[0], place[1], place[2]
        self.state, self.field, self.later, self.halo = state, field, later, halo
        self.depth, self.height = depth, height
        self.padded = state.shape[2]
        lane = lane_index((8, LANES))
        self.last, self.start = lane == LANES - 1, lane == 0

    def load(self, ref, c, layer, row):
        return ref[c, layer, pl.ds(row, 8), :]

    def strips(self, wide):
        depth, height = self.depth, self.height
        count_z, count_y, count_x = self.counts
        half = 2 * LANES
        shape = (self.padded, 2 * half)
        lane, row = lane_index(shape), row_index(shape)
        q = lane % 4
        slot = (lane % half) // 4
        right = lane >= half
        inside = (row >= PAD - 2) & (row < PAD + height + 2) & (slot < depth + 4)
        inside = inside & ((row >= PAD) | (self.y > 0))
        inside = inside & ((row < PAD + height) | (self.y < count_y - 1))
        inside = inside & ((slot >= 2) | (self.z > 0))
        inside = inside & ((slot < depth + 2) | (self.z < count_z - 1))
        inside = inside & (right | (q >= 2) | (self.x > 0))
        inside = inside & (~right | (q < 2) | (self.x < count_x - 1))
        a = [jnp.where(inside, wide[c], 0.0) for c in range(2)]
        a.append(jnp.zeros_like(a[0]))
        b = strip_field(a)
        pick = (lane_index((self.padded, half)) % 4) == 2

        def keep(at, upper, lower):
            value = jnp.where(pick, upper[:, half:], lower[:, :half])
            self.halo[at, 0] = value[:, :LANES]
            self.halo[at, 1] = value[:, LANES:]

        keep(0, a[1], b[1])
        keep(1, a[2], b[2])
        a = [jnp.where(inside, value, 0.0) for value in push(a, b, strip_current(b))]
        b = strip_field(a)
        keep(2, a[1], b[1])
        keep(3, a[2], b[2])

    def beside(self, at, layer, row):
        shift = LANES - 2 - 4 * (layer % GROUP)
        return pltpu.roll(self.halo[at, layer // GROUP, pl.ds(row, 8), :], shift, 1)

    def right_of(self, value, edge):
        return following(jnp.where(self.start, edge, value), 1)

    def left_of(self, value, edge):
        return preceding(jnp.where(self.last, edge, value), 1)

    def first_field(self, layer, r):
        load, state = self.load, self.state
        ax, ay = load(state, 0, layer, r), load(state, 1, layer, r)
        ay_right = self.right_of(ay, self.beside(0, layer, r))
        to = pl.ds(r, 8)
        self.field[0, layer, to, :] = ay - load(state, 1, layer + 1, r)
        self.field[1, layer, to, :] = load(state, 0, layer + 1, r) - ax
        self.field[2, layer, to, :] = ay_right - ay - (load(state, 0, layer, r + 1) - ax)

    def currents(self, layer, r, at):
        load, field = self.load, self.field
        bx, by, bz = (load(field, c, layer, r) for c in range(3))
        by_left = self.left_of(by, self.beside(at, layer, r))
        bz_left = self.left_of(bz, self.beside(at + 1, layer, r))
        jx = bz - load(field, 2, layer, r - 1) - (by - load(field, 1, layer - 1, r))
        jy = bx - load(field, 0, layer - 1, r) - (bz - bz_left)
        jz = by - by_left - (bx - load(field, 0, layer, r - 1))
        return (bx, by, bz), (jx, jy, jz)

    def first_push(self, layer, r):
        b, j = self.currents(layer, r, 0)
        a = [self.load(self.state, c, layer, r) for c in range(2)]
        a.append(jnp.zeros_like(a[0]))
        for c, value in enumerate(push(a, b, j)):
            self.later[c, layer, pl.ds(r, 8), :] = value

    def second_field(self, layer, r):
        load, later = self.load, self.later
        ax, ay, az = (load(later, c, layer, r) for c in range(3))
        ay_right = self.right_of(ay, self.beside(2, layer, r))
        az_right = self.right_of(az, self.beside(3, layer, r))
        to = pl.ds(r, 8)
        self.field[0, layer, to, :] = (
            load(later, 2, layer, r + 1) - az - (load(later, 1, layer + 1, r) - ay)
        )
        self.field[1, layer, to, :] = load(later, 0, layer + 1, r) - ax - (az_right - az)
        self.field[2, layer, to, :] = ay_right - ay - (load(later, 0, layer, r + 1) - ax)

    def second_push(self, layer, r):
        b, j = self.currents(layer, r, 2)
        a = [self.load(self.later, c, layer, r) for c in range(3)]
        return [spacing * value for value in push(a, b, j)]

    def clear(self, rows):
        depth, height = self.depth, self.height
        count_z, count_y, _ = self.counts
        zeros = jnp.zeros((height + 8, LANES), jnp.float32)
        line = jnp.zeros((depth + 4, LANES), jnp.float32)
        for exists, layer in ((self.z > 0, 1), (self.z < count_z - 1, depth + 2)):

            @pl.when(jnp.logical_not(exists))
            def _():
                for c in range(3):
                    self.later[c, layer, pl.ds(PAD - 1, height + 8), :] = zeros

        if not rows:
            return
        for exists, row in ((self.y > 0, PAD - 1), (self.y < count_y - 1, PAD + height)):

            @pl.when(jnp.logical_not(exists))
            def _():
                for c in range(3):
                    flat_later = self.later.at[c].reshape((depth + 4) * self.padded, LANES)
                    flat_later[pl.ds(row, depth + 4, stride=self.padded), :] = line

    def run(self, tiles, rows, out, block, sems, pieces=6):
        depth = self.depth
        for layer in range(depth + 3):
            for r in tiles[0]:
                self.first_field(layer, r)
        for layer in range(1, depth + 3):
            for r in tiles[1]:
                self.first_push(layer, r)
        self.clear(rows)
        for layer in range(1, depth + 2):
            for r in tiles[2]:
                self.second_field(layer, r)
        copies = []
        size = depth // pieces
        for piece in range(pieces):
            layers = pl.ds(piece * size, size)
            for layer in range(piece * size, (piece + 1) * size):
                for k, r in enumerate(tiles[3]):
                    for c, value in enumerate(self.second_push(layer + 2, r)):
                        block[c, layer, pl.ds(8 * k, 8), :] = value
            k = 0
            while k < len(tiles[3]):
                run = 1
                while k + run < len(tiles[3]) and tiles[3][k + run] == tiles[3][k] + 8 * run:
                    run += 1
                copies.append(
                    pltpu.make_async_copy(
                        block.at[:, layers, pl.ds(8 * k, 8 * run), :],
                        out.at[:, layers, pl.ds(tiles[3][k] - PAD, 8 * run), :],
                        sems.at[piece, k],
                    )
                )
                copies[-1].start()
                k += run
        for copy in copies:
            copy.wait()


def inner_tiles(height):
    whole = [PAD + r for r in range(0, height, 8)]
    inner = whole[1:-1]
    return whole, whole, [r - 1 for r in inner] + [inner[-1]], inner


def outer_tiles(height):
    top = PAD + height - 8
    return (PAD - 2, top + 1), (PAD - 1, top + 1), (PAD - 1, top), (PAD, top)


def inner_kernel(
    counts, place, side, flat, ext, strips, state, field, later, out, halo, wide, block, sems
):
    depth, height = side.shape[1], side.shape[2]
    rows = pl.ds(PAD, height)
    for c in range(2):
        for k, at in enumerate((0, 1, depth + 2, depth + 3)):
            state[c, at, rows, :] = ext[c, k]
    sums = [jnp.zeros((height, LANES), jnp.float32) for _ in range(2)]
    for layer in range(depth):
        sums = [total + side[c, layer] for c, total in enumerate(sums)]
        state[0, layer + 2, rows, :] = flat[0] + sums[1]
        state[1, layer + 2, rows, :] = flat[1] - sums[0]
    for c in range(2):
        wide[c, rows, :] = strips[c]
        wide[c, pl.ds(0, PAD), :] = jnp.zeros((PAD, wide.shape[2]), jnp.float32)
        wide[c, pl.ds(PAD + height, PAD), :] = jnp.zeros((PAD, wide.shape[2]), jnp.float32)
    stepper = Stepper(counts, place, state, field, later, halo, depth, height)
    stepper.strips(wide)
    stepper.run(inner_tiles(height), False, out, block, sems)


def outer_kernel(
    counts, depth, place, strips, first, second, _s, _f, _l, _o,
    state, field, later, out, halo, wide, block, sems,
):
    _, count_y, _ = counts
    height, padded = strips.shape[1], state.shape[2]
    y = place[1]
    slots = slot_rows(depth)
    layers = depth + 4
    odd = y % 2 == 1
    for low in (True, False):
        exists = (y > 0) if low else (y < count_y - 1)
        row = PAD - 2 if low else PAD + height

        def received(take):
            a, b = first[take, :], second[take, :]
            value = jnp.where(odd, a, b) if low else jnp.where(odd, b, a)
            return jnp.where(exists, value, 0.0)

        for c in range(2):
            flat_state = state.at[c].reshape(layers * padded, LANES)
            for r in range(2):
                flat_state[pl.ds(row + r, layers, stride=padded), :] = received(
                    pl.ds((c * 2 + r) * slots, layers)
                )
            for tile in range(4):
                wide[c, pl.ds(row, 2), pl.ds(tile * LANES, LANES)] = received(
                    pl.ds(4 * slots + (c * 4 + tile) * 2, 2)
                )
    for c in range(2):
        wide[c, pl.ds(PAD, height), :] = strips[c]
    stepper = Stepper(counts, place, state, field, later, halo, depth, height)
    stepper.strips(wide)
    stepper.run(outer_tiles(height), True, out, block, sems)


def call(kernel, shapes, args, scratch=(), limit=16, far_out=0, far_in=(), aliases={}):
    vmem, far = pl.BlockSpec(memory_space=pltpu.VMEM), pl.BlockSpec(memory_space=pltpu.HBM)
    specs = [far if k in far_in else vmem for k in range(1, len(args))]
    return pl.pallas_call(
        kernel,
        out_shape=[jax.ShapeDtypeStruct(shape, jnp.float32) for shape in shapes],
        in_specs=[pl.BlockSpec(memory_space=pltpu.SMEM)] + specs,
        out_specs=[vmem] * (len(shapes) - far_out) + [far] * far_out,
        scratch_shapes=[
            pltpu.VMEM(shape, jnp.float32) if isinstance(shape, tuple) else shape
            for shape in scratch
        ],
        input_output_aliases=aliases,
        compiler_params=pltpu.CompilerParams(vmem_limit_bytes=limit * 2**20),
    )(*args)


def gathered_carries(rows, columns):
    height, width = rows.shape
    x, y = lax.axis_index("gx"), lax.axis_index("gy")
    row_totals = lax.all_gather(rows[:, -1], "gx")
    before = (jnp.arange(row_totals.shape[0]) < x)[:, None]
    row_carry = jnp.sum(jnp.where(before, row_totals, 0.0), axis=0)
    column_totals = lax.all_gather(columns[-1], "gy")
    before = (jnp.arange(column_totals.shape[0]) < y)[:, None]
    column_carry = jnp.sum(jnp.where(before, column_totals, 0.0), axis=0)
    return (
        jnp.broadcast_to(row_carry[:, None], (height, width)),
        jnp.broadcast_to(column_carry[None], (8, width)),
    )


def local(side, mag):
    counts = tuple(lax.axis_size(axis) for axis in ("gz", "gy", "gx"))
    count_z, count_y, count_x = counts
    _, depth, height, width = side.shape
    place = jnp.stack([lax.axis_index(axis) for axis in ("gz", "gy", "gx")]).astype(jnp.int32)
    plane, block = (height, width), (2, height, width)

    first, second, total, rows, columns, side = call(
        totals_kernel,
        [(2, 2) + plane, (2, 2) + plane, block, plane, plane, side.shape],
        [place, side, mag],
        [plane, pltpu.SemaphoreType.DMA((9,))],
        far_in=(1, 2),
    )
    first = swap_first(first, "gz")
    second = swap_second(second, "gz") if count_z > 2 else first
    others = [
        swap(total, "gz", functools.partial(lambda step, i: i ^ step, step))
        for step in far_steps(count_z)
    ]
    direct = count_y == 2 and count_x in (2, 4)
    if direct:
        column_carry = swap_first(columns[-8:], "gy")
    else:
        row_carry, column_carry = gathered_carries(rows, columns)
    packed, edges = call(
        lambda _, *refs: pack_kernel(*refs),
        [(2, height, 2 * LANES), (2, 4, depth, width)],
        [place, side],
        [(2, depth * height, width)],
    )
    far = len(others)
    packed, beside, shared = call(
        functools.partial(z_kernel, count_z, depth, far),
        [(2, height, 2 * LANES), (2, 4) + plane, block],
        [place, first, second, total, columns, column_carry, rows, packed, *others],
    )
    first = swap_first(packed, "gx")
    second = swap_second(packed, "gx") if count_x > 2 else first
    if not direct:
        far_rows = row_carry
    elif count_x == 4:
        far_rows = swap(rows, "gx", lambda i: i ^ 2)
    else:
        far_rows = rows
    messages = 1 if count_y == 2 else 2
    message_rows = 4 * slot_rows(depth) + 16
    strips, flat, ext, edge_rows = call(
        functools.partial(x_kernel, counts, depth),
        [(2, height, 4 * LANES), block, (2, 4) + plane, (messages, message_rows, width)],
        [place, packed, first, second, far_rows, rows, shared, beside, edges],
    )
    first = swap_first(edge_rows[0], "gy")
    second = swap_second(edge_rows[1], "gy") if count_y > 2 else first
    grids = inner_steps(counts, place, side, flat, ext, strips)
    return outer_steps(counts, depth, place, strips, first, second, grids)


def inner_steps(counts, place, side, flat, ext, strips):
    _, depth, height, width = side.shape
    grid = (depth + 4, height + 2 * PAD, width)
    return call(
        functools.partial(inner_kernel, counts),
        [(2,) + grid, (3,) + grid, (3,) + grid, (3, depth, height, width)],
        [place, side, flat, ext, strips],
        [
            (4, 2, height + 2 * PAD, LANES),
            (2, height + 2 * PAD, 4 * LANES),
            (3, depth, height - 16, width),
            pltpu.SemaphoreType.DMA((6, 4)),
        ],
        far_out=1,
    )


def outer_steps(counts, depth, place, strips, first, second, grids):
    height, width = strips.shape[1], first.shape[1]
    result = call(
        functools.partial(outer_kernel, counts, depth),
        [grid.shape for grid in grids],
        [place, strips, first, second, *grids],
        [
            (4, 2, height + 2 * PAD, LANES),
            (2, height + 2 * PAD, 4 * LANES),
            (3, depth, 16, width),
            pltpu.SemaphoreType.DMA((6, 4)),
        ],
        far_out=1,
        far_in=(7,),
        aliases={4 + k: k for k in range(4)},
    )
    return result[3]


def solution(mesh):
    return jax.shard_map(
        local,
        mesh=mesh,
        in_specs=(P(None, "gz", "gy", "gx"), P("gy", "gx")),
        out_specs=P(None, "gz", "gy", "gx"),
        check_vma=False,
    )
```

```python
import functools

import jax
import jax.numpy as jnp
from jax import lax
from jax.experimental import pallas as pl
from jax.experimental.pallas import tpu as pltpu
from jax.sharding import PartitionSpec as P

spacing = 0.0625
friction = 0.004
gain = friction / (spacing * spacing)
LANES = 128
PAD = 8
GROUP = LANES // 4
LONG = pl.CostEstimate(flops=10**10, bytes_accessed=10**5, transcendentals=0)


def near(index, count):
    return (index + 1) % count if index % 2 else (index - 1) % count


def swap(part, axis, partner):
    count = lax.axis_size(axis)
    return lax.ppermute(part, axis, [(i, partner(i)) for i in range(count)])


def swap_first(part, axis):
    return swap(part, axis, lambda i: i ^ 1)


def swap_second(part, axis):
    count = lax.axis_size(axis)
    return swap(part, axis, lambda i: near(i, count))


def far_steps(count):
    return [2] if count == 4 else list(range(2, count))


def lane_index(shape):
    return lax.broadcasted_iota(jnp.int32, shape, len(shape) - 1)


def row_index(shape):
    return lax.broadcasted_iota(jnp.int32, shape, len(shape) - 2)


def columns_at(values, slot):
    first = 4 * (slot % GROUP)
    rolled = pltpu.roll(values, (first + 2) % LANES, 1)
    lane = lane_index(values.shape)
    return jnp.where((lane >= first) & (lane < first + 4), rolled, 0.0)


def spread(values, first):
    lane = lane_index(values.shape)
    moved = pltpu.roll(values, (LANES - first) % LANES, 1) if first else values
    alone = jnp.where(lane < 4, moved, 0.0)
    four = (alone + pltpu.roll(alone, 4, 1)) + (pltpu.roll(alone, 8, 1) + pltpu.roll(alone, 12, 1))
    parts = [four] + [pltpu.roll(four, step, 1) for step in range(16, LANES, 16)]
    while len(parts) > 1:
        parts = [a + b for a, b in zip(parts[::2], parts[1::2])]
    return parts[0]


def place_kernel(place, place_out):
    for k in range(place.shape[0]):
        place_out[k] = place[k]


def plane_kernel(_, mag, rows_out, columns_out):
    rows = columns = mag[...]
    lane, row = lane_index(rows.shape), row_index(rows.shape)
    step = 1
    while step < LANES:
        rows = rows + jnp.where(lane >= step, pltpu.roll(rows, step, 1), 0.0)
        step *= 2
    rows_out[...] = rows
    step = 1
    while step < columns.shape[0]:
        columns = columns + jnp.where(row >= step, pltpu.roll(columns, step, 0), 0.0)
        step *= 2
    columns_out[...] = columns


def totals_kernel(place, side, columns, first_out, second_out, total_out, last_out):
    depth = side.shape[1]
    odd = place[0] % 2 == 1
    upward = odd | (place[0] == 0)
    for c in range(2):
        low0 = side[c, 0]
        low1 = low0 + side[c, 1]
        before = low1
        for layer in range(2, depth - 1):
            before = before + side[c, layer]
        total = before + side[c, depth - 1]
        first_out[c, 0] = jnp.where(odd, low0, before)
        first_out[c, 1] = jnp.where(odd, low1, total)
        second_out[c, 0] = jnp.where(upward, before, low0)
        second_out[c, 1] = jnp.where(upward, total, low1)
        total_out[c] = total
    last_out[...] = columns[pl.ds(columns.shape[0] - 8, 8), :]


def pack_kernel(side, packed_out, rows_out, running):
    depth, height = side.shape[1], side.shape[2]
    for c in range(2):
        total = jnp.zeros(side.shape[2:], jnp.float32)
        packed = [jnp.zeros(side.shape[2:], jnp.float32) for _ in range(2)]
        for layer in range(depth):
            total = total + side[c, layer]
            running[c, pl.ds(layer * height, height), :] = total
            slot = layer + 2
            packed[slot // GROUP] += columns_at(total, slot)
        for tile in range(2):
            packed_out[c, :, pl.ds(tile * LANES, LANES)] = packed[tile]
        for k, row in enumerate((0, 1, height - 2, height - 1)):
            rows_out[c, k] = running[c, pl.ds(row, depth, stride=height), :]


def z_kernel(
    count, depth, far, place, first, second, total, columns, column_carry, rows, packed, *rest
):
    others, (x_out, ext_out, flat_out) = rest[:far], rest[far:]
    z, y = place[0], place[1]
    odd = z % 2 == 1
    for c in range(2):
        near_a, near_b = (first[c, 0], first[c, 1]), (second[c, 0], second[c, 1])
        low = [jnp.where(odd, a, b) for a, b in zip(near_a, near_b)]
        high = [jnp.where(odd, b, a) for a, b in zip(near_a, near_b)]
        carry = jnp.where(odd, near_a[1], 0.0)
        if count == 4:
            carry = carry + jnp.where((z == 2) | (z == 3), near_b[1], 0.0)
        for step, other in zip(far_steps(count), others):
            carry = carry + jnp.where((z ^ step) < z, other[c], 0.0)
        if c == 0:
            shared = 0.5 * rows[...] - carry
        else:
            before = jnp.where(y > 0, column_carry[7:8, :], 0.0)
            shared = carry - 0.5 * (columns[...] + before)
        layers = (low[0] - low[1], None, total[c] + high[0], total[c] + high[1])
        flat_out[c] = shared
        for k in (0, 2, 3):
            ext_out[c, k] = layers[k]
        ext_out[c, 1] = jnp.zeros_like(carry)
        for tile in range(2):
            values = packed[c, :, pl.ds(tile * LANES, LANES)]
            slots = [(0, layers[0]), (depth + 2, layers[2]), (depth + 3, layers[3])]
            for at, layer in slots + [(depth + 4, shared), (depth + 5, rows[...])]:
                if at // GROUP == tile:
                    values = values + columns_at(layer, at)
            x_out[c, :, pl.ds(tile * LANES, LANES)] = values


def x_kernel(
    counts, depth, place, packed, first, second, far_rows, rows, shared, beside, edges,
    strips_out, flat_out, ext_out, y_out,
):
    count_z, count_y, count_x = counts
    height = packed.shape[1]
    z, y, x = place[0], place[1], place[2]
    odd = x % 2 == 1
    base_tile, base_lane = (depth + 4) // GROUP, 4 * ((depth + 4) % GROUP)
    rows_tile, rows_lane = (depth + 5) // GROUP, 4 * ((depth + 5) % GROUP)

    def tile_of(ref, c, tile):
        return ref[c, :, pl.ds(tile * LANES, LANES)]

    def row_totals(ref):
        return tile_of(ref, 0, rows_tile)[:, rows_lane + 1 : rows_lane + 2]

    own_total = rows[...][:, LANES - 1 :]
    total_a, total_b = row_totals(first), row_totals(second)
    far_total = far_rows[...][:, LANES - 1 :]
    if count_x == 2:
        row_carry = jnp.where(odd, total_a, 0.0)
    elif count_x == 4:
        row_carry = jnp.where(odd, total_a, 0.0) + jnp.where(x >= 2, total_b + far_total, 0.0)
    else:
        row_carry = far_total
    left_total = jnp.where(odd, total_a, total_b)

    lane = lane_index((height, LANES))
    q = lane % 4
    for part in range(2):
        merged = []
        for c in range(2):
            tiles = []
            for tile in range(2):
                own, a, b = (tile_of(ref, c, tile) for ref in (packed, first, second))
                if part == 0:
                    tiles.append(jnp.where(q < 2, jnp.where(odd, a, b), own))
                else:
                    tiles.append(jnp.where(q < 2, own, jnp.where(odd, b, a)))
            merged.append(tiles)
        if part == 0:
            carry = jnp.where(q < 2, row_carry - left_total, row_carry)
        else:
            carry = jnp.where(q < 2, row_carry, row_carry + own_total)
        base_y = spread(merged[0][base_tile], base_lane) + 0.5 * carry
        base_x = spread(merged[1][base_tile], base_lane)
        for tile in range(2):
            slot = lane // 4 + tile * GROUP
            inside = (slot < depth + 4) & ((slot >= 2) | (z > 0))
            inside = inside & ((slot < depth + 2) | (z < count_z - 1))
            if part == 0:
                inside = inside & ((q >= 2) | (x > 0))
            else:
                inside = inside & ((q < 2) | (x < count_x - 1))
            place_at = pl.ds((part * 2 + tile) * LANES, LANES)
            strips_out[0, :, place_at] = jnp.where(inside, base_x + merged[1][tile], 0.0)
            strips_out[1, :, place_at] = jnp.where(inside, base_y - merged[0][tile], 0.0)

    flat_x = shared[1]
    flat_y = shared[0] + 0.5 * row_carry
    flat_out[0] = flat_x
    flat_out[1] = flat_y
    for k in range(4):
        inside = (z > 0) if k < 2 else (z < count_z - 1)
        ext_out[0, k] = jnp.where(inside, flat_x + beside[1, k], 0.0)
        ext_out[1, k] = jnp.where(inside, flat_y - beside[0, k], 0.0)

    slots = slot_rows(depth)
    for message in range(y_out.shape[0]):
        downward = (y % 2 == 1) if message == 0 else (y % 2 == 0)
        for c in range(2):
            for r in range(2):
                start = (c * 2 + r) * slots
                low, high = pl.ds(r, 1), pl.ds(height - 2 + r, 1)
                flat = jnp.where(downward, flat_out[c, low, :], flat_out[c, high, :])
                edge = jnp.where(downward, edges[1 - c, r], edges[1 - c, 2 + r])
                edge = edge if c == 0 else -edge
                y_out[message, pl.ds(start + 2, depth), :] = flat + edge
                for k, at in enumerate((0, 1, depth + 2, depth + 3)):
                    y_out[message, pl.ds(start + at, 1), :] = jnp.where(
                        downward, ext_out[c, k, low, :], ext_out[c, k, high, :]
                    )
            for tile in range(4):
                start = 4 * slots + (c * 4 + tile) * 2
                lanes = pl.ds(tile * LANES, LANES)
                y_out[message, pl.ds(start, 2), :] = jnp.where(
                    downward,
                    strips_out[c, pl.ds(0, 2), lanes],
                    strips_out[c, pl.ds(height - 2, 2), lanes],
                )


def slot_rows(depth):
    return (depth + 4 + 7) // 8 * 8


def following(values, axis, step=1):
    return pltpu.roll(values, values.shape[axis] - step, axis)


def preceding(values, axis, step=1):
    return pltpu.roll(values, step, axis)


def push(a, field, current):
    square = field[0] * field[0] + field[1] * field[1] + field[2] * field[2]
    along = current[0] * field[0] + current[1] * field[1] + current[2] * field[2]
    factor = gain / (square + 1.0)
    p, q = along * factor, square * factor
    return [a[c] + (field[c] * p - current[c] * q) for c in range(3)]


def strip_field(a):
    x, y, z = a
    field_x = following(z, 0) - z - (following(y, 1, 4) - y)
    field_y = following(x, 1, 4) - x - (following(z, 1) - z)
    field_z = following(y, 1) - y - (following(x, 0) - x)
    return field_x, field_y, field_z


def strip_current(b):
    x, y, z = b
    current_x = z - preceding(z, 0) - (y - preceding(y, 1, 4))
    current_y = x - preceding(x, 1, 4) - (z - preceding(z, 1))
    current_z = y - preceding(y, 1) - (x - preceding(x, 0))
    return current_x, current_y, current_z


class Stepper:
    def __init__(self, counts, place, state, field, later, halo, depth, height):
        self.counts = counts
        self.z, self.y, self.x = place[0], place[1], place[2]
        self.state, self.field, self.later, self.halo = state, field, later, halo
        self.depth, self.height = depth, height
        self.padded = state.shape[2]
        lane = lane_index((8, LANES))
        self.last, self.start = lane == LANES - 1, lane == 0

    def load(self, ref, c, layer, row):
        return ref[c, layer, pl.ds(row, 8), :]

    def strips(self, wide):
        depth, height = self.depth, self.height
        count_z, count_y, count_x = self.counts
        half = 2 * LANES
        shape = (self.padded, 2 * half)
        lane, row = lane_index(shape), row_index(shape)
        q = lane % 4
        slot = (lane % half) // 4
        right = lane >= half
        inside = (row >= PAD - 2) & (row < PAD + height + 2) & (slot < depth + 4)
        inside = inside & ((row >= PAD) | (self.y > 0))
        inside = inside & ((row < PAD + height) | (self.y < count_y - 1))
        inside = inside & ((slot >= 2) | (self.z > 0))
        inside = inside & ((slot < depth + 2) | (self.z < count_z - 1))
        inside = inside & (right | (q >= 2) | (self.x > 0))
        inside = inside & (~right | (q < 2) | (self.x < count_x - 1))
        a = [jnp.where(inside, wide[c], 0.0) for c in range(2)]
        a.append(jnp.zeros_like(a[0]))
        b = strip_field(a)
        pick = (lane_index((self.padded, half)) % 4) == 2

        def keep(at, upper, lower):
            value = jnp.where(pick, upper[:, half:], lower[:, :half])
            self.halo[at, 0] = value[:, :LANES]
            self.halo[at, 1] = value[:, LANES:]

        keep(0, a[1], b[1])
        keep(1, a[2], b[2])
        a = [jnp.where(inside, value, 0.0) for value in push(a, b, strip_current(b))]
        b = strip_field(a)
        keep(2, a[1], b[1])
        keep(3, a[2], b[2])

    def beside(self, at, layer, row):
        shift = LANES - 2 - 4 * (layer % GROUP)
        return pltpu.roll(self.halo[at, layer // GROUP, pl.ds(row, 8), :], shift, 1)

    def right_of(self, value, edge):
        return following(jnp.where(self.start, edge, value), 1)

    def left_of(self, value, edge):
        return preceding(jnp.where(self.last, edge, value), 1)

    def first_field(self, layer, r):
        load, state = self.load, self.state
        ax, ay = load(state, 0, layer, r), load(state, 1, layer, r)
        ay_right = self.right_of(ay, self.beside(0, layer, r))
        to = pl.ds(r, 8)
        self.field[0, layer, to, :] = ay - load(state, 1, layer + 1, r)
        self.field[1, layer, to, :] = load(state, 0, layer + 1, r) - ax
        self.field[2, layer, to, :] = ay_right - ay - (load(state, 0, layer, r + 1) - ax)

    def currents(self, layer, r, at):
        load, field = self.load, self.field
        bx, by, bz = (load(field, c, layer, r) for c in range(3))
        by_left = self.left_of(by, self.beside(at, layer, r))
        bz_left = self.left_of(bz, self.beside(at + 1, layer, r))
        jx = bz - load(field, 2, layer, r - 1) - (by - load(field, 1, layer - 1, r))
        jy = bx - load(field, 0, layer - 1, r) - (bz - bz_left)
        jz = by - by_left - (bx - load(field, 0, layer, r - 1))
        return (bx, by, bz), (jx, jy, jz)

    def first_push(self, layer, r):
        b, j = self.currents(layer, r, 0)
        a = [self.load(self.state, c, layer, r) for c in range(2)]
        a.append(jnp.zeros_like(a[0]))
        for c, value in enumerate(push(a, b, j)):
            self.later[c, layer, pl.ds(r, 8), :] = value

    def second_field(self, layer, r):
        load, later = self.load, self.later
        ax, ay, az = (load(later, c, layer, r) for c in range(3))
        ay_right = self.right_of(ay, self.beside(2, layer, r))
        az_right = self.right_of(az, self.beside(3, layer, r))
        to = pl.ds(r, 8)
        self.field[0, layer, to, :] = (
            load(later, 2, layer, r + 1) - az - (load(later, 1, layer + 1, r) - ay)
        )
        self.field[1, layer, to, :] = load(later, 0, layer + 1, r) - ax - (az_right - az)
        self.field[2, layer, to, :] = ay_right - ay - (load(later, 0, layer, r + 1) - ax)

    def second_push(self, layer, r):
        b, j = self.currents(layer, r, 2)
        a = [self.load(self.later, c, layer, r) for c in range(3)]
        return [spacing * value for value in push(a, b, j)]

    def clear(self, rows):
        depth, height = self.depth, self.height
        count_z, count_y, _ = self.counts
        zeros = jnp.zeros((height + 8, LANES), jnp.float32)
        line = jnp.zeros((depth + 4, LANES), jnp.float32)
        for exists, layer in ((self.z > 0, 1), (self.z < count_z - 1, depth + 2)):

            @pl.when(jnp.logical_not(exists))
            def _():
                for c in range(3):
                    self.later[c, layer, pl.ds(PAD - 1, height + 8), :] = zeros

        if not rows:
            return
        for exists, row in ((self.y > 0, PAD - 1), (self.y < count_y - 1, PAD + height)):

            @pl.when(jnp.logical_not(exists))
            def _():
                for c in range(3):
                    flat_later = self.later.at[c].reshape((depth + 4) * self.padded, LANES)
                    flat_later[pl.ds(row, depth + 4, stride=self.padded), :] = line

    def run(self, tiles, rows, out, block, sems, pieces=6):
        depth = self.depth
        for layer in range(depth + 3):
            for r in tiles[0]:
                self.first_field(layer, r)
        for layer in range(1, depth + 3):
            for r in tiles[1]:
                self.first_push(layer, r)
        self.clear(rows)
        for layer in range(1, depth + 2):
            for r in tiles[2]:
                self.second_field(layer, r)
        copies = []
        size = depth // pieces
        for piece in range(pieces):
            layers = pl.ds(piece * size, size)
            for layer in range(piece * size, (piece + 1) * size):
                for k, r in enumerate(tiles[3]):
                    for c, value in enumerate(self.second_push(layer + 2, r)):
                        block[c, layer, pl.ds(8 * k, 8), :] = value
            k = 0
            while k < len(tiles[3]):
                run = 1
                while k + run < len(tiles[3]) and tiles[3][k + run] == tiles[3][k] + 8 * run:
                    run += 1
                copies.append(
                    pltpu.make_async_copy(
                        block.at[:, layers, pl.ds(8 * k, 8 * run), :],
                        out.at[:, layers, pl.ds(tiles[3][k] - PAD, 8 * run), :],
                        sems.at[piece, k],
                    )
                )
                copies[-1].start()
                k += run
        for copy in copies:
            copy.wait()


def inner_tiles(height):
    whole = [PAD + r for r in range(0, height, 8)]
    inner = whole[1:-1]
    return whole, whole, [r - 1 for r in inner] + [inner[-1]], inner


def outer_tiles(height):
    top = PAD + height - 8
    return (PAD - 2, top + 1), (PAD - 1, top + 1), (PAD - 1, top), (PAD, top)


def inner_kernel(
    counts, place, side, flat, ext, strips, state, field, later, out, halo, wide, block, sems
):
    depth, height = side.shape[1], side.shape[2]
    rows = pl.ds(PAD, height)
    for c in range(2):
        for k, at in enumerate((0, 1, depth + 2, depth + 3)):
            state[c, at, rows, :] = ext[c, k]
    sums = [jnp.zeros((height, LANES), jnp.float32) for _ in range(2)]
    for layer in range(depth):
        sums = [total + side[c, layer] for c, total in enumerate(sums)]
        state[0, layer + 2, rows, :] = flat[0] + sums[1]
        state[1, layer + 2, rows, :] = flat[1] - sums[0]
    for c in range(2):
        wide[c, rows, :] = strips[c]
        wide[c, pl.ds(0, PAD), :] = jnp.zeros((PAD, wide.shape[2]), jnp.float32)
        wide[c, pl.ds(PAD + height, PAD), :] = jnp.zeros((PAD, wide.shape[2]), jnp.float32)
    stepper = Stepper(counts, place, state, field, later, halo, depth, height)
    stepper.strips(wide)
    stepper.run(inner_tiles(height), False, out, block, sems)


def outer_kernel(
    counts, depth, place, strips, first, second, _s, _f, _l, _o,
    state, field, later, out, halo, wide, block, sems,
):
    _, count_y, _ = counts
    height, padded = strips.shape[1], state.shape[2]
    y = place[1]
    slots = slot_rows(depth)
    layers = depth + 4
    odd = y % 2 == 1
    for low in (True, False):
        exists = (y > 0) if low else (y < count_y - 1)
        row = PAD - 2 if low else PAD + height

        def received(take):
            a, b = first[take, :], second[take, :]
            value = jnp.where(odd, a, b) if low else jnp.where(odd, b, a)
            return jnp.where(exists, value, 0.0)

        for c in range(2):
            flat_state = state.at[c].reshape(layers * padded, LANES)
            for r in range(2):
                flat_state[pl.ds(row + r, layers, stride=padded), :] = received(
                    pl.ds((c * 2 + r) * slots, layers)
                )
            for tile in range(4):
                wide[c, pl.ds(row, 2), pl.ds(tile * LANES, LANES)] = received(
                    pl.ds(4 * slots + (c * 4 + tile) * 2, 2)
                )
    for c in range(2):
        wide[c, pl.ds(PAD, height), :] = strips[c]
    stepper = Stepper(counts, place, state, field, later, halo, depth, height)
    stepper.strips(wide)
    stepper.run(outer_tiles(height), True, out, block, sems)


def call(kernel, shapes, args, scratch=(), limit=16, far_out=0, far_in=(), aliases={}, cost=None):
    vmem, far = pl.BlockSpec(memory_space=pltpu.VMEM), pl.BlockSpec(memory_space=pltpu.HBM)
    specs = [far if k in far_in else vmem for k in range(1, len(args))]
    return pl.pallas_call(
        kernel,
        out_shape=[jax.ShapeDtypeStruct(shape, jnp.float32) for shape in shapes],
        in_specs=[pl.BlockSpec(memory_space=pltpu.SMEM)] + specs,
        out_specs=[vmem] * (len(shapes) - far_out) + [far] * far_out,
        scratch_shapes=[
            pltpu.VMEM(shape, jnp.float32) if isinstance(shape, tuple) else shape
            for shape in scratch
        ],
        input_output_aliases=aliases,
        cost_estimate=cost,
        compiler_params=pltpu.CompilerParams(vmem_limit_bytes=int(limit * 2**20)),
    )(*args)


def gathered_carries(rows, columns):
    height, width = rows.shape
    x, y = lax.axis_index("gx"), lax.axis_index("gy")
    row_totals = lax.all_gather(rows[:, -1], "gx")
    before = (jnp.arange(row_totals.shape[0]) < x)[:, None]
    row_carry = jnp.sum(jnp.where(before, row_totals, 0.0), axis=0)
    column_totals = lax.all_gather(columns[-1], "gy")
    before = (jnp.arange(column_totals.shape[0]) < y)[:, None]
    column_carry = jnp.sum(jnp.where(before, column_totals, 0.0), axis=0)
    return (
        jnp.broadcast_to(row_carry[:, None], (height, width)),
        jnp.broadcast_to(column_carry[None], (8, width)),
    )


def local(side, mag):
    counts = tuple(lax.axis_size(axis) for axis in ("gz", "gy", "gx"))
    count_z, count_y, count_x = counts
    _, depth, height, width = side.shape
    place = jnp.stack([lax.axis_index(axis) for axis in ("gz", "gy", "gx")]).astype(jnp.int32)
    plane, block = (height, width), (2, height, width)
    smem = pl.BlockSpec(memory_space=pltpu.SMEM)
    place = pl.pallas_call(
        place_kernel,
        out_shape=jax.ShapeDtypeStruct(place.shape, jnp.int32),
        in_specs=[smem],
        out_specs=smem,
        cost_estimate=LONG,
    )(place)

    rows, columns = call(plane_kernel, [plane, plane], [place, mag])
    first, second, total, last = call(
        totals_kernel,
        [(2, 2) + plane, (2, 2) + plane, block, (8, width)],
        [place, side, columns],
    )
    first = swap_first(first, "gz")
    second = swap_second(second, "gz") if count_z > 2 else first
    others = [
        swap(total, "gz", functools.partial(lambda step, i: i ^ step, step))
        for step in far_steps(count_z)
    ]
    direct = count_y == 2 and count_x in (2, 4)
    if direct:
        column_carry = swap_first(last, "gy")
    else:
        row_carry, column_carry = gathered_carries(rows, columns)
    packed, edges = call(
        lambda _, *refs: pack_kernel(*refs),
        [(2, height, 2 * LANES), (2, 4, depth, width)],
        [place, side],
        [(2, depth * height, width)],
    )
    far = len(others)
    packed, beside, shared = call(
        functools.partial(z_kernel, count_z, depth, far),
        [(2, height, 2 * LANES), (2, 4) + plane, block],
        [place, first, second, total, columns, column_carry, rows, packed, *others],
    )
    first = swap_first(packed, "gx")
    second = swap_second(packed, "gx") if count_x > 2 else first
    if not direct:
        far_rows = row_carry
    elif count_x == 4:
        far_rows = swap(rows, "gx", lambda i: i ^ 2)
    else:
        far_rows = rows
    messages = 1 if count_y == 2 else 2
    message_rows = 4 * slot_rows(depth) + 16
    strips, flat, ext, edge_rows = call(
        functools.partial(x_kernel, counts, depth),
        [(2, height, 4 * LANES), block, (2, 4) + plane, (messages, message_rows, width)],
        [place, packed, first, second, far_rows, rows, shared, beside, edges],
    )
    first = swap_first(edge_rows[0], "gy")
    second = swap_second(edge_rows[1], "gy") if count_y > 2 else first
    grids = inner_steps(counts, place, side, flat, ext, strips)
    return outer_steps(counts, depth, place, strips, first, second, grids)


def inner_steps(counts, place, side, flat, ext, strips):
    _, depth, height, width = side.shape
    grid = (depth + 4, height + 2 * PAD, width)
    return call(
        functools.partial(inner_kernel, counts),
        [(2,) + grid, (3,) + grid, (3,) + grid, (3, depth, height, width)],
        [place, side, flat, ext, strips],
        [
            (4, 2, height + 2 * PAD, LANES),
            (2, height + 2 * PAD, 4 * LANES),
            (3, depth, height - 16, width),
            pltpu.SemaphoreType.DMA((6, 4)),
        ],
        far_out=1,
    )


def outer_steps(counts, depth, place, strips, first, second, grids):
    height, width = strips.shape[1], first.shape[1]
    result = call(
        functools.partial(outer_kernel, counts, depth),
        [grid.shape for grid in grids],
        [place, strips, first, second, *grids],
        [
            (4, 2, height + 2 * PAD, LANES),
            (2, height + 2 * PAD, 4 * LANES),
            (3, depth, 16, width),
            pltpu.SemaphoreType.DMA((6, 4)),
        ],
        far_out=1,
        far_in=(7,),
        aliases={4 + k: k for k in range(4)},
    )
    return result[3]


def solution(mesh):
    return jax.shard_map(
        local,
        mesh=mesh,
        in_specs=(P(None, "gz", "gy", "gx"), P("gy", "gx")),
        out_specs=P(None, "gz", "gy", "gx"),
        check_vma=False,
    )
```

```python
import functools

import jax
import jax.numpy as jnp
from jax import lax
from jax.experimental import pallas as pl
from jax.experimental.pallas import tpu as pltpu
from jax.sharding import PartitionSpec as P

spacing = 0.0625
friction = 0.004
gain = friction / (spacing * spacing)
LANES = 128
PAD = 8
GROUP = LANES // 4
AXES = ("gz", "gy", "gx")
LONG = pl.CostEstimate(flops=10**10, bytes_accessed=10**5, transcendentals=0)


def near(index, count):
    return (index + 1) % count if index % 2 else (index - 1) % count


def swap(part, axis, partner):
    count = lax.axis_size(axis)
    return lax.ppermute(part, axis, [(i, partner(i)) for i in range(count)])


def swap_first(part, axis):
    return swap(part, axis, lambda i: i ^ 1)


def swap_second(part, axis):
    count = lax.axis_size(axis)
    return swap(part, axis, lambda i: near(i, count))


def far_steps(count):
    return [2] if count == 4 else list(range(2, count))


def lane_index(shape):
    return lax.broadcasted_iota(jnp.int32, shape, len(shape) - 1)


def row_index(shape):
    return lax.broadcasted_iota(jnp.int32, shape, len(shape) - 2)


def columns_at(values, slot):
    first = 4 * (slot % GROUP)
    rolled = pltpu.roll(values, (first + 2) % LANES, 1)
    lane = lane_index(values.shape)
    return jnp.where((lane >= first) & (lane < first + 4), rolled, 0.0)


def spread(values, first):
    lane = lane_index(values.shape)
    moved = pltpu.roll(values, (LANES - first) % LANES, 1) if first else values
    alone = jnp.where(lane < 4, moved, 0.0)
    four = (alone + pltpu.roll(alone, 4, 1)) + (pltpu.roll(alone, 8, 1) + pltpu.roll(alone, 12, 1))
    parts = [four] + [pltpu.roll(four, step, 1) for step in range(16, LANES, 16)]
    while len(parts) > 1:
        parts = [a + b for a, b in zip(parts[::2], parts[1::2])]
    return parts[0]


def place():
    return [lax.axis_index(axis) for axis in AXES]


def token_kernel(out):
    out[...] = jnp.zeros_like(out)


def plane_kernel(mag, rows_out, columns_out):
    rows = columns = mag[...]
    lane, row = lane_index(rows.shape), row_index(rows.shape)
    step = 1
    while step < LANES:
        rows = rows + jnp.where(lane >= step, pltpu.roll(rows, step, 1), 0.0)
        step *= 2
    rows_out[...] = rows
    step = 1
    while step < columns.shape[0]:
        columns = columns + jnp.where(row >= step, pltpu.roll(columns, step, 0), 0.0)
        step *= 2
    columns_out[...] = columns


def totals_kernel(side, columns, first_out, second_out, total_out, last_out):
    depth = side.shape[1]
    z, _, _ = place()
    odd = z % 2 == 1
    upward = odd | (z == 0)
    for c in range(2):
        low0 = side[c, 0]
        low1 = low0 + side[c, 1]
        before = low1
        for layer in range(2, depth - 1):
            before = before + side[c, layer]
        total = before + side[c, depth - 1]
        first_out[c, 0] = jnp.where(odd, low0, before)
        first_out[c, 1] = jnp.where(odd, low1, total)
        second_out[c, 0] = jnp.where(upward, before, low0)
        second_out[c, 1] = jnp.where(upward, total, low1)
        total_out[c] = total
    last_out[...] = columns[pl.ds(columns.shape[0] - 8, 8), :]


def pack_kernel(side, packed_out, rows_out, running):
    depth, height = side.shape[1], side.shape[2]
    for c in range(2):
        total = jnp.zeros(side.shape[2:], jnp.float32)
        packed = [jnp.zeros(side.shape[2:], jnp.float32) for _ in range(2)]
        for layer in range(depth):
            total = total + side[c, layer]
            running[c, pl.ds(layer * height, height), :] = total
            slot = layer + 2
            packed[slot // GROUP] += columns_at(total, slot)
        for tile in range(2):
            packed_out[c, :, pl.ds(tile * LANES, LANES)] = packed[tile]
        for k, row in enumerate((0, 1, height - 2, height - 1)):
            rows_out[c, k] = running[c, pl.ds(row, depth, stride=height), :]


def z_kernel(
    count, depth, far, first, second, total, columns, column_carry, rows, packed, *rest
):
    others, (x_out, ext_out, flat_out) = rest[:far], rest[far:]
    z, y, _ = place()
    odd = z % 2 == 1
    for c in range(2):
        near_a, near_b = (first[c, 0], first[c, 1]), (second[c, 0], second[c, 1])
        low = [jnp.where(odd, a, b) for a, b in zip(near_a, near_b)]
        high = [jnp.where(odd, b, a) for a, b in zip(near_a, near_b)]
        carry = jnp.where(odd, near_a[1], 0.0)
        if count == 4:
            carry = carry + jnp.where((z == 2) | (z == 3), near_b[1], 0.0)
        for step, other in zip(far_steps(count), others):
            carry = carry + jnp.where((z ^ step) < z, other[c], 0.0)
        if c == 0:
            shared = 0.5 * rows[...] - carry
        else:
            before = jnp.where(y > 0, column_carry[7:8, :], 0.0)
            shared = carry - 0.5 * (columns[...] + before)
        layers = (low[0] - low[1], None, total[c] + high[0], total[c] + high[1])
        flat_out[c] = shared
        for k in (0, 2, 3):
            ext_out[c, k] = layers[k]
        ext_out[c, 1] = jnp.zeros_like(carry)
        for tile in range(2):
            values = packed[c, :, pl.ds(tile * LANES, LANES)]
            slots = [(0, layers[0]), (depth + 2, layers[2]), (depth + 3, layers[3])]
            for at, layer in slots + [(depth + 4, shared), (depth + 5, rows[...])]:
                if at // GROUP == tile:
                    values = values + columns_at(layer, at)
            x_out[c, :, pl.ds(tile * LANES, LANES)] = values


def x_kernel(
    counts, depth, packed, first, second, far_rows, rows, shared, beside, edges,
    strips_out, flat_out, ext_out, y_out,
):
    count_z, count_y, count_x = counts
    height = packed.shape[1]
    z, y, x = place()
    odd = x % 2 == 1
    base_tile, base_lane = (depth + 4) // GROUP, 4 * ((depth + 4) % GROUP)
    rows_tile, rows_lane = (depth + 5) // GROUP, 4 * ((depth + 5) % GROUP)

    def tile_of(ref, c, tile):
        return ref[c, :, pl.ds(tile * LANES, LANES)]

    def row_totals(ref):
        return tile_of(ref, 0, rows_tile)[:, rows_lane + 1 : rows_lane + 2]

    own_total = rows[...][:, LANES - 1 :]
    total_a, total_b = row_totals(first), row_totals(second)
    far_total = far_rows[...][:, LANES - 1 :]
    if count_x == 2:
        row_carry = jnp.where(odd, total_a, 0.0)
    elif count_x == 4:
        row_carry = jnp.where(odd, total_a, 0.0) + jnp.where(x >= 2, total_b + far_total, 0.0)
    else:
        row_carry = far_total
    left_total = jnp.where(odd, total_a, total_b)

    lane = lane_index((height, LANES))
    q = lane % 4
    for part in range(2):
        merged = []
        for c in range(2):
            tiles = []
            for tile in range(2):
                own, a, b = (tile_of(ref, c, tile) for ref in (packed, first, second))
                if part == 0:
                    tiles.append(jnp.where(q < 2, jnp.where(odd, a, b), own))
                else:
                    tiles.append(jnp.where(q < 2, own, jnp.where(odd, b, a)))
            merged.append(tiles)
        if part == 0:
            carry = jnp.where(q < 2, row_carry - left_total, row_carry)
        else:
            carry = jnp.where(q < 2, row_carry, row_carry + own_total)
        base_y = spread(merged[0][base_tile], base_lane) + 0.5 * carry
        base_x = spread(merged[1][base_tile], base_lane)
        for tile in range(2):
            slot = lane // 4 + tile * GROUP
            inside = (slot < depth + 4) & ((slot >= 2) | (z > 0))
            inside = inside & ((slot < depth + 2) | (z < count_z - 1))
            if part == 0:
                inside = inside & ((q >= 2) | (x > 0))
            else:
                inside = inside & ((q < 2) | (x < count_x - 1))
            place_at = pl.ds((part * 2 + tile) * LANES, LANES)
            strips_out[0, :, place_at] = jnp.where(inside, base_x + merged[1][tile], 0.0)
            strips_out[1, :, place_at] = jnp.where(inside, base_y - merged[0][tile], 0.0)

    flat_x = shared[1]
    flat_y = shared[0] + 0.5 * row_carry
    flat_out[0] = flat_x
    flat_out[1] = flat_y
    for k in range(4):
        inside = (z > 0) if k < 2 else (z < count_z - 1)
        ext_out[0, k] = jnp.where(inside, flat_x + beside[1, k], 0.0)
        ext_out[1, k] = jnp.where(inside, flat_y - beside[0, k], 0.0)

    slots = slot_rows(depth)
    for message in range(y_out.shape[0]):
        downward = (y % 2 == 1) if message == 0 else (y % 2 == 0)
        for c in range(2):
            for r in range(2):
                start = (c * 2 + r) * slots
                low, high = pl.ds(r, 1), pl.ds(height - 2 + r, 1)
                flat = jnp.where(downward, flat_out[c, low, :], flat_out[c, high, :])
                edge = jnp.where(downward, edges[1 - c, r], edges[1 - c, 2 + r])
                edge = edge if c == 0 else -edge
                y_out[message, pl.ds(start + 2, depth), :] = flat + edge
                for k, at in enumerate((0, 1, depth + 2, depth + 3)):
                    y_out[message, pl.ds(start + at, 1), :] = jnp.where(
                        downward, ext_out[c, k, low, :], ext_out[c, k, high, :]
                    )
            for tile in range(4):
                start = 4 * slots + (c * 4 + tile) * 2
                lanes = pl.ds(tile * LANES, LANES)
                y_out[message, pl.ds(start, 2), :] = jnp.where(
                    downward,
                    strips_out[c, pl.ds(0, 2), lanes],
                    strips_out[c, pl.ds(height - 2, 2), lanes],
                )


def slot_rows(depth):
    return (depth + 4 + 7) // 8 * 8


def following(values, axis, step=1):
    return pltpu.roll(values, values.shape[axis] - step, axis)


def preceding(values, axis, step=1):
    return pltpu.roll(values, step, axis)


def push(a, field, current):
    square = field[0] * field[0] + field[1] * field[1] + field[2] * field[2]
    along = current[0] * field[0] + current[1] * field[1] + current[2] * field[2]
    factor = gain / (square + 1.0)
    p, q = along * factor, square * factor
    return [a[c] + (field[c] * p - current[c] * q) for c in range(3)]


def strip_field(a):
    x, y, z = a
    field_x = following(z, 0) - z - (following(y, 1, 4) - y)
    field_y = following(x, 1, 4) - x - (following(z, 1) - z)
    field_z = following(y, 1) - y - (following(x, 0) - x)
    return field_x, field_y, field_z


def strip_current(b):
    x, y, z = b
    current_x = z - preceding(z, 0) - (y - preceding(y, 1, 4))
    current_y = x - preceding(x, 1, 4) - (z - preceding(z, 1))
    current_z = y - preceding(y, 1) - (x - preceding(x, 0))
    return current_x, current_y, current_z


class Stepper:
    def __init__(self, counts, state, field, later, halo, depth, height):
        self.counts = counts
        self.z, self.y, self.x = place()
        self.state, self.field, self.later, self.halo = state, field, later, halo
        self.depth, self.height = depth, height
        self.padded = state.shape[2]
        lane = lane_index((8, LANES))
        self.last, self.start = lane == LANES - 1, lane == 0

    def load(self, ref, c, layer, row):
        return ref[c, layer, pl.ds(row, 8), :]

    def strips(self, wide):
        depth, height = self.depth, self.height
        count_z, count_y, count_x = self.counts
        half = 2 * LANES
        shape = (self.padded, 2 * half)
        lane, row = lane_index(shape), row_index(shape)
        q = lane % 4
        slot = (lane % half) // 4
        right = lane >= half
        inside = (row >= PAD - 2) & (row < PAD + height + 2) & (slot < depth + 4)
        inside = inside & ((row >= PAD) | (self.y > 0))
        inside = inside & ((row < PAD + height) | (self.y < count_y - 1))
        inside = inside & ((slot >= 2) | (self.z > 0))
        inside = inside & ((slot < depth + 2) | (self.z < count_z - 1))
        inside = inside & (right | (q >= 2) | (self.x > 0))
        inside = inside & (~right | (q < 2) | (self.x < count_x - 1))
        a = [jnp.where(inside, wide[c], 0.0) for c in range(2)]
        a.append(jnp.zeros_like(a[0]))
        b = strip_field(a)
        pick = (lane_index((self.padded, half)) % 4) == 2

        def keep(at, upper, lower):
            value = jnp.where(pick, upper[:, half:], lower[:, :half])
            self.halo[at, 0] = value[:, :LANES]
            self.halo[at, 1] = value[:, LANES:]

        keep(0, a[1], b[1])
        keep(1, a[2], b[2])
        a = [jnp.where(inside, value, 0.0) for value in push(a, b, strip_current(b))]
        b = strip_field(a)
        keep(2, a[1], b[1])
        keep(3, a[2], b[2])

    def beside(self, at, layer, row):
        shift = LANES - 2 - 4 * (layer % GROUP)
        return pltpu.roll(self.halo[at, layer // GROUP, pl.ds(row, 8), :], shift, 1)

    def right_of(self, value, edge):
        return following(jnp.where(self.start, edge, value), 1)

    def left_of(self, value, edge):
        return preceding(jnp.where(self.last, edge, value), 1)

    def first_field(self, layer, r):
        load, state = self.load, self.state
        ax, ay = load(state, 0, layer, r), load(state, 1, layer, r)
        ay_right = self.right_of(ay, self.beside(0, layer, r))
        to = pl.ds(r, 8)
        self.field[0, layer, to, :] = ay - load(state, 1, layer + 1, r)
        self.field[1, layer, to, :] = load(state, 0, layer + 1, r) - ax
        self.field[2, layer, to, :] = ay_right - ay - (load(state, 0, layer, r + 1) - ax)

    def currents(self, layer, r, at):
        load, field = self.load, self.field
        bx, by, bz = (load(field, c, layer, r) for c in range(3))
        by_left = self.left_of(by, self.beside(at, layer, r))
        bz_left = self.left_of(bz, self.beside(at + 1, layer, r))
        jx = bz - load(field, 2, layer, r - 1) - (by - load(field, 1, layer - 1, r))
        jy = bx - load(field, 0, layer - 1, r) - (bz - bz_left)
        jz = by - by_left - (bx - load(field, 0, layer, r - 1))
        return (bx, by, bz), (jx, jy, jz)

    def first_push(self, layer, r):
        b, j = self.currents(layer, r, 0)
        a = [self.load(self.state, c, layer, r) for c in range(2)]
        a.append(jnp.zeros_like(a[0]))
        for c, value in enumerate(push(a, b, j)):
            self.later[c, layer, pl.ds(r, 8), :] = value

    def second_field(self, layer, r):
        load, later = self.load, self.later
        ax, ay, az = (load(later, c, layer, r) for c in range(3))
        ay_right = self.right_of(ay, self.beside(2, layer, r))
        az_right = self.right_of(az, self.beside(3, layer, r))
        to = pl.ds(r, 8)
        self.field[0, layer, to, :] = (
            load(later, 2, layer, r + 1) - az - (load(later, 1, layer + 1, r) - ay)
        )
        self.field[1, layer, to, :] = load(later, 0, layer + 1, r) - ax - (az_right - az)
        self.field[2, layer, to, :] = ay_right - ay - (load(later, 0, layer, r + 1) - ax)

    def second_push(self, layer, r):
        b, j = self.currents(layer, r, 2)
        a = [self.load(self.later, c, layer, r) for c in range(3)]
        return [spacing * value for value in push(a, b, j)]

    def clear(self, rows):
        depth, height = self.depth, self.height
        count_z, count_y, _ = self.counts
        zeros = jnp.zeros((height + 8, LANES), jnp.float32)
        line = jnp.zeros((depth + 4, LANES), jnp.float32)
        for exists, layer in ((self.z > 0, 1), (self.z < count_z - 1, depth + 2)):

            @pl.when(jnp.logical_not(exists))
            def _():
                for c in range(3):
                    self.later[c, layer, pl.ds(PAD - 1, height + 8), :] = zeros

        if not rows:
            return
        for exists, row in ((self.y > 0, PAD - 1), (self.y < count_y - 1, PAD + height)):

            @pl.when(jnp.logical_not(exists))
            def _():
                for c in range(3):
                    flat_later = self.later.at[c].reshape((depth + 4) * self.padded, LANES)
                    flat_later[pl.ds(row, depth + 4, stride=self.padded), :] = line

    def run(self, tiles, rows, out, block, sems, pieces=6):
        depth = self.depth
        for layer in range(depth + 3):
            for r in tiles[0]:
                self.first_field(layer, r)
        for layer in range(1, depth + 3):
            for r in tiles[1]:
                self.first_push(layer, r)
        self.clear(rows)
        for layer in range(1, depth + 2):
            for r in tiles[2]:
                self.second_field(layer, r)
        copies = []
        size = depth // pieces
        for piece in range(pieces):
            layers = pl.ds(piece * size, size)
            for layer in range(piece * size, (piece + 1) * size):
                for k, r in enumerate(tiles[3]):
                    for c, value in enumerate(self.second_push(layer + 2, r)):
                        block[c, layer, pl.ds(8 * k, 8), :] = value
            k = 0
            while k < len(tiles[3]):
                run = 1
                while k + run < len(tiles[3]) and tiles[3][k + run] == tiles[3][k] + 8 * run:
                    run += 1
                copies.append(
                    pltpu.make_async_copy(
                        block.at[:, layers, pl.ds(8 * k, 8 * run), :],
                        out.at[:, layers, pl.ds(tiles[3][k] - PAD, 8 * run), :],
                        sems.at[piece, k],
                    )
                )
                copies[-1].start()
                k += run
        for copy in copies:
            copy.wait()


def inner_tiles(height):
    whole = [PAD + r for r in range(0, height, 8)]
    inner = whole[1:-1]
    return whole, whole, [r - 1 for r in inner] + [inner[-1]], inner


def outer_tiles(height):
    top = PAD + height - 8
    return (PAD - 2, top + 1), (PAD - 1, top + 1), (PAD - 1, top), (PAD, top)


def inner_kernel(
    counts, side, flat, ext, strips, state, field, later, out, halo, wide, block, sems
):
    depth, height = side.shape[1], side.shape[2]
    rows = pl.ds(PAD, height)
    for c in range(2):
        for k, at in enumerate((0, 1, depth + 2, depth + 3)):
            state[c, at, rows, :] = ext[c, k]
    sums = [jnp.zeros((height, LANES), jnp.float32) for _ in range(2)]
    for layer in range(depth):
        sums = [total + side[c, layer] for c, total in enumerate(sums)]
        state[0, layer + 2, rows, :] = flat[0] + sums[1]
        state[1, layer + 2, rows, :] = flat[1] - sums[0]
    for c in range(2):
        wide[c, rows, :] = strips[c]
        wide[c, pl.ds(0, PAD), :] = jnp.zeros((PAD, wide.shape[2]), jnp.float32)
        wide[c, pl.ds(PAD + height, PAD), :] = jnp.zeros((PAD, wide.shape[2]), jnp.float32)
    stepper = Stepper(counts, state, field, later, halo, depth, height)
    stepper.strips(wide)
    stepper.run(inner_tiles(height), False, out, block, sems)


def outer_kernel(
    counts, depth, strips, first, second, _s, _f, _l, _o,
    state, field, later, out, halo, wide, block, sems,
):
    _, count_y, _ = counts
    height, padded = strips.shape[1], state.shape[2]
    _, y, _ = place()
    slots = slot_rows(depth)
    layers = depth + 4
    odd = y % 2 == 1
    for low in (True, False):
        exists = (y > 0) if low else (y < count_y - 1)
        row = PAD - 2 if low else PAD + height

        def received(take):
            a, b = first[take, :], second[take, :]
            value = jnp.where(odd, a, b) if low else jnp.where(odd, b, a)
            return jnp.where(exists, value, 0.0)

        for c in range(2):
            flat_state = state.at[c].reshape(layers * padded, LANES)
            for r in range(2):
                flat_state[pl.ds(row + r, layers, stride=padded), :] = received(
                    pl.ds((c * 2 + r) * slots, layers)
                )
            for tile in range(4):
                wide[c, pl.ds(row, 2), pl.ds(tile * LANES, LANES)] = received(
                    pl.ds(4 * slots + (c * 4 + tile) * 2, 2)
                )
    for c in range(2):
        wide[c, pl.ds(PAD, height), :] = strips[c]
    stepper = Stepper(counts, state, field, later, halo, depth, height)
    stepper.strips(wide)
    stepper.run(outer_tiles(height), True, out, block, sems)


def call(kernel, shapes, args, scratch=(), limit=16, far_out=0, far_in=(), aliases={}, cost=None):
    vmem, far = pl.BlockSpec(memory_space=pltpu.VMEM), pl.BlockSpec(memory_space=pltpu.HBM)
    specs = [far if k in far_in else vmem for k in range(len(args))]
    return pl.pallas_call(
        kernel,
        out_shape=[jax.ShapeDtypeStruct(shape, jnp.float32) for shape in shapes],
        in_specs=specs,
        out_specs=[vmem] * (len(shapes) - far_out) + [far] * far_out,
        scratch_shapes=[
            pltpu.VMEM(shape, jnp.float32) if isinstance(shape, tuple) else shape
            for shape in scratch
        ],
        input_output_aliases=aliases,
        cost_estimate=cost,
        compiler_params=pltpu.CompilerParams(vmem_limit_bytes=int(limit * 2**20)),
    )(*args)


def gathered_carries(rows, columns):
    height, width = rows.shape
    x, y = lax.axis_index("gx"), lax.axis_index("gy")
    row_totals = lax.all_gather(rows[:, -1], "gx")
    before = (jnp.arange(row_totals.shape[0]) < x)[:, None]
    row_carry = jnp.sum(jnp.where(before, row_totals, 0.0), axis=0)
    column_totals = lax.all_gather(columns[-1], "gy")
    before = (jnp.arange(column_totals.shape[0]) < y)[:, None]
    column_carry = jnp.sum(jnp.where(before, column_totals, 0.0), axis=0)
    return (
        jnp.broadcast_to(row_carry[:, None], (height, width)),
        jnp.broadcast_to(column_carry[None], (8, width)),
    )


def local(side, mag):
    counts = tuple(lax.axis_size(axis) for axis in ("gz", "gy", "gx"))
    count_z, count_y, count_x = counts
    _, depth, height, width = side.shape
    plane, block = (height, width), (2, height, width)
    (token,) = call(token_kernel, [(8, LANES)], [], cost=LONG)
    rows, columns = call(
        lambda _, *refs: plane_kernel(*refs), [plane, plane], [token, mag]
    )
    first, second, total, last = call(
        totals_kernel,
        [(2, 2) + plane, (2, 2) + plane, block, (8, width)],
        [side, columns],
    )
    first = swap_first(first, "gz")
    second = swap_second(second, "gz") if count_z > 2 else first
    others = [
        swap(total, "gz", functools.partial(lambda step, i: i ^ step, step))
        for step in far_steps(count_z)
    ]
    direct = count_y == 2 and count_x in (2, 4)
    if direct:
        column_carry = swap_first(last, "gy")
    else:
        row_carry, column_carry = gathered_carries(rows, columns)
    packed, edges = call(
        pack_kernel,
        [(2, height, 2 * LANES), (2, 4, depth, width)],
        [side],
        [(2, depth * height, width)],
    )
    far = len(others)
    packed, beside, shared = call(
        functools.partial(z_kernel, count_z, depth, far),
        [(2, height, 2 * LANES), (2, 4) + plane, block],
        [first, second, total, columns, column_carry, rows, packed, *others],
    )
    first = swap_first(packed, "gx")
    second = swap_second(packed, "gx") if count_x > 2 else first
    if not direct:
        far_rows = row_carry
    elif count_x == 4:
        far_rows = swap(rows, "gx", lambda i: i ^ 2)
    else:
        far_rows = rows
    messages = 1 if count_y == 2 else 2
    message_rows = 4 * slot_rows(depth) + 16
    strips, flat, ext, edge_rows = call(
        functools.partial(x_kernel, counts, depth),
        [(2, height, 4 * LANES), block, (2, 4) + plane, (messages, message_rows, width)],
        [packed, first, second, far_rows, rows, shared, beside, edges],
    )
    first = swap_first(edge_rows[0], "gy")
    second = swap_second(edge_rows[1], "gy") if count_y > 2 else first
    grids = inner_steps(counts, side, flat, ext, strips)
    return outer_steps(counts, depth, strips, first, second, grids)


def inner_steps(counts, side, flat, ext, strips):
    _, depth, height, width = side.shape
    grid = (depth + 4, height + 2 * PAD, width)
    return call(
        functools.partial(inner_kernel, counts),
        [(2,) + grid, (3,) + grid, (3,) + grid, (3, depth, height, width)],
        [side, flat, ext, strips],
        [
            (4, 2, height + 2 * PAD, LANES),
            (2, height + 2 * PAD, 4 * LANES),
            (3, depth, height - 16, width),
            pltpu.SemaphoreType.DMA((6, 4)),
        ],
        far_out=1,
    )


def outer_steps(counts, depth, strips, first, second, grids):
    height, width = strips.shape[1], first.shape[1]
    result = call(
        functools.partial(outer_kernel, counts, depth),
        [grid.shape for grid in grids],
        [strips, first, second, *grids],
        [
            (4, 2, height + 2 * PAD, LANES),
            (2, height + 2 * PAD, 4 * LANES),
            (3, depth, 16, width),
            pltpu.SemaphoreType.DMA((6, 4)),
        ],
        far_out=1,
        far_in=(6,),
        aliases={3 + k: k for k in range(4)},
    )
    return result[3]


def solution(mesh):
    return jax.shard_map(
        local,
        mesh=mesh,
        in_specs=(P(None, "gz", "gy", "gx"), P("gy", "gx")),
        out_specs=P(None, "gz", "gy", "gx"),
        check_vma=False,
    )
```

```python
import functools

import jax
import jax.numpy as jnp
from jax import lax
from jax.experimental import pallas as pl
from jax.experimental.pallas import tpu as pltpu
from jax.sharding import PartitionSpec as P

spacing = 0.0625
friction = 0.004
gain = friction / (spacing * spacing)
LANES = 128
PAD = 8
GROUP = LANES // 4
AXES = ("gz", "gy", "gx")
LONG = pl.CostEstimate(flops=10**10, bytes_accessed=10**5, transcendentals=0)


def near(index, count):
    return (index + 1) % count if index % 2 else (index - 1) % count


def swap(part, axis, partner):
    count = lax.axis_size(axis)
    return lax.ppermute(part, axis, [(i, partner(i)) for i in range(count)])


def swap_first(part, axis):
    return swap(part, axis, lambda i: i ^ 1)


def swap_second(part, axis):
    count = lax.axis_size(axis)
    return swap(part, axis, lambda i: near(i, count))


def far_steps(count):
    return [2] if count == 4 else list(range(2, count))


def lane_index(shape):
    return lax.broadcasted_iota(jnp.int32, shape, len(shape) - 1)


def row_index(shape):
    return lax.broadcasted_iota(jnp.int32, shape, len(shape) - 2)


def columns_at(values, slot):
    first = 4 * (slot % GROUP)
    rolled = pltpu.roll(values, (first + 2) % LANES, 1)
    lane = lane_index(values.shape)
    return jnp.where((lane >= first) & (lane < first + 4), rolled, 0.0)


def spread(values, first):
    lane = lane_index(values.shape)
    moved = pltpu.roll(values, (LANES - first) % LANES, 1) if first else values
    alone = jnp.where(lane < 4, moved, 0.0)
    four = (alone + pltpu.roll(alone, 4, 1)) + (pltpu.roll(alone, 8, 1) + pltpu.roll(alone, 12, 1))
    parts = [four] + [pltpu.roll(four, step, 1) for step in range(16, LANES, 16)]
    while len(parts) > 1:
        parts = [a + b for a, b in zip(parts[::2], parts[1::2])]
    return parts[0]


def place():
    return [lax.axis_index(axis) for axis in AXES]


def token_kernel(out):
    out[...] = jnp.zeros_like(out)


def plane_kernel(mag, rows_out, columns_out):
    rows = columns = mag[...]
    lane, row = lane_index(rows.shape), row_index(rows.shape)
    step = 1
    while step < LANES:
        rows = rows + jnp.where(lane >= step, pltpu.roll(rows, step, 1), 0.0)
        step *= 2
    rows_out[...] = rows
    step = 1
    while step < columns.shape[0]:
        columns = columns + jnp.where(row >= step, pltpu.roll(columns, step, 0), 0.0)
        step *= 2
    columns_out[...] = columns


def totals_kernel(side, columns, first_out, second_out, total_out, last_out):
    depth = side.shape[1]
    z, _, _ = place()
    odd = z % 2 == 1
    upward = odd | (z == 0)
    for c in range(2):
        low0 = side[c, 0]
        low1 = low0 + side[c, 1]
        before = low1
        for layer in range(2, depth - 1):
            before = before + side[c, layer]
        total = before + side[c, depth - 1]
        first_out[c, 0] = jnp.where(odd, low0, before)
        first_out[c, 1] = jnp.where(odd, low1, total)
        second_out[c, 0] = jnp.where(upward, before, low0)
        second_out[c, 1] = jnp.where(upward, total, low1)
        total_out[c] = total
    last_out[...] = columns[pl.ds(columns.shape[0] - 8, 8), :]


def pack_kernel(side, packed_out, rows_out, running):
    depth, height = side.shape[1], side.shape[2]
    for c in range(2):
        total = jnp.zeros(side.shape[2:], jnp.float32)
        packed = [jnp.zeros(side.shape[2:], jnp.float32) for _ in range(2)]
        for layer in range(depth):
            total = total + side[c, layer]
            running[c, pl.ds(layer * height, height), :] = total
            slot = layer + 2
            packed[slot // GROUP] += columns_at(total, slot)
        for tile in range(2):
            packed_out[c, :, pl.ds(tile * LANES, LANES)] = packed[tile]
        for k, row in enumerate((0, 1, height - 2, height - 1)):
            rows_out[c, k] = running[c, pl.ds(row, depth, stride=height), :]


def z_kernel(
    count, depth, far, first, second, total, columns, column_carry, far_rows, rows, packed, *rest
):
    others, (x_out, ext_out, flat_out, far_out) = rest[:far], rest[far:]
    far_out[...] = far_rows[...]
    z, y, _ = place()
    odd = z % 2 == 1
    for c in range(2):
        near_a, near_b = (first[c, 0], first[c, 1]), (second[c, 0], second[c, 1])
        low = [jnp.where(odd, a, b) for a, b in zip(near_a, near_b)]
        high = [jnp.where(odd, b, a) for a, b in zip(near_a, near_b)]
        carry = jnp.where(odd, near_a[1], 0.0)
        if count == 4:
            carry = carry + jnp.where((z == 2) | (z == 3), near_b[1], 0.0)
        for step, other in zip(far_steps(count), others):
            carry = carry + jnp.where((z ^ step) < z, other[c], 0.0)
        if c == 0:
            shared = 0.5 * rows[...] - carry
        else:
            before = jnp.where(y > 0, column_carry[7:8, :], 0.0)
            shared = carry - 0.5 * (columns[...] + before)
        layers = (low[0] - low[1], None, total[c] + high[0], total[c] + high[1])
        flat_out[c] = shared
        for k in (0, 2, 3):
            ext_out[c, k] = layers[k]
        ext_out[c, 1] = jnp.zeros_like(carry)
        for tile in range(2):
            values = packed[c, :, pl.ds(tile * LANES, LANES)]
            slots = [(0, layers[0]), (depth + 2, layers[2]), (depth + 3, layers[3])]
            for at, layer in slots + [(depth + 4, shared), (depth + 5, rows[...])]:
                if at // GROUP == tile:
                    values = values + columns_at(layer, at)
            x_out[c, :, pl.ds(tile * LANES, LANES)] = values


def x_kernel(
    counts, depth, packed, first, second, far_rows, rows, shared, beside, edges,
    strips_out, flat_out, ext_out, y_out,
):
    count_z, count_y, count_x = counts
    height = packed.shape[1]
    z, y, x = place()
    odd = x % 2 == 1
    base_tile, base_lane = (depth + 4) // GROUP, 4 * ((depth + 4) % GROUP)
    rows_tile, rows_lane = (depth + 5) // GROUP, 4 * ((depth + 5) % GROUP)

    def tile_of(ref, c, tile):
        return ref[c, :, pl.ds(tile * LANES, LANES)]

    def row_totals(ref):
        return tile_of(ref, 0, rows_tile)[:, rows_lane + 1 : rows_lane + 2]

    own_total = rows[...][:, LANES - 1 :]
    total_a, total_b = row_totals(first), row_totals(second)
    far_total = far_rows[...][:, LANES - 1 :]
    if count_x == 2:
        row_carry = jnp.where(odd, total_a, 0.0)
    elif count_x == 4:
        row_carry = jnp.where(odd, total_a, 0.0) + jnp.where(x >= 2, total_b + far_total, 0.0)
    else:
        row_carry = far_total
    left_total = jnp.where(odd, total_a, total_b)

    lane = lane_index((height, LANES))
    q = lane % 4
    for part in range(2):
        merged = []
        for c in range(2):
            tiles = []
            for tile in range(2):
                own, a, b = (tile_of(ref, c, tile) for ref in (packed, first, second))
                if part == 0:
                    tiles.append(jnp.where(q < 2, jnp.where(odd, a, b), own))
                else:
                    tiles.append(jnp.where(q < 2, own, jnp.where(odd, b, a)))
            merged.append(tiles)
        if part == 0:
            carry = jnp.where(q < 2, row_carry - left_total, row_carry)
        else:
            carry = jnp.where(q < 2, row_carry, row_carry + own_total)
        base_y = spread(merged[0][base_tile], base_lane) + 0.5 * carry
        base_x = spread(merged[1][base_tile], base_lane)
        for tile in range(2):
            slot = lane // 4 + tile * GROUP
            inside = (slot < depth + 4) & ((slot >= 2) | (z > 0))
            inside = inside & ((slot < depth + 2) | (z < count_z - 1))
            if part == 0:
                inside = inside & ((q >= 2) | (x > 0))
            else:
                inside = inside & ((q < 2) | (x < count_x - 1))
            place_at = pl.ds((part * 2 + tile) * LANES, LANES)
            strips_out[0, :, place_at] = jnp.where(inside, base_x + merged[1][tile], 0.0)
            strips_out[1, :, place_at] = jnp.where(inside, base_y - merged[0][tile], 0.0)

    flat_x = shared[1]
    flat_y = shared[0] + 0.5 * row_carry
    flat_out[0] = flat_x
    flat_out[1] = flat_y
    for k in range(4):
        inside = (z > 0) if k < 2 else (z < count_z - 1)
        ext_out[0, k] = jnp.where(inside, flat_x + beside[1, k], 0.0)
        ext_out[1, k] = jnp.where(inside, flat_y - beside[0, k], 0.0)

    slots = slot_rows(depth)
    for message in range(y_out.shape[0]):
        downward = (y % 2 == 1) if message == 0 else (y % 2 == 0)
        for c in range(2):
            for r in range(2):
                start = (c * 2 + r) * slots
                low, high = pl.ds(r, 1), pl.ds(height - 2 + r, 1)
                flat = jnp.where(downward, flat_out[c, low, :], flat_out[c, high, :])
                edge = jnp.where(downward, edges[1 - c, r], edges[1 - c, 2 + r])
                edge = edge if c == 0 else -edge
                y_out[message, pl.ds(start + 2, depth), :] = flat + edge
                for k, at in enumerate((0, 1, depth + 2, depth + 3)):
                    y_out[message, pl.ds(start + at, 1), :] = jnp.where(
                        downward, ext_out[c, k, low, :], ext_out[c, k, high, :]
                    )
            for tile in range(4):
                start = 4 * slots + (c * 4 + tile) * 2
                lanes = pl.ds(tile * LANES, LANES)
                y_out[message, pl.ds(start, 2), :] = jnp.where(
                    downward,
                    strips_out[c, pl.ds(0, 2), lanes],
                    strips_out[c, pl.ds(height - 2, 2), lanes],
                )


def slot_rows(depth):
    return (depth + 4 + 7) // 8 * 8


def following(values, axis, step=1):
    return pltpu.roll(values, values.shape[axis] - step, axis)


def preceding(values, axis, step=1):
    return pltpu.roll(values, step, axis)


def push(a, field, current):
    square = field[0] * field[0] + field[1] * field[1] + field[2] * field[2]
    along = current[0] * field[0] + current[1] * field[1] + current[2] * field[2]
    factor = gain / (square + 1.0)
    p, q = along * factor, square * factor
    return [a[c] + (field[c] * p - current[c] * q) for c in range(3)]


def strip_field(a):
    x, y, z = a
    field_x = following(z, 0) - z - (following(y, 1, 4) - y)
    field_y = following(x, 1, 4) - x - (following(z, 1) - z)
    field_z = following(y, 1) - y - (following(x, 0) - x)
    return field_x, field_y, field_z


def strip_current(b):
    x, y, z = b
    current_x = z - preceding(z, 0) - (y - preceding(y, 1, 4))
    current_y = x - preceding(x, 1, 4) - (z - preceding(z, 1))
    current_z = y - preceding(y, 1) - (x - preceding(x, 0))
    return current_x, current_y, current_z


class Stepper:
    def __init__(self, counts, state, field, later, halo, depth, height):
        self.counts = counts
        self.z, self.y, self.x = place()
        self.state, self.field, self.later, self.halo = state, field, later, halo
        self.depth, self.height = depth, height
        self.padded = state.shape[2]
        lane = lane_index((8, LANES))
        self.last, self.start = lane == LANES - 1, lane == 0

    def load(self, ref, c, layer, row):
        return ref[c, layer, pl.ds(row, 8), :]

    def strips(self, wide):
        depth, height = self.depth, self.height
        count_z, count_y, count_x = self.counts
        half = 2 * LANES
        shape = (self.padded, 2 * half)
        lane, row = lane_index(shape), row_index(shape)
        q = lane % 4
        slot = (lane % half) // 4
        right = lane >= half
        inside = (row >= PAD - 2) & (row < PAD + height + 2) & (slot < depth + 4)
        inside = inside & ((row >= PAD) | (self.y > 0))
        inside = inside & ((row < PAD + height) | (self.y < count_y - 1))
        inside = inside & ((slot >= 2) | (self.z > 0))
        inside = inside & ((slot < depth + 2) | (self.z < count_z - 1))
        inside = inside & (right | (q >= 2) | (self.x > 0))
        inside = inside & (~right | (q < 2) | (self.x < count_x - 1))
        a = [jnp.where(inside, wide[c], 0.0) for c in range(2)]
        a.append(jnp.zeros_like(a[0]))
        b = strip_field(a)
        pick = (lane_index((self.padded, half)) % 4) == 2

        def keep(at, upper, lower):
            value = jnp.where(pick, upper[:, half:], lower[:, :half])
            self.halo[at, 0] = value[:, :LANES]
            self.halo[at, 1] = value[:, LANES:]

        keep(0, a[1], b[1])
        keep(1, a[2], b[2])
        a = [jnp.where(inside, value, 0.0) for value in push(a, b, strip_current(b))]
        b = strip_field(a)
        keep(2, a[1], b[1])
        keep(3, a[2], b[2])

    def beside(self, at, layer, row):
        shift = LANES - 2 - 4 * (layer % GROUP)
        return pltpu.roll(self.halo[at, layer // GROUP, pl.ds(row, 8), :], shift, 1)

    def right_of(self, value, edge):
        return following(jnp.where(self.start, edge, value), 1)

    def left_of(self, value, edge):
        return preceding(jnp.where(self.last, edge, value), 1)

    def first_field(self, layer, r):
        load, state = self.load, self.state
        ax, ay = load(state, 0, layer, r), load(state, 1, layer, r)
        ay_right = self.right_of(ay, self.beside(0, layer, r))
        to = pl.ds(r, 8)
        self.field[0, layer, to, :] = ay - load(state, 1, layer + 1, r)
        self.field[1, layer, to, :] = load(state, 0, layer + 1, r) - ax
        self.field[2, layer, to, :] = ay_right - ay - (load(state, 0, layer, r + 1) - ax)

    def currents(self, layer, r, at):
        load, field = self.load, self.field
        bx, by, bz = (load(field, c, layer, r) for c in range(3))
        by_left = self.left_of(by, self.beside(at, layer, r))
        bz_left = self.left_of(bz, self.beside(at + 1, layer, r))
        jx = bz - load(field, 2, layer, r - 1) - (by - load(field, 1, layer - 1, r))
        jy = bx - load(field, 0, layer - 1, r) - (bz - bz_left)
        jz = by - by_left - (bx - load(field, 0, layer, r - 1))
        return (bx, by, bz), (jx, jy, jz)

    def first_push(self, layer, r):
        b, j = self.currents(layer, r, 0)
        a = [self.load(self.state, c, layer, r) for c in range(2)]
        a.append(jnp.zeros_like(a[0]))
        for c, value in enumerate(push(a, b, j)):
            self.later[c, layer, pl.ds(r, 8), :] = value

    def second_field(self, layer, r):
        load, later = self.load, self.later
        ax, ay, az = (load(later, c, layer, r) for c in range(3))
        ay_right = self.right_of(ay, self.beside(2, layer, r))
        az_right = self.right_of(az, self.beside(3, layer, r))
        to = pl.ds(r, 8)
        self.field[0, layer, to, :] = (
            load(later, 2, layer, r + 1) - az - (load(later, 1, layer + 1, r) - ay)
        )
        self.field[1, layer, to, :] = load(later, 0, layer + 1, r) - ax - (az_right - az)
        self.field[2, layer, to, :] = ay_right - ay - (load(later, 0, layer, r + 1) - ax)

    def second_push(self, layer, r):
        b, j = self.currents(layer, r, 2)
        a = [self.load(self.later, c, layer, r) for c in range(3)]
        return [spacing * value for value in push(a, b, j)]

    def clear(self, rows):
        depth, height = self.depth, self.height
        count_z, count_y, _ = self.counts
        zeros = jnp.zeros((height + 8, LANES), jnp.float32)
        line = jnp.zeros((depth + 4, LANES), jnp.float32)
        for exists, layer in ((self.z > 0, 1), (self.z < count_z - 1, depth + 2)):

            @pl.when(jnp.logical_not(exists))
            def _():
                for c in range(3):
                    self.later[c, layer, pl.ds(PAD - 1, height + 8), :] = zeros

        if not rows:
            return
        for exists, row in ((self.y > 0, PAD - 1), (self.y < count_y - 1, PAD + height)):

            @pl.when(jnp.logical_not(exists))
            def _():
                for c in range(3):
                    flat_later = self.later.at[c].reshape((depth + 4) * self.padded, LANES)
                    flat_later[pl.ds(row, depth + 4, stride=self.padded), :] = line

    def run(self, tiles, rows, out, block, sems, pieces=6):
        depth = self.depth
        for layer in range(depth + 3):
            for r in tiles[0]:
                self.first_field(layer, r)
        for layer in range(1, depth + 3):
            for r in tiles[1]:
                self.first_push(layer, r)
        self.clear(rows)
        for layer in range(1, depth + 2):
            for r in tiles[2]:
                self.second_field(layer, r)
        copies = []
        size = depth // pieces
        for piece in range(pieces):
            layers = pl.ds(piece * size, size)
            for layer in range(piece * size, (piece + 1) * size):
                for k, r in enumerate(tiles[3]):
                    for c, value in enumerate(self.second_push(layer + 2, r)):
                        block[c, layer, pl.ds(8 * k, 8), :] = value
            k = 0
            while k < len(tiles[3]):
                run = 1
                while k + run < len(tiles[3]) and tiles[3][k + run] == tiles[3][k] + 8 * run:
                    run += 1
                copies.append(
                    pltpu.make_async_copy(
                        block.at[:, layers, pl.ds(8 * k, 8 * run), :],
                        out.at[:, layers, pl.ds(tiles[3][k] - PAD, 8 * run), :],
                        sems.at[piece, k],
                    )
                )
                copies[-1].start()
                k += run
        for copy in copies:
            copy.wait()


def inner_tiles(height):
    whole = [PAD + r for r in range(0, height, 8)]
    inner = whole[1:-1]
    return whole, whole, [r - 1 for r in inner] + [inner[-1]], inner


def outer_tiles(height):
    top = PAD + height - 8
    return (PAD - 2, top + 1), (PAD - 1, top + 1), (PAD - 1, top), (PAD, top)


def inner_kernel(
    counts, side, flat, ext, strips, state, field, later, out, halo, wide, block, sems
):
    depth, height = side.shape[1], side.shape[2]
    rows = pl.ds(PAD, height)
    for c in range(2):
        for k, at in enumerate((0, 1, depth + 2, depth + 3)):
            state[c, at, rows, :] = ext[c, k]
    sums = [jnp.zeros((height, LANES), jnp.float32) for _ in range(2)]
    for layer in range(depth):
        sums = [total + side[c, layer] for c, total in enumerate(sums)]
        state[0, layer + 2, rows, :] = flat[0] + sums[1]
        state[1, layer + 2, rows, :] = flat[1] - sums[0]
    for c in range(2):
        wide[c, rows, :] = strips[c]
        wide[c, pl.ds(0, PAD), :] = jnp.zeros((PAD, wide.shape[2]), jnp.float32)
        wide[c, pl.ds(PAD + height, PAD), :] = jnp.zeros((PAD, wide.shape[2]), jnp.float32)
    stepper = Stepper(counts, state, field, later, halo, depth, height)
    stepper.strips(wide)
    stepper.run(inner_tiles(height), False, out, block, sems)


def outer_kernel(
    counts, depth, strips, first, second, _s, _f, _l, _o,
    state, field, later, out, halo, wide, block, sems,
):
    _, count_y, _ = counts
    height, padded = strips.shape[1], state.shape[2]
    _, y, _ = place()
    slots = slot_rows(depth)
    layers = depth + 4
    odd = y % 2 == 1
    for low in (True, False):
        exists = (y > 0) if low else (y < count_y - 1)
        row = PAD - 2 if low else PAD + height

        def received(take):
            a, b = first[take, :], second[take, :]
            value = jnp.where(odd, a, b) if low else jnp.where(odd, b, a)
            return jnp.where(exists, value, 0.0)

        for c in range(2):
            flat_state = state.at[c].reshape(layers * padded, LANES)
            for r in range(2):
                flat_state[pl.ds(row + r, layers, stride=padded), :] = received(
                    pl.ds((c * 2 + r) * slots, layers)
                )
            for tile in range(4):
                wide[c, pl.ds(row, 2), pl.ds(tile * LANES, LANES)] = received(
                    pl.ds(4 * slots + (c * 4 + tile) * 2, 2)
                )
    for c in range(2):
        wide[c, pl.ds(PAD, height), :] = strips[c]
    stepper = Stepper(counts, state, field, later, halo, depth, height)
    stepper.strips(wide)
    stepper.run(outer_tiles(height), True, out, block, sems)


def call(kernel, shapes, args, scratch=(), limit=16, far_out=0, far_in=(), aliases={}, cost=None):
    vmem, far = pl.BlockSpec(memory_space=pltpu.VMEM), pl.BlockSpec(memory_space=pltpu.HBM)
    specs = [far if k in far_in else vmem for k in range(len(args))]
    return pl.pallas_call(
        kernel,
        out_shape=[jax.ShapeDtypeStruct(shape, jnp.float32) for shape in shapes],
        in_specs=specs,
        out_specs=[vmem] * (len(shapes) - far_out) + [far] * far_out,
        scratch_shapes=[
            pltpu.VMEM(shape, jnp.float32) if isinstance(shape, tuple) else shape
            for shape in scratch
        ],
        input_output_aliases=aliases,
        cost_estimate=cost,
        compiler_params=pltpu.CompilerParams(vmem_limit_bytes=int(limit * 2**20)),
    )(*args)


def gathered_carries(rows, columns):
    height, width = rows.shape
    x, y = lax.axis_index("gx"), lax.axis_index("gy")
    row_totals = lax.all_gather(rows[:, -1], "gx")
    before = (jnp.arange(row_totals.shape[0]) < x)[:, None]
    row_carry = jnp.sum(jnp.where(before, row_totals, 0.0), axis=0)
    column_totals = lax.all_gather(columns[-1], "gy")
    before = (jnp.arange(column_totals.shape[0]) < y)[:, None]
    column_carry = jnp.sum(jnp.where(before, column_totals, 0.0), axis=0)
    return (
        jnp.broadcast_to(row_carry[:, None], (height, width)),
        jnp.broadcast_to(column_carry[None], (8, width)),
    )


def local(side, mag):
    counts = tuple(lax.axis_size(axis) for axis in ("gz", "gy", "gx"))
    count_z, count_y, count_x = counts
    _, depth, height, width = side.shape
    plane, block = (height, width), (2, height, width)
    (token,) = call(token_kernel, [(8, LANES)], [], cost=LONG)
    rows, columns = call(
        lambda _, *refs: plane_kernel(*refs), [plane, plane], [token, mag]
    )
    first, second, total, last = call(
        totals_kernel,
        [(2, 2) + plane, (2, 2) + plane, block, (8, width)],
        [side, columns],
    )
    first = swap_first(first, "gz")
    second = swap_second(second, "gz") if count_z > 2 else first
    others = [
        swap(total, "gz", functools.partial(lambda step, i: i ^ step, step))
        for step in far_steps(count_z)
    ]
    direct = count_y == 2 and count_x in (2, 4)
    if direct:
        column_carry = swap_first(last, "gy")
        far_rows = swap(rows, "gx", lambda i: i ^ 2) if count_x == 4 else rows
    else:
        far_rows, column_carry = gathered_carries(rows, columns)
    packed, edges = call(
        pack_kernel,
        [(2, height, 2 * LANES), (2, 4, depth, width)],
        [side],
        [(2, depth * height, width)],
    )
    far = len(others)
    packed, beside, shared, far_rows = call(
        functools.partial(z_kernel, count_z, depth, far),
        [(2, height, 2 * LANES), (2, 4) + plane, block, plane],
        [first, second, total, columns, column_carry, far_rows, rows, packed, *others],
    )
    first = swap_first(packed, "gx")
    second = swap_second(packed, "gx") if count_x > 2 else first
    messages = 1 if count_y == 2 else 2
    message_rows = 4 * slot_rows(depth) + 16
    strips, flat, ext, edge_rows = call(
        functools.partial(x_kernel, counts, depth),
        [(2, height, 4 * LANES), block, (2, 4) + plane, (messages, message_rows, width)],
        [packed, first, second, far_rows, rows, shared, beside, edges],
    )
    first = swap_first(edge_rows[0], "gy")
    second = swap_second(edge_rows[1], "gy") if count_y > 2 else first
    grids = inner_steps(counts, side, flat, ext, strips)
    return outer_steps(counts, depth, strips, first, second, grids)


def inner_steps(counts, side, flat, ext, strips):
    _, depth, height, width = side.shape
    grid = (depth + 4, height + 2 * PAD, width)
    return call(
        functools.partial(inner_kernel, counts),
        [(2,) + grid, (3,) + grid, (3,) + grid, (3, depth, height, width)],
        [side, flat, ext, strips],
        [
            (4, 2, height + 2 * PAD, LANES),
            (2, height + 2 * PAD, 4 * LANES),
            (3, depth, height - 16, width),
            pltpu.SemaphoreType.DMA((6, 4)),
        ],
        far_out=1,
    )


def outer_steps(counts, depth, strips, first, second, grids):
    height, width = strips.shape[1], first.shape[1]
    result = call(
        functools.partial(outer_kernel, counts, depth),
        [grid.shape for grid in grids],
        [strips, first, second, *grids],
        [
            (4, 2, height + 2 * PAD, LANES),
            (2, height + 2 * PAD, 4 * LANES),
            (3, depth, 16, width),
            pltpu.SemaphoreType.DMA((6, 4)),
        ],
        far_out=1,
        far_in=(6,),
        aliases={3 + k: k for k in range(4)},
    )
    return result[3]


def solution(mesh):
    return jax.shard_map(
        local,
        mesh=mesh,
        in_specs=(P(None, "gz", "gy", "gx"), P("gy", "gx")),
        out_specs=P(None, "gz", "gy", "gx"),
        check_vma=False,
    )
```

```python
import functools

import jax
import jax.numpy as jnp
from jax import lax
from jax.experimental import pallas as pl
from jax.experimental.pallas import tpu as pltpu
from jax.sharding import PartitionSpec as P

spacing = 0.0625
friction = 0.004
gain = friction / (spacing * spacing)
LANES = 128
PAD = 8
GROUP = LANES // 4
AXES = ("gz", "gy", "gx")
LONG = pl.CostEstimate(flops=10**10, bytes_accessed=10**5, transcendentals=0)


def near(index, count):
    return (index + 1) % count if index % 2 else (index - 1) % count


def swap(part, axis, partner):
    count = lax.axis_size(axis)
    return lax.ppermute(part, axis, [(i, partner(i)) for i in range(count)])


def swap_first(part, axis):
    return swap(part, axis, lambda i: i ^ 1)


def swap_second(part, axis):
    count = lax.axis_size(axis)
    return swap(part, axis, lambda i: near(i, count))


def far_steps(count):
    return [2] if count == 4 else list(range(2, count))


def lane_index(shape):
    return lax.broadcasted_iota(jnp.int32, shape, len(shape) - 1)


def row_index(shape):
    return lax.broadcasted_iota(jnp.int32, shape, len(shape) - 2)


def columns_at(values, slot):
    first = 4 * (slot % GROUP)
    rolled = pltpu.roll(values, (first + 2) % LANES, 1)
    lane = lane_index(values.shape)
    return jnp.where((lane >= first) & (lane < first + 4), rolled, 0.0)


def spread(values, first):
    lane = lane_index(values.shape)
    moved = pltpu.roll(values, (LANES - first) % LANES, 1) if first else values
    alone = jnp.where(lane < 4, moved, 0.0)
    four = (alone + pltpu.roll(alone, 4, 1)) + (pltpu.roll(alone, 8, 1) + pltpu.roll(alone, 12, 1))
    parts = [four] + [pltpu.roll(four, step, 1) for step in range(16, LANES, 16)]
    while len(parts) > 1:
        parts = [a + b for a, b in zip(parts[::2], parts[1::2])]
    return parts[0]


def place():
    return [lax.axis_index(axis) for axis in AXES]


def token_kernel(out):
    out[...] = jnp.zeros_like(out)


def plane_kernel(mag, rows_out, columns_out):
    rows = columns = mag[...]
    lane, row = lane_index(rows.shape), row_index(rows.shape)
    step = 1
    while step < LANES:
        rows = rows + jnp.where(lane >= step, pltpu.roll(rows, step, 1), 0.0)
        step *= 2
    rows_out[...] = rows
    step = 1
    while step < columns.shape[0]:
        columns = columns + jnp.where(row >= step, pltpu.roll(columns, step, 0), 0.0)
        step *= 2
    columns_out[...] = columns


def totals_kernel(side, columns, first_out, second_out, total_out, last_out):
    depth = side.shape[1]
    z, _, _ = place()
    odd = z % 2 == 1
    upward = odd | (z == 0)
    for c in range(2):
        low0 = side[c, 0]
        low1 = low0 + side[c, 1]
        before = low1
        for layer in range(2, depth - 1):
            before = before + side[c, layer]
        total = before + side[c, depth - 1]
        first_out[c, 0] = jnp.where(odd, low0, before)
        first_out[c, 1] = jnp.where(odd, low1, total)
        second_out[c, 0] = jnp.where(upward, before, low0)
        second_out[c, 1] = jnp.where(upward, total, low1)
        total_out[c] = total
    last_out[...] = columns[pl.ds(columns.shape[0] - 8, 8), :]


def pack_kernel(side, packed_out, rows_out, running):
    depth, height = side.shape[1], side.shape[2]
    for c in range(2):
        total = jnp.zeros(side.shape[2:], jnp.float32)
        packed = [jnp.zeros(side.shape[2:], jnp.float32) for _ in range(2)]
        for layer in range(depth):
            total = total + side[c, layer]
            running[c, pl.ds(layer * height, height), :] = total
            slot = layer + 2
            packed[slot // GROUP] += columns_at(total, slot)
        for tile in range(2):
            packed_out[c, :, pl.ds(tile * LANES, LANES)] = packed[tile]
        for k, row in enumerate((0, 1, height - 2, height - 1)):
            rows_out[c, k] = running[c, pl.ds(row, depth, stride=height), :]


def z_kernel(
    count, depth, far, first, second, total, columns, column_carry, far_rows, rows, packed, *rest
):
    others, (x_out, ext_out, flat_out, far_out) = rest[:far], rest[far:]
    far_out[...] = far_rows[...]
    z, y, _ = place()
    odd = z % 2 == 1
    for c in range(2):
        near_a, near_b = (first[c, 0], first[c, 1]), (second[c, 0], second[c, 1])
        low = [jnp.where(odd, a, b) for a, b in zip(near_a, near_b)]
        high = [jnp.where(odd, b, a) for a, b in zip(near_a, near_b)]
        carry = jnp.where(odd, near_a[1], 0.0)
        if count == 4:
            carry = carry + jnp.where((z == 2) | (z == 3), near_b[1], 0.0)
        for step, other in zip(far_steps(count), others):
            carry = carry + jnp.where((z ^ step) < z, other[c], 0.0)
        if c == 0:
            shared = 0.5 * rows[...] - carry
        else:
            before = jnp.where(y > 0, column_carry[7:8, :], 0.0)
            shared = carry - 0.5 * (columns[...] + before)
        layers = (low[0] - low[1], None, total[c] + high[0], total[c] + high[1])
        flat_out[c] = shared
        for k in (0, 2, 3):
            ext_out[c, k] = layers[k]
        ext_out[c, 1] = jnp.zeros_like(carry)
        for tile in range(2):
            values = packed[c, :, pl.ds(tile * LANES, LANES)]
            slots = [(0, layers[0]), (depth + 2, layers[2]), (depth + 3, layers[3])]
            for at, layer in slots + [(depth + 4, shared), (depth + 5, rows[...])]:
                if at // GROUP == tile:
                    values = values + columns_at(layer, at)
            x_out[c, :, pl.ds(tile * LANES, LANES)] = values


def x_kernel(
    counts, depth, packed, first, second, far_rows, rows, shared, beside, edges,
    strips_out, flat_out, ext_out, y_out,
):
    count_z, count_y, count_x = counts
    height = packed.shape[1]
    z, y, x = place()
    odd = x % 2 == 1
    base_tile, base_lane = (depth + 4) // GROUP, 4 * ((depth + 4) % GROUP)
    rows_tile, rows_lane = (depth + 5) // GROUP, 4 * ((depth + 5) % GROUP)

    def tile_of(ref, c, tile):
        return ref[c, :, pl.ds(tile * LANES, LANES)]

    def row_totals(ref):
        return tile_of(ref, 0, rows_tile)[:, rows_lane + 1 : rows_lane + 2]

    own_total = rows[...][:, LANES - 1 :]
    total_a, total_b = row_totals(first), row_totals(second)
    far_total = far_rows[...][:, LANES - 1 :]
    if count_x == 2:
        row_carry = jnp.where(odd, total_a, 0.0)
    elif count_x == 4:
        row_carry = jnp.where(odd, total_a, 0.0) + jnp.where(x >= 2, total_b + far_total, 0.0)
    else:
        row_carry = far_total
    left_total = jnp.where(odd, total_a, total_b)

    lane = lane_index((height, LANES))
    q = lane % 4
    for part in range(2):
        merged = []
        for c in range(2):
            tiles = []
            for tile in range(2):
                own, a, b = (tile_of(ref, c, tile) for ref in (packed, first, second))
                if part == 0:
                    tiles.append(jnp.where(q < 2, jnp.where(odd, a, b), own))
                else:
                    tiles.append(jnp.where(q < 2, own, jnp.where(odd, b, a)))
            merged.append(tiles)
        if part == 0:
            carry = jnp.where(q < 2, row_carry - left_total, row_carry)
        else:
            carry = jnp.where(q < 2, row_carry, row_carry + own_total)
        base_y = spread(merged[0][base_tile], base_lane) + 0.5 * carry
        base_x = spread(merged[1][base_tile], base_lane)
        for tile in range(2):
            slot = lane // 4 + tile * GROUP
            inside = (slot < depth + 4) & ((slot >= 2) | (z > 0))
            inside = inside & ((slot < depth + 2) | (z < count_z - 1))
            if part == 0:
                inside = inside & ((q >= 2) | (x > 0))
            else:
                inside = inside & ((q < 2) | (x < count_x - 1))
            place_at = pl.ds((part * 2 + tile) * LANES, LANES)
            strips_out[0, :, place_at] = jnp.where(inside, base_x + merged[1][tile], 0.0)
            strips_out[1, :, place_at] = jnp.where(inside, base_y - merged[0][tile], 0.0)

    flat_x = shared[1]
    flat_y = shared[0] + 0.5 * row_carry
    flat_out[0] = flat_x
    flat_out[1] = flat_y
    for k in range(4):
        inside = (z > 0) if k < 2 else (z < count_z - 1)
        ext_out[0, k] = jnp.where(inside, flat_x + beside[1, k], 0.0)
        ext_out[1, k] = jnp.where(inside, flat_y - beside[0, k], 0.0)

    slots = slot_rows(depth)
    for message in range(y_out.shape[0]):
        downward = (y % 2 == 1) if message == 0 else (y % 2 == 0)
        for c in range(2):
            for r in range(2):
                start = (c * 2 + r) * slots
                low, high = pl.ds(r, 1), pl.ds(height - 2 + r, 1)
                flat = jnp.where(downward, flat_out[c, low, :], flat_out[c, high, :])
                edge = jnp.where(downward, edges[1 - c, r], edges[1 - c, 2 + r])
                edge = edge if c == 0 else -edge
                y_out[message, pl.ds(start + 2, depth), :] = flat + edge
                for k, at in enumerate((0, 1, depth + 2, depth + 3)):
                    y_out[message, pl.ds(start + at, 1), :] = jnp.where(
                        downward, ext_out[c, k, low, :], ext_out[c, k, high, :]
                    )
            for tile in range(4):
                start = 4 * slots + (c * 4 + tile) * 2
                lanes = pl.ds(tile * LANES, LANES)
                y_out[message, pl.ds(start, 2), :] = jnp.where(
                    downward,
                    strips_out[c, pl.ds(0, 2), lanes],
                    strips_out[c, pl.ds(height - 2, 2), lanes],
                )


def slot_rows(depth):
    return (depth + 4 + 7) // 8 * 8


def following(values, axis, step=1):
    return pltpu.roll(values, values.shape[axis] - step, axis)


def preceding(values, axis, step=1):
    return pltpu.roll(values, step, axis)


def push(a, field, current):
    square = field[0] * field[0] + field[1] * field[1] + field[2] * field[2]
    along = current[0] * field[0] + current[1] * field[1] + current[2] * field[2]
    factor = gain / (square + 1.0)
    p, q = along * factor, square * factor
    return [a[c] + (field[c] * p - current[c] * q) for c in range(3)]


def strip_field(a):
    x, y, z = a
    field_x = following(z, 0) - z - (following(y, 1, 4) - y)
    field_y = following(x, 1, 4) - x - (following(z, 1) - z)
    field_z = following(y, 1) - y - (following(x, 0) - x)
    return field_x, field_y, field_z


def strip_current(b):
    x, y, z = b
    current_x = z - preceding(z, 0) - (y - preceding(y, 1, 4))
    current_y = x - preceding(x, 1, 4) - (z - preceding(z, 1))
    current_z = y - preceding(y, 1) - (x - preceding(x, 0))
    return current_x, current_y, current_z


class Stepper:
    def __init__(self, counts, state, field, later, halo, depth, height):
        self.counts = counts
        self.z, self.y, self.x = place()
        self.state, self.field, self.later, self.halo = state, field, later, halo
        self.depth, self.height = depth, height
        self.padded = state.shape[2]
        lane = lane_index((8, LANES))
        self.last, self.start = lane == LANES - 1, lane == 0

    def load(self, ref, c, layer, row):
        return ref[c, layer, pl.ds(row, 8), :]

    def strips(self, wide):
        depth, height = self.depth, self.height
        count_z, count_y, count_x = self.counts
        half = 2 * LANES
        shape = (self.padded, 2 * half)
        lane, row = lane_index(shape), row_index(shape)
        q = lane % 4
        slot = (lane % half) // 4
        right = lane >= half
        inside = (row >= PAD - 2) & (row < PAD + height + 2) & (slot < depth + 4)
        inside = inside & ((row >= PAD) | (self.y > 0))
        inside = inside & ((row < PAD + height) | (self.y < count_y - 1))
        inside = inside & ((slot >= 2) | (self.z > 0))
        inside = inside & ((slot < depth + 2) | (self.z < count_z - 1))
        inside = inside & (right | (q >= 2) | (self.x > 0))
        inside = inside & (~right | (q < 2) | (self.x < count_x - 1))
        a = [jnp.where(inside, wide[c], 0.0) for c in range(2)]
        a.append(jnp.zeros_like(a[0]))
        b = strip_field(a)
        pick = (lane_index((self.padded, half)) % 4) == 2

        def keep(at, upper, lower):
            value = jnp.where(pick, upper[:, half:], lower[:, :half])
            self.halo[at, 0] = value[:, :LANES]
            self.halo[at, 1] = value[:, LANES:]

        keep(0, a[1], b[1])
        keep(1, a[2], b[2])
        a = [jnp.where(inside, value, 0.0) for value in push(a, b, strip_current(b))]
        b = strip_field(a)
        keep(2, a[1], b[1])
        keep(3, a[2], b[2])

    def beside(self, at, layer, row):
        shift = LANES - 2 - 4 * (layer % GROUP)
        return pltpu.roll(self.halo[at, layer // GROUP, pl.ds(row, 8), :], shift, 1)

    def right_of(self, value, edge):
        return following(jnp.where(self.start, edge, value), 1)

    def left_of(self, value, edge):
        return preceding(jnp.where(self.last, edge, value), 1)

    def first_field(self, layer, r):
        load, state = self.load, self.state
        ax, ay = load(state, 0, layer, r), load(state, 1, layer, r)
        ay_right = self.right_of(ay, self.beside(0, layer, r))
        to = pl.ds(r, 8)
        self.field[0, layer, to, :] = ay - load(state, 1, layer + 1, r)
        self.field[1, layer, to, :] = load(state, 0, layer + 1, r) - ax
        self.field[2, layer, to, :] = ay_right - ay - (load(state, 0, layer, r + 1) - ax)

    def currents(self, layer, r, at):
        load, field = self.load, self.field
        bx, by, bz = (load(field, c, layer, r) for c in range(3))
        by_left = self.left_of(by, self.beside(at, layer, r))
        bz_left = self.left_of(bz, self.beside(at + 1, layer, r))
        jx = bz - load(field, 2, layer, r - 1) - (by - load(field, 1, layer - 1, r))
        jy = bx - load(field, 0, layer - 1, r) - (bz - bz_left)
        jz = by - by_left - (bx - load(field, 0, layer, r - 1))
        return (bx, by, bz), (jx, jy, jz)

    def first_push(self, layer, r):
        b, j = self.currents(layer, r, 0)
        a = [self.load(self.state, c, layer, r) for c in range(2)]
        a.append(jnp.zeros_like(a[0]))
        for c, value in enumerate(push(a, b, j)):
            self.later[c, layer, pl.ds(r, 8), :] = value

    def second_field(self, layer, r):
        load, later = self.load, self.later
        ax, ay, az = (load(later, c, layer, r) for c in range(3))
        ay_right = self.right_of(ay, self.beside(2, layer, r))
        az_right = self.right_of(az, self.beside(3, layer, r))
        to = pl.ds(r, 8)
        self.field[0, layer, to, :] = (
            load(later, 2, layer, r + 1) - az - (load(later, 1, layer + 1, r) - ay)
        )
        self.field[1, layer, to, :] = load(later, 0, layer + 1, r) - ax - (az_right - az)
        self.field[2, layer, to, :] = ay_right - ay - (load(later, 0, layer, r + 1) - ax)

    def second_push(self, layer, r):
        b, j = self.currents(layer, r, 2)
        a = [self.load(self.later, c, layer, r) for c in range(3)]
        return [spacing * value for value in push(a, b, j)]

    def clear(self, rows):
        depth, height = self.depth, self.height
        count_z, count_y, _ = self.counts
        zeros = jnp.zeros((height + 8, LANES), jnp.float32)
        line = jnp.zeros((depth + 4, LANES), jnp.float32)
        for exists, layer in ((self.z > 0, 1), (self.z < count_z - 1, depth + 2)):

            @pl.when(jnp.logical_not(exists))
            def _():
                for c in range(3):
                    self.later[c, layer, pl.ds(PAD - 1, height + 8), :] = zeros

        if not rows:
            return
        for exists, row in ((self.y > 0, PAD - 1), (self.y < count_y - 1, PAD + height)):

            @pl.when(jnp.logical_not(exists))
            def _():
                for c in range(3):
                    flat_later = self.later.at[c].reshape((depth + 4) * self.padded, LANES)
                    flat_later[pl.ds(row, depth + 4, stride=self.padded), :] = line

    def run(self, tiles, rows, out, block, sems):
        depth = self.depth
        for layer in range(depth + 3):
            for r in tiles[0]:
                self.first_field(layer, r)
        for layer in range(1, depth + 3):
            for r in tiles[1]:
                self.first_push(layer, r)
        self.clear(rows)
        for layer in range(1, depth + 2):
            for r in tiles[2]:
                self.second_field(layer, r)
        for layer in range(depth):
            for k, r in enumerate(tiles[3]):
                for c, value in enumerate(self.second_push(layer + 2, r)):
                    block[c, layer, pl.ds(8 * k, 8), :] = value
        copies = []
        k = 0
        while k < len(tiles[3]):
            run = 1
            while k + run < len(tiles[3]) and tiles[3][k + run] == tiles[3][k] + 8 * run:
                run += 1
            copies.append(
                pltpu.make_async_copy(
                    block.at[:, :, pl.ds(8 * k, 8 * run), :],
                    out.at[:, :, pl.ds(tiles[3][k] - PAD, 8 * run), :],
                    sems.at[len(copies)],
                )
            )
            copies[-1].start()
            k += run
        for copy in copies:
            copy.wait()


def inner_tiles(height):
    whole = [PAD + r for r in range(0, height, 8)]
    inner = whole[1:-1]
    return whole, whole, [r - 1 for r in inner] + [inner[-1]], inner


def outer_tiles(height):
    top = PAD + height - 8
    return (PAD - 2, top + 1), (PAD - 1, top + 1), (PAD - 1, top), (PAD, top)


def inner_kernel(
    counts, side, flat, ext, strips, state, field, later, out, halo, wide, block, sems
):
    depth, height = side.shape[1], side.shape[2]
    rows = pl.ds(PAD, height)
    for c in range(2):
        for k, at in enumerate((0, 1, depth + 2, depth + 3)):
            state[c, at, rows, :] = ext[c, k]
    sums = [jnp.zeros((height, LANES), jnp.float32) for _ in range(2)]
    for layer in range(depth):
        sums = [total + side[c, layer] for c, total in enumerate(sums)]
        state[0, layer + 2, rows, :] = flat[0] + sums[1]
        state[1, layer + 2, rows, :] = flat[1] - sums[0]
    for c in range(2):
        wide[c, rows, :] = strips[c]
        wide[c, pl.ds(0, PAD), :] = jnp.zeros((PAD, wide.shape[2]), jnp.float32)
        wide[c, pl.ds(PAD + height, PAD), :] = jnp.zeros((PAD, wide.shape[2]), jnp.float32)
    stepper = Stepper(counts, state, field, later, halo, depth, height)
    stepper.strips(wide)
    stepper.run(inner_tiles(height), False, out, block, sems)


def outer_kernel(
    counts, depth, strips, first, second, _s, _f, _l, _o,
    state, field, later, out, halo, wide, block, sems,
):
    _, count_y, _ = counts
    height, padded = strips.shape[1], state.shape[2]
    _, y, _ = place()
    slots = slot_rows(depth)
    layers = depth + 4
    odd = y % 2 == 1
    for low in (True, False):
        exists = (y > 0) if low else (y < count_y - 1)
        row = PAD - 2 if low else PAD + height

        def received(take):
            a, b = first[take, :], second[take, :]
            value = jnp.where(odd, a, b) if low else jnp.where(odd, b, a)
            return jnp.where(exists, value, 0.0)

        for c in range(2):
            flat_state = state.at[c].reshape(layers * padded, LANES)
            for r in range(2):
                flat_state[pl.ds(row + r, layers, stride=padded), :] = received(
                    pl.ds((c * 2 + r) * slots, layers)
                )
            for tile in range(4):
                wide[c, pl.ds(row, 2), pl.ds(tile * LANES, LANES)] = received(
                    pl.ds(4 * slots + (c * 4 + tile) * 2, 2)
                )
    for c in range(2):
        wide[c, pl.ds(PAD, height), :] = strips[c]
    stepper = Stepper(counts, state, field, later, halo, depth, height)
    stepper.strips(wide)
    stepper.run(outer_tiles(height), True, out, block, sems)


def call(kernel, shapes, args, scratch=(), limit=16, far_out=0, far_in=(), aliases={}, cost=None):
    vmem, far = pl.BlockSpec(memory_space=pltpu.VMEM), pl.BlockSpec(memory_space=pltpu.HBM)
    specs = [far if k in far_in else vmem for k in range(len(args))]
    return pl.pallas_call(
        kernel,
        out_shape=[jax.ShapeDtypeStruct(shape, jnp.float32) for shape in shapes],
        in_specs=specs,
        out_specs=[vmem] * (len(shapes) - far_out) + [far] * far_out,
        scratch_shapes=[
            pltpu.VMEM(shape, jnp.float32) if isinstance(shape, tuple) else shape
            for shape in scratch
        ],
        input_output_aliases=aliases,
        cost_estimate=cost,
        compiler_params=pltpu.CompilerParams(vmem_limit_bytes=int(limit * 2**20)),
    )(*args)


def gathered_carries(rows, columns):
    height, width = rows.shape
    x, y = lax.axis_index("gx"), lax.axis_index("gy")
    row_totals = lax.all_gather(rows[:, -1], "gx")
    before = (jnp.arange(row_totals.shape[0]) < x)[:, None]
    row_carry = jnp.sum(jnp.where(before, row_totals, 0.0), axis=0)
    column_totals = lax.all_gather(columns[-1], "gy")
    before = (jnp.arange(column_totals.shape[0]) < y)[:, None]
    column_carry = jnp.sum(jnp.where(before, column_totals, 0.0), axis=0)
    return (
        jnp.broadcast_to(row_carry[:, None], (height, width)),
        jnp.broadcast_to(column_carry[None], (8, width)),
    )


def local(side, mag):
    counts = tuple(lax.axis_size(axis) for axis in ("gz", "gy", "gx"))
    count_z, count_y, count_x = counts
    _, depth, height, width = side.shape
    plane, block = (height, width), (2, height, width)
    (token,) = call(token_kernel, [(8, LANES)], [], cost=LONG)
    rows, columns = call(
        lambda _, *refs: plane_kernel(*refs), [plane, plane], [token, mag]
    )
    first, second, total, last = call(
        totals_kernel,
        [(2, 2) + plane, (2, 2) + plane, block, (8, width)],
        [side, columns],
    )
    first = swap_first(first, "gz")
    second = swap_second(second, "gz") if count_z > 2 else first
    others = [
        swap(total, "gz", functools.partial(lambda step, i: i ^ step, step))
        for step in far_steps(count_z)
    ]
    direct = count_y == 2 and count_x in (2, 4)
    if direct:
        column_carry = swap_first(last, "gy")
        far_rows = swap(rows, "gx", lambda i: i ^ 2) if count_x == 4 else rows
    else:
        far_rows, column_carry = gathered_carries(rows, columns)
    packed, edges = call(
        pack_kernel,
        [(2, height, 2 * LANES), (2, 4, depth, width)],
        [side],
        [(2, depth * height, width)],
    )
    far = len(others)
    packed, beside, shared, far_rows = call(
        functools.partial(z_kernel, count_z, depth, far),
        [(2, height, 2 * LANES), (2, 4) + plane, block, plane],
        [first, second, total, columns, column_carry, far_rows, rows, packed, *others],
    )
    first = swap_first(packed, "gx")
    second = swap_second(packed, "gx") if count_x > 2 else first
    messages = 1 if count_y == 2 else 2
    message_rows = 4 * slot_rows(depth) + 16
    strips, flat, ext, edge_rows = call(
        functools.partial(x_kernel, counts, depth),
        [(2, height, 4 * LANES), block, (2, 4) + plane, (messages, message_rows, width)],
        [packed, first, second, far_rows, rows, shared, beside, edges],
    )
    first = swap_first(edge_rows[0], "gy")
    second = swap_second(edge_rows[1], "gy") if count_y > 2 else first
    grids = inner_steps(counts, side, flat, ext, strips)
    return outer_steps(counts, depth, strips, first, second, grids)


def inner_steps(counts, side, flat, ext, strips):
    _, depth, height, width = side.shape
    grid = (depth + 4, height + 2 * PAD, width)
    return call(
        functools.partial(inner_kernel, counts),
        [(2,) + grid, (3,) + grid, (3,) + grid, (3, depth, height, width)],
        [side, flat, ext, strips],
        [
            (4, 2, height + 2 * PAD, LANES),
            (2, height + 2 * PAD, 4 * LANES),
            (3, depth, height - 16, width),
            pltpu.SemaphoreType.DMA((height // 8,)),
        ],
        far_out=1,
    )


def outer_steps(counts, depth, strips, first, second, grids):
    height, width = strips.shape[1], first.shape[1]
    result = call(
        functools.partial(outer_kernel, counts, depth),
        [grid.shape for grid in grids],
        [strips, first, second, *grids],
        [
            (4, 2, height + 2 * PAD, LANES),
            (2, height + 2 * PAD, 4 * LANES),
            (3, depth, 16, width),
            pltpu.SemaphoreType.DMA((height // 8,)),
        ],
        far_out=1,
        far_in=(6,),
        aliases={3 + k: k for k in range(4)},
    )
    return result[3]


def solution(mesh):
    return jax.shard_map(
        local,
        mesh=mesh,
        in_specs=(P(None, "gz", "gy", "gx"), P("gy", "gx")),
        out_specs=P(None, "gz", "gy", "gx"),
        check_vma=False,
    )
```

```python
import functools

import jax
import jax.numpy as jnp
from jax import lax
from jax.experimental import pallas as pl
from jax.experimental.pallas import tpu as pltpu
from jax.sharding import PartitionSpec as P

spacing = 0.0625
friction = 0.004
gain = friction / (spacing * spacing)
LANES = 128
PAD = 8
GROUP = LANES // 4
AXES = ("gz", "gy", "gx")
LONG = pl.CostEstimate(flops=10**10, bytes_accessed=10**5, transcendentals=0)


def near(index, count):
    return (index + 1) % count if index % 2 else (index - 1) % count


def swap(part, axis, partner):
    count = lax.axis_size(axis)
    return lax.ppermute(part, axis, [(i, partner(i)) for i in range(count)])


def swap_first(part, axis):
    return swap(part, axis, lambda i: i ^ 1)


def swap_second(part, axis):
    count = lax.axis_size(axis)
    return swap(part, axis, lambda i: near(i, count))


def far_steps(count):
    return [2] if count == 4 else list(range(2, count))


def lane_index(shape):
    return lax.broadcasted_iota(jnp.int32, shape, len(shape) - 1)


def row_index(shape):
    return lax.broadcasted_iota(jnp.int32, shape, len(shape) - 2)


def columns_at(values, slot):
    first = 4 * (slot % GROUP)
    rolled = pltpu.roll(values, (first + 2) % LANES, 1)
    lane = lane_index(values.shape)
    return jnp.where((lane >= first) & (lane < first + 4), rolled, 0.0)


def spread(values, first):
    lane = lane_index(values.shape)
    moved = pltpu.roll(values, (LANES - first) % LANES, 1) if first else values
    alone = jnp.where(lane < 4, moved, 0.0)
    four = (alone + pltpu.roll(alone, 4, 1)) + (pltpu.roll(alone, 8, 1) + pltpu.roll(alone, 12, 1))
    parts = [four] + [pltpu.roll(four, step, 1) for step in range(16, LANES, 16)]
    while len(parts) > 1:
        parts = [a + b for a, b in zip(parts[::2], parts[1::2])]
    return parts[0]


def place():
    return [lax.axis_index(axis) for axis in AXES]


def token_kernel(out):
    out[...] = jnp.zeros_like(out)


def plane_kernel(mag, rows_out, columns_out):
    rows = columns = mag[...]
    lane, row = lane_index(rows.shape), row_index(rows.shape)
    step = 1
    while step < LANES:
        rows = rows + jnp.where(lane >= step, pltpu.roll(rows, step, 1), 0.0)
        step *= 2
    rows_out[...] = rows
    step = 1
    while step < columns.shape[0]:
        columns = columns + jnp.where(row >= step, pltpu.roll(columns, step, 0), 0.0)
        step *= 2
    columns_out[...] = columns


def totals_kernel(side, columns, first_out, second_out, total_out, last_out):
    depth = side.shape[1]
    z, _, _ = place()
    odd = z % 2 == 1
    upward = odd | (z == 0)
    for c in range(2):
        low0 = side[c, 0]
        low1 = low0 + side[c, 1]
        before = low1
        for layer in range(2, depth - 1):
            before = before + side[c, layer]
        total = before + side[c, depth - 1]
        first_out[c, 0] = jnp.where(odd, low0, before)
        first_out[c, 1] = jnp.where(odd, low1, total)
        second_out[c, 0] = jnp.where(upward, before, low0)
        second_out[c, 1] = jnp.where(upward, total, low1)
        total_out[c] = total
    last_out[...] = columns[pl.ds(columns.shape[0] - 8, 8), :]


def pack_kernel(side, packed_out, rows_out, running):
    depth, height = side.shape[1], side.shape[2]
    for c in range(2):
        total = jnp.zeros(side.shape[2:], jnp.float32)
        packed = [jnp.zeros(side.shape[2:], jnp.float32) for _ in range(2)]
        for layer in range(depth):
            total = total + side[c, layer]
            running[c, pl.ds(layer * height, height), :] = total
            slot = layer + 2
            packed[slot // GROUP] += columns_at(total, slot)
        for tile in range(2):
            packed_out[c, :, pl.ds(tile * LANES, LANES)] = packed[tile]
        for k, row in enumerate((0, 1, height - 2, height - 1)):
            rows_out[c, k] = running[c, pl.ds(row, depth, stride=height), :]


def z_kernel(
    count, depth, far, first, second, total, columns, column_carry, far_rows, rows, packed, *rest
):
    others, (x_out, ext_out, flat_out, far_out) = rest[:far], rest[far:]
    far_out[...] = far_rows[...]
    z, y, _ = place()
    odd = z % 2 == 1
    for c in range(2):
        near_a, near_b = (first[c, 0], first[c, 1]), (second[c, 0], second[c, 1])
        low = [jnp.where(odd, a, b) for a, b in zip(near_a, near_b)]
        high = [jnp.where(odd, b, a) for a, b in zip(near_a, near_b)]
        carry = jnp.where(odd, near_a[1], 0.0)
        if count == 4:
            carry = carry + jnp.where((z == 2) | (z == 3), near_b[1], 0.0)
        for step, other in zip(far_steps(count), others):
            carry = carry + jnp.where((z ^ step) < z, other[c], 0.0)
        if c == 0:
            shared = 0.5 * rows[...] - carry
        else:
            before = jnp.where(y > 0, column_carry[...][7:8, :], 0.0)
            shared = carry - 0.5 * (columns[...] + before)
        layers = (low[0] - low[1], None, total[c] + high[0], total[c] + high[1])
        flat_out[c] = shared
        for k in (0, 2, 3):
            ext_out[c, k] = layers[k]
        ext_out[c, 1] = jnp.zeros_like(carry)
        for tile in range(2):
            values = packed[c, :, pl.ds(tile * LANES, LANES)]
            slots = [(0, layers[0]), (depth + 2, layers[2]), (depth + 3, layers[3])]
            for at, layer in slots + [(depth + 4, shared), (depth + 5, rows[...])]:
                if at // GROUP == tile:
                    values = values + columns_at(layer, at)
            x_out[c, :, pl.ds(tile * LANES, LANES)] = values


def x_kernel(
    counts, depth, packed, first, second, far_rows, rows, shared, beside, edges,
    strips_out, flat_out, ext_out, y_out,
):
    count_z, count_y, count_x = counts
    height = packed.shape[1]
    z, y, x = place()
    odd = x % 2 == 1
    base_tile, base_lane = (depth + 4) // GROUP, 4 * ((depth + 4) % GROUP)
    rows_tile, rows_lane = (depth + 5) // GROUP, 4 * ((depth + 5) % GROUP)

    def tile_of(ref, c, tile):
        return ref[c, :, pl.ds(tile * LANES, LANES)]

    def row_totals(ref):
        return tile_of(ref, 0, rows_tile)[:, rows_lane + 1 : rows_lane + 2]

    own_total = rows[...][:, LANES - 1 :]
    total_a, total_b = row_totals(first), row_totals(second)
    far_total = far_rows[...][:, LANES - 1 :]
    if count_x == 2:
        row_carry = jnp.where(odd, total_a, 0.0)
    elif count_x == 4:
        row_carry = jnp.where(odd, total_a, 0.0) + jnp.where(x >= 2, total_b + far_total, 0.0)
    else:
        row_carry = far_total
    left_total = jnp.where(odd, total_a, total_b)

    lane = lane_index((height, LANES))
    q = lane % 4
    for part in range(2):
        merged = []
        for c in range(2):
            tiles = []
            for tile in range(2):
                own, a, b = (tile_of(ref, c, tile) for ref in (packed, first, second))
                if part == 0:
                    tiles.append(jnp.where(q < 2, jnp.where(odd, a, b), own))
                else:
                    tiles.append(jnp.where(q < 2, own, jnp.where(odd, b, a)))
            merged.append(tiles)
        if part == 0:
            carry = jnp.where(q < 2, row_carry - left_total, row_carry)
        else:
            carry = jnp.where(q < 2, row_carry, row_carry + own_total)
        base_y = spread(merged[0][base_tile], base_lane) + 0.5 * carry
        base_x = spread(merged[1][base_tile], base_lane)
        for tile in range(2):
            slot = lane // 4 + tile * GROUP
            inside = (slot < depth + 4) & ((slot >= 2) | (z > 0))
            inside = inside & ((slot < depth + 2) | (z < count_z - 1))
            if part == 0:
                inside = inside & ((q >= 2) | (x > 0))
            else:
                inside = inside & ((q < 2) | (x < count_x - 1))
            place_at = pl.ds((part * 2 + tile) * LANES, LANES)
            strips_out[0, :, place_at] = jnp.where(inside, base_x + merged[1][tile], 0.0)
            strips_out[1, :, place_at] = jnp.where(inside, base_y - merged[0][tile], 0.0)

    flat_x = shared[1]
    flat_y = shared[0] + 0.5 * row_carry
    flat_out[0] = flat_x
    flat_out[1] = flat_y
    for k in range(4):
        inside = (z > 0) if k < 2 else (z < count_z - 1)
        ext_out[0, k] = jnp.where(inside, flat_x + beside[1, k], 0.0)
        ext_out[1, k] = jnp.where(inside, flat_y - beside[0, k], 0.0)

    slots = slot_rows(depth)
    for message in range(y_out.shape[0]):
        downward = (y % 2 == 1) if message == 0 else (y % 2 == 0)

        def edge_row(values, r):
            return jnp.where(downward, values[r : r + 1], values[height - 2 + r : height - 1 + r])

        for c in range(2):
            for r in range(2):
                start = (c * 2 + r) * slots
                flat = edge_row(flat_out[c], r)
                edge = jnp.where(downward, edges[1 - c, r], edges[1 - c, 2 + r])
                edge = edge if c == 0 else -edge
                y_out[message, pl.ds(start + 2, depth), :] = flat + edge
                for k, at in enumerate((0, 1, depth + 2, depth + 3)):
                    y_out[message, pl.ds(start + at, 1), :] = edge_row(ext_out[c, k], r)
            for tile in range(4):
                start = 4 * slots + (c * 4 + tile) * 2
                lanes = pl.ds(tile * LANES, LANES)
                y_out[message, pl.ds(start, 2), :] = jnp.where(
                    downward,
                    strips_out[c, pl.ds(0, 8), lanes][:2],
                    strips_out[c, pl.ds(height - 8, 8), lanes][6:],
                )


def slot_rows(depth):
    return (depth + 4 + 7) // 8 * 8


def following(values, axis, step=1):
    return pltpu.roll(values, values.shape[axis] - step, axis)


def preceding(values, axis, step=1):
    return pltpu.roll(values, step, axis)


def push(a, field, current):
    square = field[0] * field[0] + field[1] * field[1] + field[2] * field[2]
    along = current[0] * field[0] + current[1] * field[1] + current[2] * field[2]
    factor = gain / (square + 1.0)
    p, q = along * factor, square * factor
    return [a[c] + (field[c] * p - current[c] * q) for c in range(3)]


def strip_field(a):
    x, y, z = a
    field_x = following(z, 0) - z - (following(y, 1, 4) - y)
    field_y = following(x, 1, 4) - x - (following(z, 1) - z)
    field_z = following(y, 1) - y - (following(x, 0) - x)
    return field_x, field_y, field_z


def strip_current(b):
    x, y, z = b
    current_x = z - preceding(z, 0) - (y - preceding(y, 1, 4))
    current_y = x - preceding(x, 1, 4) - (z - preceding(z, 1))
    current_z = y - preceding(y, 1) - (x - preceding(x, 0))
    return current_x, current_y, current_z


class Stepper:
    def __init__(self, counts, state, field, later, halo, depth, height):
        self.counts = counts
        self.z, self.y, self.x = place()
        self.state, self.field, self.later, self.halo = state, field, later, halo
        self.depth, self.height = depth, height
        self.padded = state.shape[2]
        lane = lane_index((8, LANES))
        self.last, self.start = lane == LANES - 1, lane == 0

    def load(self, ref, c, layer, row):
        return ref[c, layer, pl.ds(row, 8), :]

    def strips(self, wide):
        depth, height = self.depth, self.height
        count_z, count_y, count_x = self.counts
        half = 2 * LANES
        shape = (self.padded, 2 * half)
        lane, row = lane_index(shape), row_index(shape)
        q = lane % 4
        slot = (lane % half) // 4
        right = lane >= half
        inside = (row >= PAD - 2) & (row < PAD + height + 2) & (slot < depth + 4)
        inside = inside & ((row >= PAD) | (self.y > 0))
        inside = inside & ((row < PAD + height) | (self.y < count_y - 1))
        inside = inside & ((slot >= 2) | (self.z > 0))
        inside = inside & ((slot < depth + 2) | (self.z < count_z - 1))
        inside = inside & (right | (q >= 2) | (self.x > 0))
        inside = inside & (~right | (q < 2) | (self.x < count_x - 1))
        a = [jnp.where(inside, wide[c], 0.0) for c in range(2)]
        a.append(jnp.zeros_like(a[0]))
        b = strip_field(a)
        pick = (lane_index((self.padded, half)) % 4) == 2

        def keep(at, upper, lower):
            value = jnp.where(pick, upper[:, half:], lower[:, :half])
            self.halo[at, 0] = value[:, :LANES]
            self.halo[at, 1] = value[:, LANES:]

        keep(0, a[1], b[1])
        keep(1, a[2], b[2])
        a = [jnp.where(inside, value, 0.0) for value in push(a, b, strip_current(b))]
        b = strip_field(a)
        keep(2, a[1], b[1])
        keep(3, a[2], b[2])

    def beside(self, at, layer, row):
        shift = LANES - 2 - 4 * (layer % GROUP)
        return pltpu.roll(self.halo[at, layer // GROUP, pl.ds(row, 8), :], shift, 1)

    def right_of(self, value, edge):
        return following(jnp.where(self.start, edge, value), 1)

    def left_of(self, value, edge):
        return preceding(jnp.where(self.last, edge, value), 1)

    def first_field(self, layer, r):
        load, state = self.load, self.state
        ax, ay = load(state, 0, layer, r), load(state, 1, layer, r)
        ay_right = self.right_of(ay, self.beside(0, layer, r))
        to = pl.ds(r, 8)
        self.field[0, layer, to, :] = ay - load(state, 1, layer + 1, r)
        self.field[1, layer, to, :] = load(state, 0, layer + 1, r) - ax
        self.field[2, layer, to, :] = ay_right - ay - (load(state, 0, layer, r + 1) - ax)

    def currents(self, layer, r, at):
        load, field = self.load, self.field
        bx, by, bz = (load(field, c, layer, r) for c in range(3))
        by_left = self.left_of(by, self.beside(at, layer, r))
        bz_left = self.left_of(bz, self.beside(at + 1, layer, r))
        jx = bz - load(field, 2, layer, r - 1) - (by - load(field, 1, layer - 1, r))
        jy = bx - load(field, 0, layer - 1, r) - (bz - bz_left)
        jz = by - by_left - (bx - load(field, 0, layer, r - 1))
        return (bx, by, bz), (jx, jy, jz)

    def first_push(self, layer, r):
        b, j = self.currents(layer, r, 0)
        a = [self.load(self.state, c, layer, r) for c in range(2)]
        a.append(jnp.zeros_like(a[0]))
        for c, value in enumerate(push(a, b, j)):
            self.later[c, layer, pl.ds(r, 8), :] = value

    def second_field(self, layer, r):
        load, later = self.load, self.later
        ax, ay, az = (load(later, c, layer, r) for c in range(3))
        ay_right = self.right_of(ay, self.beside(2, layer, r))
        az_right = self.right_of(az, self.beside(3, layer, r))
        to = pl.ds(r, 8)
        self.field[0, layer, to, :] = (
            load(later, 2, layer, r + 1) - az - (load(later, 1, layer + 1, r) - ay)
        )
        self.field[1, layer, to, :] = load(later, 0, layer + 1, r) - ax - (az_right - az)
        self.field[2, layer, to, :] = ay_right - ay - (load(later, 0, layer, r + 1) - ax)

    def second_push(self, layer, r):
        b, j = self.currents(layer, r, 2)
        a = [self.load(self.later, c, layer, r) for c in range(3)]
        return [spacing * value for value in push(a, b, j)]

    def clear(self, rows):
        depth, height = self.depth, self.height
        count_z, count_y, _ = self.counts
        zeros = jnp.zeros((height + 8, LANES), jnp.float32)
        line = jnp.zeros((depth + 4, LANES), jnp.float32)
        for exists, layer in ((self.z > 0, 1), (self.z < count_z - 1, depth + 2)):

            @pl.when(jnp.logical_not(exists))
            def _():
                for c in range(3):
                    self.later[c, layer, pl.ds(PAD - 1, height + 8), :] = zeros

        if not rows:
            return
        for exists, row in ((self.y > 0, PAD - 1), (self.y < count_y - 1, PAD + height)):

            @pl.when(jnp.logical_not(exists))
            def _():
                for c in range(3):
                    flat_later = self.later.at[c].reshape(self.later.shape[1] * self.padded, LANES)
                    flat_later[pl.ds(row, depth + 4, stride=self.padded), :] = line

    def run(self, tiles, rows, out, block, sems):
        depth = self.depth
        for layer in range(depth + 3):
            for r in tiles[0]:
                self.first_field(layer, r)
        for layer in range(1, depth + 3):
            for r in tiles[1]:
                self.first_push(layer, r)
        self.clear(rows)
        for layer in range(1, depth + 2):
            for r in tiles[2]:
                self.second_field(layer, r)
        for layer in range(depth):
            for k, r in enumerate(tiles[3]):
                for c, value in enumerate(self.second_push(layer + 2, r)):
                    block[c, layer, pl.ds(8 * k, 8), :] = value
        copies = []
        k = 0
        while k < len(tiles[3]):
            run = 1
            while k + run < len(tiles[3]) and tiles[3][k + run] == tiles[3][k] + 8 * run:
                run += 1
            copies.append(
                pltpu.make_async_copy(
                    block.at[:, :, pl.ds(8 * k, 8 * run), :],
                    out.at[:, :, pl.ds(tiles[3][k] - PAD, 8 * run), :],
                    sems.at[len(copies)],
                )
            )
            copies[-1].start()
            k += run
        for copy in copies:
            copy.wait()


def inner_tiles(height):
    whole = [PAD + r for r in range(0, height, 8)]
    inner = whole[1:-1]
    return whole, whole, [r - 1 for r in inner] + [inner[-1]], inner


def outer_tiles(height):
    top = PAD + height - 8
    return (PAD - 2, top + 1), (PAD - 1, top + 1), (PAD - 1, top), (PAD, top)


def inner_kernel(
    counts, side, flat, ext, strips, state, field, later, out, halo, wide, block, sems
):
    depth, height = side.shape[1], side.shape[2]
    rows = pl.ds(PAD, height)
    for c in range(2):
        for k, at in enumerate((0, 1, depth + 2, depth + 3)):
            state[c, at, rows, :] = ext[c, k]
    sums = [jnp.zeros((height, LANES), jnp.float32) for _ in range(2)]
    for layer in range(depth):
        sums = [total + side[c, layer] for c, total in enumerate(sums)]
        state[0, layer + 2, rows, :] = flat[0] + sums[1]
        state[1, layer + 2, rows, :] = flat[1] - sums[0]
    for c in range(2):
        wide[c, rows, :] = strips[c]
        wide[c, pl.ds(0, PAD), :] = jnp.zeros((PAD, wide.shape[2]), jnp.float32)
        wide[c, pl.ds(PAD + height, PAD), :] = jnp.zeros((PAD, wide.shape[2]), jnp.float32)
    stepper = Stepper(counts, state, field, later, halo, depth, height)
    stepper.strips(wide)
    stepper.run(inner_tiles(height), False, out, block, sems)


def outer_kernel(
    counts, depth, strips, first, second, _s, _f, _l, _o,
    state, field, later, out, halo, wide, block, sems,
):
    _, count_y, _ = counts
    height, padded = strips.shape[1], state.shape[2]
    _, y, _ = place()
    slots = slot_rows(depth)
    layers = depth + 4
    odd = y % 2 == 1
    for low in (True, False):
        exists = (y > 0) if low else (y < count_y - 1)
        row = PAD - 2 if low else PAD + height

        def received(take):
            a, b = first[take, :], second[take, :]
            value = jnp.where(odd, a, b) if low else jnp.where(odd, b, a)
            return jnp.where(exists, value, 0.0)

        for c in range(2):
            flat_state = state.at[c].reshape(state.shape[1] * padded, LANES)
            for r in range(2):
                flat_state[pl.ds(row + r, layers, stride=padded), :] = received(
                    pl.ds((c * 2 + r) * slots, layers)
                )
            for tile in range(4):
                wide[c, pl.ds(row, 2), pl.ds(tile * LANES, LANES)] = received(
                    pl.ds(4 * slots + (c * 4 + tile) * 2, 2)
                )
    for c in range(2):
        wide[c, pl.ds(PAD, height), :] = strips[c]
    stepper = Stepper(counts, state, field, later, halo, depth, height)
    stepper.strips(wide)
    stepper.run(outer_tiles(height), True, out, block, sems)


def call(kernel, shapes, args, scratch=(), limit=16, far_out=0, far_in=(), aliases={}, cost=None):
    vmem, far = pl.BlockSpec(memory_space=pltpu.VMEM), pl.BlockSpec(memory_space=pltpu.HBM)
    specs = [far if k in far_in else vmem for k in range(len(args))]
    return pl.pallas_call(
        kernel,
        out_shape=[jax.ShapeDtypeStruct(shape, jnp.float32) for shape in shapes],
        in_specs=specs,
        out_specs=[vmem] * (len(shapes) - far_out) + [far] * far_out,
        scratch_shapes=[
            pltpu.VMEM(shape, jnp.float32) if isinstance(shape, tuple) else shape
            for shape in scratch
        ],
        input_output_aliases=aliases,
        cost_estimate=cost,
        compiler_params=pltpu.CompilerParams(vmem_limit_bytes=int(limit * 2**20)),
    )(*args)


def gathered_carries(rows, columns):
    height, width = rows.shape
    x, y = lax.axis_index("gx"), lax.axis_index("gy")
    row_totals = lax.all_gather(rows[:, -1], "gx")
    before = (jnp.arange(row_totals.shape[0]) < x)[:, None]
    row_carry = jnp.sum(jnp.where(before, row_totals, 0.0), axis=0)
    column_totals = lax.all_gather(columns[-1], "gy")
    before = (jnp.arange(column_totals.shape[0]) < y)[:, None]
    column_carry = jnp.sum(jnp.where(before, column_totals, 0.0), axis=0)
    return (
        jnp.broadcast_to(row_carry[:, None], (height, width)),
        jnp.broadcast_to(column_carry[None], (8, width)),
    )


def local(side, mag):
    counts = tuple(lax.axis_size(axis) for axis in ("gz", "gy", "gx"))
    count_z, count_y, count_x = counts
    _, depth, height, width = side.shape
    plane, block = (height, width), (2, height, width)
    (token,) = call(token_kernel, [(8, LANES)], [], cost=LONG)
    rows, columns = call(
        lambda _, *refs: plane_kernel(*refs), [plane, plane], [token, mag]
    )
    first, second, total, last = call(
        totals_kernel,
        [(2, 2) + plane, (2, 2) + plane, block, (8, width)],
        [side, columns],
    )
    first = swap_first(first, "gz")
    second = swap_second(second, "gz") if count_z > 2 else first
    others = [
        swap(total, "gz", functools.partial(lambda step, i: i ^ step, step))
        for step in far_steps(count_z)
    ]
    direct = count_y == 2 and count_x in (2, 4)
    if direct:
        column_carry = swap_first(last, "gy")
        far_rows = swap(rows, "gx", lambda i: i ^ 2) if count_x == 4 else rows
    else:
        far_rows, column_carry = gathered_carries(rows, columns)
    packed, edges = call(
        pack_kernel,
        [(2, height, 2 * LANES), (2, 4, depth, width)],
        [side],
        [(2, depth * height, width)],
    )
    far = len(others)
    packed, beside, shared, far_rows = call(
        functools.partial(z_kernel, count_z, depth, far),
        [(2, height, 2 * LANES), (2, 4) + plane, block, plane],
        [first, second, total, columns, column_carry, far_rows, rows, packed, *others],
    )
    first = swap_first(packed, "gx")
    second = swap_second(packed, "gx") if count_x > 2 else first
    messages = 1 if count_y == 2 else 2
    message_rows = 4 * slot_rows(depth) + 24
    strips, flat, ext, edge_rows = call(
        functools.partial(x_kernel, counts, depth),
        [(2, height, 4 * LANES), block, (2, 4) + plane, (messages, message_rows, width)],
        [packed, first, second, far_rows, rows, shared, beside, edges],
    )
    first = swap_first(edge_rows[0], "gy")
    second = swap_second(edge_rows[1], "gy") if count_y > 2 else first
    grids = inner_steps(counts, side, flat, ext, strips)
    return outer_steps(counts, depth, strips, first, second, grids)


def inner_steps(counts, side, flat, ext, strips):
    _, depth, height, width = side.shape
    grid = (slot_rows(depth), height + 2 * PAD, width)
    return call(
        functools.partial(inner_kernel, counts),
        [(2,) + grid, (3,) + grid, (3,) + grid, (3, depth, height, width)],
        [side, flat, ext, strips],
        [
            (4, 2, height + 2 * PAD, LANES),
            (2, height + 2 * PAD, 4 * LANES),
            (3, depth, height - 16, width),
            pltpu.SemaphoreType.DMA((height // 8,)),
        ],
        far_out=1,
    )


def outer_steps(counts, depth, strips, first, second, grids):
    height, width = strips.shape[1], first.shape[1]
    result = call(
        functools.partial(outer_kernel, counts, depth),
        [grid.shape for grid in grids],
        [strips, first, second, *grids],
        [
            (4, 2, height + 2 * PAD, LANES),
            (2, height + 2 * PAD, 4 * LANES),
            (3, depth, 16, width),
            pltpu.SemaphoreType.DMA((height // 8,)),
        ],
        far_out=1,
        far_in=(6,),
        aliases={3 + k: k for k in range(4)},
    )
    return result[3]


def solution(mesh):
    return jax.shard_map(
        local,
        mesh=mesh,
        in_specs=(P(None, "gz", "gy", "gx"), P("gy", "gx")),
        out_specs=P(None, "gz", "gy", "gx"),
        check_vma=False,
    )
```
